32 devices in a mesh: level: 2 (over core), blk: 16 (over z, y, x).
Axes of the slice: x: 2, y: 2, z: 4, core: 2. Of those that a mesh axis runs over, the one named last changes fastest.
Arguments:
- fluid_state: float32 [2, 256, 5, 16, 256], P('level', 'blk'), may hold values from -0.5 to 4, as said below
- neighbours: int32 [256, 6], replicated, may hold values from 0 to 255, as said below
- parents: int32 [256, 2], replicated, may hold values from 0 to 255, as said below
Outputs:
- updated: float32 [2, 256, 5, 16, 256], P('level', 'blk')
The draws below stay inside these ranges and needn't reach their ends.
Inputs may be any that keep to these rules, and one draw needn't show every extreme that they name: Row b lists the coarse blocks beyond block b's low and high face along x, then y, then z; the relation is symmetric (the block beyond b's high face along an axis has b beyond its low face along it); block g is held by blk index g // 16, never by the same device as its neighbours; among the (block, face) pairs of one device at most 12 have their neighbour on any one other device, and some pairs of devices reach 12; no block beside a parent is a parent. `parents`: row g gives the coarse parent of refined block g and g's octant in it (4 x half + 2 y half + z half); the parent is held by the same blk index as g; every parent has one child of each octant, so each device's refined blocks are the children of 2 of its coarse blocks. `fluid_state`: components are density, x, y, z momentum and total energy of states with density 0.6 to 1.6, velocity components -0.3 to 0.3 and pressure 0.7 to 1.4, gamma 1.4.
All inputs are finite; a program needn't handle non-finite values.
Results may differ from the reference program's by a relative error of at most 0.0003.
Values sent between devices are 32-bit elements; how exact they have to be, the bound alone decides.
No kernel may reach another device: no remote copies, remote signals or barrier semaphores. Data moves between devices by JAX's collectives and lax.ppermute only.
A program may use at most 192 MiB of HBM per device.

```python
import math
import jax
import jax.numpy as jnp
from jax import lax

EDGE = 16
BLK_DEV = 16
BLOCKS = 256


GAS_GAMMA = 1.4


def layout_of(key):
    device_count = BLOCKS // BLK_DEV
    span_size = device_count // 2
    parent_count = BLK_DEV // 8
    base_key = jax.random.fold_in(key, 1013)
    key_list = jax.random.split(base_key, 4)
    relabel = jax.random.permutation(key_list[0], BLK_DEV)
    offsets = (1 + (jax.random.permutation(key_list[1], 3 * BLK_DEV) + span_size - 1) % span_size).reshape(3, BLK_DEV)
    turn_sizes = jax.random.randint(key_list[2], (3,), parent_count, BLK_DEV - parent_count + 1)
    fine_order = jax.random.permutation(key_list[3], BLK_DEV)
    return (relabel, offsets, turn_sizes, fine_order)


def draw_neighbours(key, part):
    relabel, offsets, turn_sizes, fine_order = layout_of(key)
    device_count = BLOCKS // BLK_DEV
    canonical = jnp.argsort(relabel, stable=True)
    devices = jnp.arange(device_count)[:, None]
    canon_slots = jnp.broadcast_to(canonical[None, :], (device_count, BLK_DEV))
    columns = []
    for direction in range(3):
        upward = (canon_slots + turn_sizes[direction]) % BLK_DEV
        downward = (canon_slots - turn_sizes[direction]) % BLK_DEV
        high_device = (devices + offsets[direction][canon_slots]) % device_count
        low_device = (devices - offsets[direction][downward]) % device_count
        columns.append(low_device * BLK_DEV + relabel[downward])
        columns.append(high_device * BLK_DEV + relabel[upward])
    return jnp.stack(columns, axis=-1).reshape(BLOCKS, 6).astype(jnp.int32)


def draw_parents(key, part):
    relabel, offsets, turn_sizes, fine_order = layout_of(key)
    device_count = BLOCKS // BLK_DEV
    devices = jnp.arange(device_count)[:, None]
    child_ids = jnp.broadcast_to(fine_order[None, :], (device_count, BLK_DEV))
    parent = devices * BLK_DEV + relabel[child_ids // 8]
    octant = child_ids % 8
    return jnp.stack([parent, octant], axis=-1).reshape(BLOCKS, 2).astype(jnp.int32)


def draw_fluid_state(key, part):
    key_list = jax.random.split(jax.random.fold_in(key, 2027), 10)
    cell_shape = (2, BLOCKS, EDGE, EDGE * EDGE)

    def mixed(key_cell, key_block):
        return jax.random.uniform(key_cell, cell_shape)
    density = 0.6 + 1.0 * mixed(key_list[0], key_list[1])
    velocity = [-0.3 + 0.6 * mixed(key_list[2 + 2 * component], key_list[3 + 2 * component]) for component in range(3)]
    pressure = 0.7 + 0.7 * mixed(key_list[8], key_list[9])
    kinetic = velocity[0] * velocity[0] + velocity[1] * velocity[1] + velocity[2] * velocity[2]
    energy = pressure / (GAS_GAMMA - 1.0) + 0.5 * density * kinetic
    momenta = [density * velocity[component] for component in range(3)]
    return jnp.stack([density] + momenta + [energy], axis=2).astype(jnp.float32)


def setup_inputs(seed: int = 0) -> dict:
    seeds = jax.random.split(jax.random.key(seed), 4)
    fluid_state = draw_fluid_state(jax.random.fold_in(seeds[3], 71), 0)
    neighbours = draw_neighbours(jax.random.fold_in(seeds[3], 71), 0)
    parents = draw_parents(jax.random.fold_in(seeds[3], 71), 0)
    return {"fluid_state": fluid_state, "neighbours": neighbours, "parents": parents}


GAS_GAMMA = 1.4
STEP_RATIO = 0.12
OPPOSITE = (1, 0, 3, 2, 5, 4)
FACE_SIGNS = (-1.0, 1.0, -1.0, 1.0, -1.0, 1.0)
BIT_OF = (4, 2, 1)
TANGENT = ((2, 1), (4, 1), (4, 2))

def primitive(state_vec):
    density = state_vec[0]
    velocity = state_vec[1:4] / density
    pressure = (GAS_GAMMA - 1.0) * (state_vec[4] - 0.5 * lax.optimization_barrier(jnp.sum(state_vec[1:4] * velocity, axis=0)))
    return (density, velocity, pressure)

def physical_flux(state_vec, normal, density, velocity, pressure):
    normal_speed = velocity[normal]
    pieces = [state_vec[component] * normal_speed for component in range(4)]
    pieces.append((state_vec[4] + pressure) * normal_speed)
    pieces[1 + normal] = pieces[1 + normal] + pressure
    return jnp.stack(pieces)

def contact_flux(low_state, high_state, normal):
    density_low, velocity_low, pressure_low = primitive(low_state)
    density_high, velocity_high, pressure_high = primitive(high_state)
    sound_low = jnp.sqrt(GAS_GAMMA * pressure_low / density_low)
    sound_high = jnp.sqrt(GAS_GAMMA * pressure_high / density_high)
    speed_low = velocity_low[normal]
    speed_high = velocity_high[normal]
    slowest = jnp.minimum(speed_low - sound_low, speed_high - sound_high)
    fastest = jnp.maximum(speed_low + sound_low, speed_high + sound_high)
    mass_low = density_low * (slowest - speed_low)
    mass_high = density_high * (fastest - speed_high)
    contact = (pressure_high - pressure_low + speed_low * mass_low - speed_high * mass_high) / (mass_low - mass_high)
    flux_low = physical_flux(low_state, normal, density_low, velocity_low, pressure_low)
    flux_high = physical_flux(high_state, normal, density_high, velocity_high, pressure_high)

    def star_flux(state_vec, density, velocity, pressure, mass_flow, wave_speed, flux_here):
        factor = mass_flow / (wave_speed - contact)
        momenta = [factor * velocity[component] for component in range(3)]
        momenta[normal] = factor * contact
        energy = factor * (state_vec[4] / density + (contact - velocity[normal]) * (contact + pressure / mass_flow))
        star_state = jnp.stack([factor] + momenta + [energy])
        return flux_here + wave_speed * (star_state - state_vec)
    star_low = star_flux(low_state, density_low, velocity_low, pressure_low, mass_low, slowest, flux_low)
    star_high = star_flux(high_state, density_high, velocity_high, pressure_high, mass_high, fastest, flux_high)
    return jnp.where(slowest >= 0.0, flux_low, jnp.where(contact >= 0.0, star_low, jnp.where(fastest > 0.0, star_high, flux_high)))

def face_fluxes(padded, normal):
    step_below = padded[:, :, 1:-1] - padded[:, :, :-2]
    step_above = padded[:, :, 2:] - padded[:, :, 1:-1]
    limited = jnp.where(step_below * step_above > 0.0, jnp.sign(step_below) * jnp.minimum(jnp.abs(step_below), jnp.abs(step_above)), 0.0)
    centre = padded[:, :, 1:-1]
    low_face = centre - 0.5 * limited
    high_face = centre + 0.5 * limited
    change = 0.5 * STEP_RATIO * (physical_flux(low_face, normal, *primitive(low_face)) - physical_flux(high_face, normal, *primitive(high_face)))
    low_face = low_face + change
    high_face = high_face + change
    return contact_flux(high_face[:, :, :-1], low_face[:, :, 1:], normal)

def oriented(block_cells, direction):
    leading = block_cells.shape[:2]
    edge_cells = block_cells.shape[2]
    cube_cells = block_cells.reshape(leading + (edge_cells, edge_cells, edge_cells))
    if direction == 1:
        cube_cells = cube_cells.transpose(0, 1, 3, 2, 4)
    elif direction == 2:
        cube_cells = cube_cells.transpose(0, 1, 4, 2, 3)
    return cube_cells.reshape(leading + (edge_cells, edge_cells * edge_cells))

def restored(block_cells, direction):
    leading = block_cells.shape[:2]
    edge_cells = block_cells.shape[2]
    cube_cells = block_cells.reshape(leading + (edge_cells, edge_cells, edge_cells))
    if direction == 1:
        cube_cells = cube_cells.transpose(0, 1, 3, 2, 4)
    elif direction == 2:
        cube_cells = cube_cells.transpose(0, 1, 3, 4, 2)
    return cube_cells.reshape(leading + (edge_cells, edge_cells * edge_cells))

def advance(block_cells, ghosts):
    divergence = jnp.zeros_like(block_cells)
    boundary = []
    for direction in range(3):
        padded = jnp.concatenate([ghosts[2 * direction], oriented(block_cells, direction), ghosts[2 * direction + 1]], axis=2)
        fluxes = face_fluxes(padded, direction)
        divergence = divergence + restored(fluxes[:, :, 1:] - fluxes[:, :, :-1], direction)
        boundary.append(fluxes[:, :, 0])
        boundary.append(fluxes[:, :, -1])
    return (block_cells - STEP_RATIO * divergence, jnp.stack(boundary))

def face_slabs(block_cells, layers):
    edge_cells = block_cells.shape[2]
    pieces = []
    for direction in range(3):
        view_cells = oriented(block_cells, direction)
        pieces.append(view_cells[:, :, :layers])
        pieces.append(view_cells[:, :, edge_cells - layers:])
    return jnp.stack(pieces).transpose(2, 0, 1, 3, 4)

def inner_rim(ghost_slabs):
    return jnp.stack([ghost_slabs[:, face_id, :, 1 - face_id % 2] for face_id in range(6)], axis=1)

def flipped_octant(octants, mask_bit):
    return octants + mask_bit - 2 * mask_bit * (octants // mask_bit % 2)

def fine_ghosts(face_set, rims, octants, siblings):
    block_count = face_set.shape[0]
    edge_sq = face_set.shape[-1]
    half_edge = math.isqrt(edge_sq) // 2
    row_ids = jnp.arange(block_count)
    result = []
    for face_id in range(6):
        direction = face_id // 2
        side_id = face_id % 2
        outward = octants // BIT_OF[direction] % 2 == side_id
        first_bit = octants // TANGENT[direction][0] % 2
        second_bit = octants // TANGENT[direction][1] % 2
        coarse_rim = rims[:, face_id].reshape(block_count, 5, 2, half_edge, 2, half_edge)
        quarter = coarse_rim[row_ids, :, first_bit, :, second_bit, :]
        widened = jnp.repeat(jnp.repeat(quarter, 2, axis=2), 2, axis=3).reshape(block_count, 5, 1, edge_sq)
        from_coarse = jnp.concatenate([widened, widened], axis=2)
        from_sibling = face_set[siblings[:, direction], OPPOSITE[face_id]]
        result.append(jnp.where(outward[:, None, None, None], from_coarse, from_sibling))
    return jnp.stack(result).transpose(0, 2, 1, 3, 4)

def restricted(block_cells, flux_total, octants):
    block_count = block_cells.shape[1]
    half_edge = block_cells.shape[2] // 2
    averages = block_cells.reshape(5, block_count, half_edge, 2, half_edge, 2, half_edge, 2).sum(axis=(3, 5, 7)) * 0.125
    averages = averages.transpose(1, 0, 2, 3, 4)
    quarters = []
    for direction in range(3):
        outward_high = octants // BIT_OF[direction] % 2 == 1
        chosen = jnp.where(outward_high[None, :, None], flux_total[2 * direction + 1], flux_total[2 * direction])
        summed = chosen.reshape(5, block_count, half_edge, 2, half_edge, 2).sum(axis=(3, 5))
        quarters.append(summed.transpose(1, 0, 2, 3) * 0.125)
    return (averages, jnp.stack(quarters, axis=1))

def assemble(averages, quarters, children, coarse_faces):
    block_count = children.shape[0]
    half_edge = averages.shape[-1]
    edge_cells = 2 * half_edge
    picked = averages[children].reshape(block_count, 2, 2, 2, 5, half_edge, half_edge, half_edge)
    new_cells = picked.transpose(4, 0, 1, 5, 2, 6, 3, 7).reshape(5, block_count, edge_cells, edge_cells * edge_cells)
    deltas = []
    for face_id in range(6):
        direction = face_id // 2
        side_id = face_id % 2
        octant_list = []
        for first_bit in (0, 1):
            for second_bit in (0, 1):
                octant_list.append(side_id * BIT_OF[direction] + first_bit * TANGENT[direction][0] + second_bit * TANGENT[direction][1])
        chosen = quarters[children[:, jnp.array(octant_list, jnp.int32)]][:, :, direction]
        fine_face = chosen.reshape(block_count, 2, 2, 5, half_edge, half_edge).transpose(0, 3, 1, 4, 2, 5).reshape(block_count, 5, edge_cells * edge_cells)
        deltas.append(coarse_faces[face_id].transpose(1, 0, 2) - fine_face)
    return (new_cells, jnp.stack(deltas, axis=1))

def apply_corrections(block_cells, corrections):
    edge_cells = block_cells.shape[2]
    for direction in range(3):
        view_cells = oriented(block_cells, direction)
        view_cells = view_cells.at[:, :, 0].add(corrections[:, 2 * direction].transpose(1, 0, 2))
        view_cells = view_cells.at[:, :, edge_cells - 1].add(corrections[:, 2 * direction + 1].transpose(1, 0, 2))
        block_cells = restored(view_cells, direction)
    return block_cells

def stepped(block_cells, ghosts):
    total_blocks = block_cells.shape[1]
    groups = total_blocks // BLK_DEV
    edge_cells = block_cells.shape[2]
    edge_sq = block_cells.shape[3]
    grouped = block_cells.reshape(5, groups, BLK_DEV, edge_cells, edge_sq).transpose(1, 0, 2, 3, 4)
    grouped_ghosts = ghosts.reshape(6, 5, groups, BLK_DEV, 2, edge_sq).transpose(2, 0, 1, 3, 4, 5)
    new_cells, boundary = lax.map(lambda operands: advance(operands[0], operands[1]), (grouped, grouped_ghosts))
    new_cells = new_cells.transpose(1, 0, 2, 3, 4).reshape(5, total_blocks, edge_cells, edge_sq)
    boundary = boundary.transpose(1, 2, 0, 3, 4).reshape(6, 5, total_blocks, edge_sq)
    return (new_cells, boundary)

def reference(fluid_state, neighbours, parents):
    coarse = fluid_state[0].transpose(1, 0, 2, 3)
    refined_cells = fluid_state[1].transpose(1, 0, 2, 3)
    opposite = jnp.array(OPPOSITE, jnp.int32)

    def ghosts_of(face_set):
        return face_set[neighbours, opposite[None, :]]
    early_ghosts = ghosts_of(face_slabs(coarse, 2))
    coarse_new, coarse_faces = stepped(coarse, early_ghosts.transpose(1, 2, 0, 3, 4))
    late_ghosts = ghosts_of(face_slabs(coarse_new, 2))
    parent = parents[:, 0]
    octants = parents[:, 1]
    total_blocks = parents.shape[0]
    children = jnp.zeros((total_blocks, 8), jnp.int32).at[parent, octants].set(jnp.arange(total_blocks, dtype=jnp.int32))
    siblings = jnp.stack([children[parent, flipped_octant(octants, BIT_OF[direction])] for direction in range(3)], axis=1)
    early_rims = inner_rim(early_ghosts)[parent]
    late_rims = inner_rim(late_ghosts)[parent]
    fine_half, first_faces = stepped(refined_cells, fine_ghosts(face_slabs(refined_cells, 2), early_rims, octants, siblings))
    fine_out, second_faces = stepped(fine_half, fine_ghosts(face_slabs(fine_half, 2), 0.5 * (early_rims + late_rims), octants, siblings))
    averages, quarters = restricted(fine_out, first_faces + second_faces, octants)
    refined = jnp.zeros((total_blocks,), jnp.float32).at[parent].set(1.0)
    parent_cells, deltas = assemble(averages, quarters, children, coarse_faces)
    coarse_mixed = jnp.where(refined[None, :, None, None] > 0.0, parent_cells, coarse_new)
    deltas = deltas * refined[:, None, None, None]
    face_signs = jnp.array(FACE_SIGNS, jnp.float32)
    corrections = deltas[neighbours, opposite[None, :]] * face_signs[None, :, None, None] * STEP_RATIO
    coarse_out = apply_corrections(coarse_mixed, corrections)
    return jnp.stack([coarse_out, fine_out]).transpose(0, 2, 1, 3, 4)
```

```python
import functools

import jax
import jax.numpy as jnp
from jax import lax
from jax.experimental import pallas as pl
from jax.experimental.pallas import tpu as pltpu
from jax.sharding import PartitionSpec as P

GAS_GAMMA = 1.4
STEP_RATIO = 0.12
BIT_OF = (4, 2, 1)
TANGENT = ((2, 1), (4, 1), (4, 2))
F32 = jnp.float32
I32 = jnp.int32
VMEM_LIMIT = 48 * 1024 * 1024
LANES = 128
ROWS = 8


def iota(shape, dim):
    return lax.broadcasted_iota(I32, shape, dim)


def reciprocal(x):
    return pltpu.reciprocal(x, approx=True)


def exact_dot(a, b):
    return jnp.dot(a, b, precision=lax.Precision.HIGHEST, preferred_element_type=F32)


def exact_dot_nt(a, b):
    return lax.dot_general(
        a, b, (((1,), (1,)), ((), ())), precision=lax.Precision.HIGHEST, preferred_element_type=F32
    )


def physical_flux(s, n):
    inv = reciprocal(s[0])
    vn = s[n] * inv
    kinetic = s[1] * s[1] + s[2] * s[2] + s[3] * s[3]
    p = (GAS_GAMMA - 1.0) * (s[4] - 0.5 * (kinetic * inv))
    out = [s[n], s[1] * vn, s[2] * vn, s[3] * vn, (s[4] + p) * vn]
    out[n] = out[n] + p
    return out


def evolve(u, below, above, n):
    low = []
    high = []
    for c in range(5):
        d = jnp.maximum(jnp.minimum(below[c], above[c]), 0.0) + jnp.minimum(
            jnp.maximum(below[c], above[c]), 0.0
        )
        d = 0.5 * d
        low.append(u[c] - d)
        high.append(u[c] + d)
    fl = physical_flux(low, n)
    fh = physical_flux(high, n)
    for c in range(5):
        change = (0.5 * STEP_RATIO) * (fl[c] - fh[c])
        low[c] = low[c] + change
        high[c] = high[c] + change
    return low, high


def side_values(s, n):
    inv = reciprocal(s[0])
    vn = s[n] * inv
    kinetic = s[1] * s[1] + s[2] * s[2] + s[3] * s[3]
    p = (GAS_GAMMA - 1.0) * (s[4] - 0.5 * (kinetic * inv))
    square = GAS_GAMMA * p * inv
    sound = square * lax.rsqrt(square)
    return vn, p, sound


def hllc(a, b, n):
    va, pa, ca = side_values(a, n)
    vb, pb, cb = side_values(b, n)
    slow = jnp.minimum(va - ca, vb - cb)
    fast = jnp.maximum(va + ca, vb + cb)
    qa = a[0] * (slow - va)
    qb = b[0] * (fast - vb)
    contact = (pb - pa + va * qa - vb * qb) * reciprocal(qa - qb)
    is_low = contact >= 0.0

    def pick(x, y):
        return jnp.where(is_low, x, y)

    s = [pick(a[c], b[c]) for c in range(5)]
    v = pick(va, vb)
    p = pick(pa, pb)
    q = pick(qa, qb)
    speed = pick(slow, fast)
    clipped = pick(jnp.minimum(slow, 0.0), jnp.maximum(fast, 0.0))
    extra = clipped * (contact - v) * reciprocal(speed - contact)
    h = v + extra
    push = extra * q
    out = [s[0] * h, s[1] * h, s[2] * h, s[3] * h, (s[4] + p) * h + push * contact]
    out[n] = out[n] + p + push
    return out


def extract(u_ref, plane_ref, layers, nb, edge):
    half_blocks = nb // 2
    for side in range(2):
        for layer in range(layers):
            x = layer if side == 0 else edge - 1 - layer
            for c in range(5):
                plane_ref[side, layer, c * nb : (c + 1) * nb, :] = u_ref[:, c, x, :]
    grp = iota((ROWS, LANES), 1) // edge
    sub = iota((ROWS, LANES), 1) % edge
    zero = jnp.zeros((ROWS, LANES), F32)
    offsets = [o for layer in range(layers) for o in (layer, edge - 1 - layer)]

    def body(k, carry):
        c = k // 2
        start = pl.multiple_of((k % 2) * ROWS, ROWS)
        ylow = [[zero, zero] for _ in range(layers)]
        yhigh = [[zero, zero] for _ in range(layers)]
        zacc = {o: [zero, zero] for o in offsets}
        for b in range(nb):
            v = [u_ref[b, c, pl.ds(start, ROWS), h * LANES : (h + 1) * LANES] for h in range(2)]
            t = b // half_blocks
            low = pltpu.roll(v[0], edge * b % LANES, 1)
            high = pltpu.roll(v[1], edge * b % LANES, 1)
            for layer in range(layers):
                ylow[layer][t] = jnp.where(grp == (b + layer) % half_blocks, low, ylow[layer][t])
                yhigh[layer][t] = jnp.where(
                    grp == (b + half_blocks - 1 - layer) % half_blocks, high, yhigh[layer][t]
                )
            for h in range(2):
                r = pltpu.roll(v[h], b, 1) if b else v[h]
                for o in offsets:
                    zacc[o][h] = jnp.where(sub == (b + o) % edge, r, zacc[o][h])
        at = pl.ds(pl.multiple_of(k * ROWS, ROWS), ROWS)
        for layer in range(layers):
            for h in range(2):
                lanes = slice(h * LANES, (h + 1) * LANES)
                plane_ref[2, layer, at, lanes] = pltpu.roll(
                    ylow[layer][h], (LANES - edge * layer) % LANES, 1
                )
                plane_ref[3, layer, at, lanes] = pltpu.roll(
                    yhigh[layer][h], edge * (1 + layer) % LANES, 1
                )
                for side, o in ((0, layer), (1, edge - 1 - layer)):
                    plane_ref[4 + side, layer, at, lanes] = pltpu.roll(
                        zacc[o][h], (LANES - o) % LANES, 1
                    )
        return carry

    lax.fori_loop(0, 10, body, 0)


def expand_add(base_ref, add_ref, out_ref, layers, nb, edge):
    half_blocks = nb // 2
    lane = iota((ROWS, LANES), 1)
    row = iota((ROWS, LANES), 0)
    grp = lane // edge
    sub = lane % edge

    def body(k, carry):
        c = k // 2
        rt = k % 2
        start = pl.multiple_of(rt * ROWS, ROWS)
        at = pl.ds(pl.multiple_of(k * ROWS, ROWS), ROWS)

        def plane(face, layer, h):
            return add_ref[face, layer, at, h * LANES : (h + 1) * LANES]

        ylow = [[plane(2, layer, h) for h in range(2)] for layer in range(layers)]
        yhigh = [[plane(3, layer, h) for h in range(2)] for layer in range(layers)]
        zlow = [[plane(4, layer, h) for h in range(2)] for layer in range(layers)]
        zhigh = [[plane(5, layer, h) for h in range(2)] for layer in range(layers)]
        for h in range(2):
            zhigh[0][h] = pltpu.roll(zhigh[0][h], edge - 1, 1)
            if layers > 1:
                ylow[1][h] = pltpu.roll(ylow[1][h], edge, 1)
                yhigh[1][h] = pltpu.roll(yhigh[1][h], LANES - edge, 1)
                zlow[1][h] = pltpu.roll(zlow[1][h], 1, 1)
                zhigh[1][h] = pltpu.roll(zhigh[1][h], edge - 2, 1)
        for b in range(nb):
            t = b // half_blocks
            place = b % half_blocks
            if layers > 1:
                low = jnp.where(grp == place, ylow[0][t], ylow[1][t])
                high = jnp.where(grp == place, yhigh[0][t], yhigh[1][t])
            else:
                low = ylow[0][t]
                high = yhigh[0][t]
            low = pltpu.roll(low, (LANES - edge * place) % LANES, 1)
            high = pltpu.roll(high, edge * (half_blocks - 1 - place) % LANES, 1)
            parts = [
                jnp.where(grp < layers, low, 0.0),
                jnp.where(grp >= half_blocks - layers, high, 0.0),
            ]
            xrows = [
                add_ref[rt, layer, pl.ds(c * nb + b, 1), :] for layer in range(layers)
            ]
            for h in range(2):
                lanes = slice(h * LANES, (h + 1) * LANES)
                if layers > 1:
                    z = jnp.where(
                        sub == b,
                        zlow[0][h],
                        jnp.where(
                            sub == (b + 1) % edge,
                            zlow[1][h],
                            jnp.where(sub == (b + edge - 1) % edge, zhigh[0][h], zhigh[1][h]),
                        ),
                    )
                else:
                    z = jnp.where(sub == b, zlow[0][h], zhigh[0][h])
                if b:
                    z = pltpu.roll(z, LANES - b, 1)
                total = parts[h] + jnp.where((sub < layers) | (sub >= edge - layers), z, 0.0)
                x = jnp.where(row == (ROWS - 1) * rt, xrows[0][:, lanes], 0.0)
                if layers > 1:
                    x = jnp.where(row == 1 + (ROWS - 3) * rt, xrows[1][:, lanes], x)
                total = total + x
                out_ref[b, c, pl.ds(start, ROWS), lanes] = (
                    base_ref[b, c, pl.ds(start, ROWS), lanes] + total
                )
        return carry

    lax.fori_loop(0, 10, body, 0)


def take_lanes(v, index):
    return jnp.take_along_axis(v, index, axis=1, mode="promise_in_bounds")


def swap_row_group(v, edge):
    lane = iota((ROWS, LANES), 1)
    row = iota((ROWS, LANES), 0)
    g = take_lanes(v, (lane + edge * row) % LANES)
    for bit in (1, 2, 4):
        g = jnp.where(((lane // edge) & bit) != 0, pltpu.roll(g, bit, 0), g)
    return take_lanes(g, edge * ((row - lane // edge + ROWS) % ROWS) + lane % edge)


def swap_group_sub(v0, v1, half, edge):
    lane = iota((ROWS, LANES), 1)
    index = edge * (lane % ROWS) + (edge // 2) * half + lane // edge
    return jnp.where(lane % edge < edge // 2, take_lanes(v0, index), take_lanes(v1, index))


def common_tile(load, axis, m, half, edge):
    if axis == 0:
        return swap_row_group(load(m - m % 2 + half, m % 2), edge)
    if axis == 1:
        return load(m, half)
    return swap_group_sub(load(m, 0), load(m, 1), half, edge)


def plane_loader(ref, face, layer):
    def load(m, half):
        return ref[face, layer, m * ROWS : (m + 1) * ROWS, half * LANES : (half + 1) * LANES]

    return load


def interleave(plane_ref, first, second, mix_ref, edge):
    odd = (iota((ROWS, LANES), 1) // edge) % 2 == 1
    for face in range(6):
        axis = face // 2
        for index, (m1, m2) in enumerate(zip(first[1], second[1])):
            for half in range(2):
                a = common_tile(plane_loader(plane_ref, face, first[0]), axis, m1, half, edge)
                b = common_tile(plane_loader(plane_ref, face, second[0]), axis, m2, half, edge)
                at = slice(index * ROWS, (index + 1) * ROWS)
                mix_ref[face, 0, half, at, :] = jnp.where(odd, pltpu.roll(b, edge, 1), a)
                mix_ref[face, 1, half, at, :] = jnp.where(odd, b, pltpu.roll(a, LANES - edge, 1))


def disentangle(mix_ref, first, second, plane_ref, temp_ref, edge):
    odd = (iota((ROWS, LANES), 1) // edge) % 2 == 1
    for face in range(6):
        axis = face // 2
        for index, (m1, m2) in enumerate(zip(first[1], second[1])):
            for half in range(2):
                at = slice(index * ROWS, (index + 1) * ROWS)
                even_tile = mix_ref[face, 0, half, at, :]
                odd_tile = mix_ref[face, 1, half, at, :]
                lanes = slice(half * LANES, (half + 1) * LANES)
                a = jnp.where(odd, pltpu.roll(odd_tile, edge, 1), even_tile)
                b = jnp.where(odd, odd_tile, pltpu.roll(even_tile, LANES - edge, 1))
                target = plane_ref if axis == 1 else temp_ref
                target[face, first[0], m1 * ROWS : (m1 + 1) * ROWS, lanes] = a
                target[face, second[0], m2 * ROWS : (m2 + 1) * ROWS, lanes] = b
        if axis == 1:
            continue
        for layer in sorted({first[0], second[0]}):
            for m in range(10):
                for half in range(2):
                    plane_ref[
                        face, layer, m * ROWS : (m + 1) * ROWS, half * LANES : (half + 1) * LANES
                    ] = common_tile(plane_loader(temp_ref, face, layer), axis, m, half, edge)


def slot_place(slot, edge):
    per_tile = LANES // (2 * edge)
    return slot // per_tile, slot % per_tile


def pack_items(tab_ref, valid_row, slot_row, mix_ref, send_ref, rows, nb, edge):
    wide = 2 * edge
    lane_slot = iota((rows, LANES), 1) // wide

    def body(i, carry):
        def move():
            block = i // 6
            face = i % 6
            half = block // (nb // 2)
            place = (block % (nb // 2)) // 2
            group, q = slot_place(tab_ref[slot_row, i], edge)
            v = mix_ref[face, block % 2, half]
            v = pltpu.roll(v, (wide * (q - place) + LANES) % LANES, 1)
            at = pl.ds(pl.multiple_of(group * rows, ROWS), rows)
            target = tab_ref[0, i]
            send_ref[target, at, :] = jnp.where(lane_slot == q, v, send_ref[target, at, :])

        if valid_row is None:
            move()
        else:
            pl.when(tab_ref[valid_row, i] > 0)(move)
        return carry

    lax.fori_loop(0, 6 * nb, body, 0)


def unpack_items(tab_ref, valid_row, slot_row, recv_ref, mix_ref, rows, nb, edge):
    wide = 2 * edge
    lane_slot = iota((rows, LANES), 1) // wide
    per_half = nb // 4

    def body(k, carry):
        face = k % 6
        parity = (k // 6) % 2
        half = k // 12
        acc = jnp.zeros((rows, LANES), F32)
        for place in range(per_half):
            i = (half * (nb // 2) + 2 * place + parity) * 6 + face
            group, q = slot_place(tab_ref[slot_row, i], edge)
            at = pl.ds(pl.multiple_of(group * rows, ROWS), rows)
            v = recv_ref[tab_ref[0, i], at, :]
            v = pltpu.roll(v, (wide * (place - q) + LANES) % LANES, 1)
            keep = lane_slot == place
            if valid_row is not None:
                keep = keep & (tab_ref[valid_row, i] > 0)
            acc = jnp.where(keep, v, acc)
        mix_ref[face, parity, half] = acc
        return carry

    lax.fori_loop(0, 24, body, 0)


def interior_kernel(nb, edge, u_ref, d_ref):
    square = edge * edge

    def sweep(u, axis, index, size, step, dim):
        n = 1 + axis
        below = [x - pltpu.roll(x, step, dim) for x in u]
        above = [pltpu.roll(x, size - step, dim) for x in below]
        low, high = evolve(u, below, above, n)
        prev = [pltpu.roll(x, step, dim) for x in high]
        inside = (index >= 2) & (index <= edge - 2)
        flux = [jnp.where(inside, x, 0.0) for x in hllc(prev, low, n)]
        return [pltpu.roll(x, size - step, dim) - x for x in flux]

    def body(b, carry):
        for rt in range(edge // ROWS):
            rows = slice(rt * ROWS, (rt + 1) * ROWS)
            u = [u_ref[b, c, rows, :] for c in range(5)]
            div = sweep(u, 1, iota((ROWS, square), 1) // edge, square, edge, 1)
            for c in range(5):
                d_ref[b, c, rows, :] = u[c] - STEP_RATIO * div[c]
        for half in range(square // LANES):
            lanes = slice(half * LANES, (half + 1) * LANES)
            u = [u_ref[b, c, :, lanes] for c in range(5)]
            div = sweep(u, 0, iota((edge, LANES), 0), edge, 1, 0)
            more = sweep(u, 2, iota((edge, LANES), 1) % edge, LANES, 1, 1)
            for c in range(5):
                d_ref[b, c, :, lanes] = d_ref[b, c, :, lanes] - STEP_RATIO * (div[c] + more[c])
        return carry

    lax.fori_loop(0, nb, body, 0)


def face_fluxes(plane_ref, ghost_ref, add_ref, face_ref, nb):
    for face in range(6):
        axis = face // 2
        side = face % 2
        n = 1 + axis
        sign = 1.0 - 2.0 * side

        def body(rt, carry):
            def load(ref, layer):
                return [
                    ref[face, layer, pl.ds(pl.multiple_of(c * nb + rt * ROWS, ROWS), ROWS), :]
                    for c in range(5)
                ]

            near, mid, deep = (load(plane_ref, layer) for layer in range(3))
            ghost, far = (load(ghost_ref, layer) for layer in range(2))

            def steps(a, b):
                return [sign * (y - x) for x, y in zip(a, b)]

            d0, d1, d2, d3 = steps(far, ghost), steps(ghost, near), steps(near, mid), steps(mid, deep)
            if side == 0:
                first = hllc(evolve(ghost, d0, d1, n)[1], evolve(near, d1, d2, n)[0], n)
                second = hllc(evolve(near, d1, d2, n)[1], evolve(mid, d2, d3, n)[0], n)
            else:
                first = hllc(evolve(near, d1, d2, n)[1], evolve(ghost, d0, d1, n)[0], n)
                second = hllc(evolve(mid, d2, d3, n)[1], evolve(near, d1, d2, n)[0], n)
            for c in range(5):
                at = pl.ds(pl.multiple_of(c * nb + rt * ROWS, ROWS), ROWS)
                face_ref[face, at, :] = first[c]
                add_ref[face, 0, at, :] = (sign * STEP_RATIO) * (first[c] - second[c])
                add_ref[face, 1, at, :] = (sign * STEP_RATIO) * second[c]
            return carry

        lax.fori_loop(0, nb // ROWS, body, 0)


ALL = tuple(range(10))
FIRST_HALF = tuple(range(5))
SECOND_HALF = tuple(range(5, 10))


def planes_kernel(nb, edge, u_ref, plane_ref):
    extract(u_ref, plane_ref, 3, nb, edge)


def pack_kernel(nb, edge, tab_ref, plane_ref, send_ref, mix_ref):
    interleave(plane_ref, (0, ALL), (1, ALL), mix_ref, edge)
    pack_items(tab_ref, None, 1, mix_ref, send_ref, 80, nb, edge)


def rim_place(p, face, edge):
    start = (face * 2 + p) * edge
    return start // LANES, start % LANES


def rims_kernel(nb, edge, parents_here, rows, tab_ref, recv_ref, rim_ref):
    slot_row = 2 if rows == 80 else 6
    lane_group = iota((rows, LANES), 1) // edge
    acc = {}
    for face in range(6):
        for p in range(parents_here):
            i = tab_ref[9, p] * 6 + face
            group, q = slot_place(tab_ref[slot_row, i], edge)
            at = pl.ds(pl.multiple_of(group * rows, ROWS), rows)
            v = recv_ref[tab_ref[0, i], at, :]
            half, lane = rim_place(p, face, edge)
            for part in range(80 // rows):
                turn = (lane - 2 * edge * q - edge * part + 2 * LANES) % LANES
                moved = pltpu.roll(v, turn, 1)
                old = acc.get((part, half), jnp.zeros((rows, LANES), F32))
                acc[part, half] = jnp.where(lane_group == lane // edge, moved, old)
    for (part, half), value in acc.items():
        rim_ref[part * rows : (part + 1) * rows, half * LANES : (half + 1) * LANES] = value


def coarse_kernel(
    nb, edge, tab_ref, d_ref, plane_ref, recv_ref, new_ref, face_ref, send_ref, mix_ref, ghost_ref,
    temp_ref, add_ref, near_ref, mix2_ref,
):
    unpack_items(tab_ref, None, 2, recv_ref, mix_ref, 80, nb, edge)
    disentangle(mix_ref, (0, ALL), (1, ALL), ghost_ref, temp_ref, edge)
    face_fluxes(plane_ref, ghost_ref, add_ref, face_ref, nb)
    expand_add(d_ref, add_ref, new_ref, 2, nb, edge)
    extract(new_ref, near_ref, 1, nb, edge)
    interleave(near_ref, (0, FIRST_HALF), (0, SECOND_HALF), mix2_ref, edge)
    pack_items(tab_ref, 3, 5, mix2_ref, send_ref, 40, nb, edge)


def kron_rows(size, edge, shift, transposed):
    i = iota((size, size), 0)
    j = iota((size, size), 1)
    if transposed:
        i, j = j, i
    hit = (i // edge == j // edge) & (j % edge == shift + (i % edge) // 2)
    return jnp.where(hit, 1.0, 0.0).astype(F32)


def key_matrix(key_row, face, edge, width):
    offset = (face * 2 * edge) % LANES
    return jnp.where(iota((2 * LANES, width), 0) == key_row + offset, 1.0, 0.0).astype(F32)


def fine_kernel(
    nb, edge, late, key_ref, d_ref, plane_ref, rim_ref, rim2_ref, new_ref, face_ref, ghost_ref,
    temp_ref, add_ref,
):
    width = nb * edge
    rim = 0.5 * (rim_ref[...] + rim2_ref[...]) if late else rim_ref[...]
    halves = [exact_dot(kron_rows(80, edge, h * (edge // 2), False), rim) for h in range(2)]
    for face in range(6):
        axis = face // 2
        side = face % 2
        opposite = face + 1 - 2 * side
        tile = (face * 2 * edge) // LANES
        both = jnp.concatenate([x[:, tile * LANES : (tile + 1) * LANES] for x in halves], axis=1)
        outer = exact_dot(both, key_matrix(key_ref[axis : axis + 1, :], face, edge, width))
        if axis == 0:
            temp_ref[face, 0] = outer
            for m in range(10):
                for half in range(2):
                    temp_ref[
                        face, 1, m * ROWS : (m + 1) * ROWS, half * LANES : (half + 1) * LANES
                    ] = common_tile(plane_loader(temp_ref, face, 0), 0, m, half, edge)
            outer = temp_ref[face, 1]
            sib = key_ref[16 : 16 + nb, 0:80]
            i = iota((80, 80), 0)
            j = iota((80, 80), 1)
            sib = jnp.concatenate([sib] * 5, axis=0)
            swap = jnp.where((j % nb == sib) & (i // nb == j // nb), 1.0, 0.0).astype(F32)
            outward = jnp.concatenate([key_ref[32 : 32 + nb, :]] * 5, axis=0) == side
        else:
            swap = jnp.where(
                iota((width, width), 0) == key_ref[2 + axis : 3 + axis, :], 1.0, 0.0
            ).astype(F32)
            outward = key_ref[4 + axis : 5 + axis, :] == side
        for layer in range(2):
            own = plane_ref[opposite, layer]
            inner = exact_dot(swap, own) if axis == 0 else exact_dot(own, swap)
            ghost_ref[face, layer] = jnp.where(outward, outer, inner)
    face_fluxes(plane_ref, ghost_ref, add_ref, face_ref, nb)
    expand_add(d_ref, add_ref, new_ref, 2, nb, edge)


def means_kernel(nb, edge, key_ref, first_ref, second_ref, mean_ref, temp_ref):
    width = nb * edge
    acc = [None, None]
    for face in range(6):
        axis = face // 2
        side = face % 2
        tile = (face * 2 * edge) // LANES
        total = first_ref[face] + second_ref[face]
        if axis == 0:
            outward = jnp.concatenate([key_ref[32 : 32 + nb, :]] * 5, axis=0) == side
            temp_ref[face, 0] = jnp.where(outward, total, 0.0)
            for m in range(10):
                for half in range(2):
                    temp_ref[
                        face, 1, m * ROWS : (m + 1) * ROWS, half * LANES : (half + 1) * LANES
                    ] = common_tile(plane_loader(temp_ref, face, 0), 0, m, half, edge)
            total = temp_ref[face, 1]
        else:
            total = jnp.where(key_ref[4 + axis : 5 + axis, :] == side, total, 0.0)
        part = exact_dot_nt(total, key_matrix(key_ref[axis : axis + 1, :], face, edge, width))
        acc[tile] = part if acc[tile] is None else acc[tile] + part
    for tile in range(2):
        mean_ref[:, tile * LANES : (tile + 1) * LANES] = 0.125 * sum(
            exact_dot(
                kron_rows(80, edge, h * (edge // 2), True),
                acc[tile][:, h * LANES : (h + 1) * LANES],
            )
            for h in range(2)
        )


def averages_kernel(nb, edge, octant_ref, u_ref, out_ref):
    square = edge * edge
    half = edge // 2
    i = iota((square, LANES), 0)
    pairs = jnp.where(
        iota((square, LANES), 1) == (i // edge // 2) * edge + (i % edge) // 2, 0.125, 0.0
    ).astype(F32)
    i = iota((5 * half, 5 * edge), 0)
    j = iota((5 * half, 5 * edge), 1)
    rows = jnp.where(j // 2 == i, 1.0, 0.0).astype(F32)
    high = (iota((5 * half, LANES), 1) % edge) // half
    out_ref[...] = jnp.zeros(out_ref.shape, F32)

    def body(b, carry):
        octant = octant_ref[0, b]
        p = octant_ref[1, b]
        oz = octant % 2
        u = u_ref[b].reshape(5 * edge, square)
        v = exact_dot(rows, exact_dot(u, pairs))
        v = jnp.where(high == oz, pltpu.roll(v, half * oz, 1), 0.0)
        lanes = pl.ds(pl.multiple_of((octant // 2 % 2) * LANES, LANES), LANES)
        at = pl.ds(pl.multiple_of((octant // 4) * ROWS, ROWS), ROWS)
        for c in range(5):
            out_ref[p, c, at, lanes] = out_ref[p, c, at, lanes] + v[c * half : (c + 1) * half, :]
        return carry

    lax.fori_loop(0, nb, body, 0)


def return_kernel(nb, edge, parents_here, tab_ref, mean_ref, send_ref):
    rows = 40
    lane_slot = iota((rows, LANES), 1) // edge
    for face in range(6):
        for p in range(parents_here):
            i = tab_ref[9, p] * 6 + face
            group, q = slot_place(tab_ref[7, i], edge)
            at = pl.ds(pl.multiple_of(group * rows, ROWS), rows)
            half, lane = rim_place(p, face, edge)
            target = tab_ref[0, i]
            value = send_ref[target, at, :]
            for part in range(2):
                v = mean_ref[part * rows : (part + 1) * rows, half * LANES : (half + 1) * LANES]
                turn = (2 * edge * q + edge * part - lane + LANES) % LANES
                v = pltpu.roll(v, turn, 1)
                value = jnp.where(lane_slot == 2 * q + part, v, value)
            send_ref[target, at, :] = value


def correct_kernel(
    nb, edge, parents_here, tab_ref, new_ref, face_ref, mask_ref, recv_ref, cells_ref, out_ref,
    mix_ref, mean_ref, temp_ref, add_ref, base_ref,
):
    unpack_items(tab_ref, 3, 8, recv_ref, mix_ref, 40, nb, edge)
    disentangle(mix_ref, (0, FIRST_HALF), (0, SECOND_HALF), mean_ref, temp_ref, edge)
    for face in range(6):
        sign = STEP_RATIO if face % 2 else -STEP_RATIO
        beside = jnp.concatenate([mask_ref[face]] * 5, axis=0) > 0.0
        add_ref[face, 0] = jnp.where(beside, sign * (face_ref[face] - mean_ref[face, 0]), 0.0)
    base_ref[...] = new_ref[...]
    for p in range(parents_here):
        base_ref[tab_ref[9, p]] = cells_ref[p]
    expand_add(base_ref, add_ref, out_ref, 1, nb, edge)


def run(kernel, outs, operands, scratch=(), scalars=0, flops=0):
    single = isinstance(outs[0], int)
    shapes = [outs] if single else list(outs)
    smem = pl.BlockSpec(memory_space=pltpu.SMEM)
    vmem = pl.BlockSpec(memory_space=pltpu.VMEM)
    result = pl.pallas_call(
        kernel,
        out_shape=[jax.ShapeDtypeStruct(s, F32) for s in shapes],
        in_specs=[smem if k < scalars else vmem for k in range(len(operands))],
        out_specs=[vmem] * len(shapes),
        scratch_shapes=[pltpu.VMEM(s, F32) for s in scratch],
        compiler_params=pltpu.CompilerParams(vmem_limit_bytes=VMEM_LIMIT),
        cost_estimate=pl.CostEstimate(
            flops=flops, bytes_accessed=4 * sum(o.size for o in operands), transcendentals=0
        ),
    )(*operands)
    return result[0] if single else result


def level_shift(array, source):
    return lax.ppermute(array, "level", [(source, 1 - source)])


def route(buffer):
    return lax.all_to_all(buffer, "blk", split_axis=0, concat_axis=0, tiled=True)


def local(fluid_state, neighbours, parents):
    level_id = lax.axis_index("level")
    blk_index = lax.axis_index("blk")
    devices = lax.axis_size("blk")
    u = fluid_state[0]
    nb, _, edge, square = u.shape
    width = nb * edge
    parents_here = nb // 8
    capacity = 2 * ((6 * nb + devices - 1) // devices)
    per_tile = LANES // (2 * edge)
    groups = (capacity + per_tile - 1) // per_tile

    own_rows = lax.dynamic_slice_in_dim(neighbours, blk_index * nb, nb, 0)
    parent_rows = lax.dynamic_slice_in_dim(parents, blk_index * nb, nb, 0)
    parent_of = parent_rows[:, 0] - blk_index * nb
    octants = parent_rows[:, 1]
    beside = jnp.any(own_rows[:, :, None] == parents[None, None, :, 0], axis=2)
    is_parent = jnp.any(jnp.arange(nb)[:, None] == parent_of[None, :], axis=1)
    flat = own_rows.reshape(-1)
    items = jnp.arange(6 * nb, dtype=I32)
    targets = flat // nb
    faces = items % 6
    wanted = flat % nb * 6 + faces + 1 - 2 * (faces % 2)
    beside_item = beside.reshape(-1)
    parent_item = jnp.repeat(is_parent, 6)
    same = targets[:, None] == targets[None, :]
    by_own = same & (items[None, :] < items[:, None])
    by_wanted = same & (wanted[None, :] < wanted[:, None])

    def rank(order, mask=None):
        return jnp.sum(order if mask is None else order & mask[None, :], axis=1, dtype=I32)

    slot_of_block = jnp.sum(parent_of[None, :] < parent_of[:, None], axis=1, dtype=I32) // 8
    parent_list = jnp.sum(
        jnp.where(
            (slot_of_block[None, :] == jnp.arange(6 * nb)[:, None]) & (octants[None, :] == 0),
            parent_of[None, :],
            0,
        ),
        axis=1,
        dtype=I32,
    )
    table = jnp.stack(
        [
            targets,
            rank(by_own),
            rank(by_wanted),
            beside_item.astype(I32),
            parent_item.astype(I32),
            rank(by_own, beside_item),
            rank(by_wanted, parent_item),
            rank(by_own, parent_item),
            rank(by_wanted, beside_item),
            parent_list,
        ]
    )
    siblings = []
    bits = []
    keys = []
    for axis in range(3):
        bit = BIT_OF[axis]
        partner = octants + bit - 2 * bit * (octants // bit % 2)
        match = (parent_of[:, None] == parent_of[None, :]) & (octants[None, :] == partner[:, None])
        siblings.append(jnp.sum(jnp.where(match, jnp.arange(nb)[None, :], 0), axis=1, dtype=I32))
        bits.append(octants // bit % 2)
        first = octants // TANGENT[axis][0] % 2
        second = octants // TANGENT[axis][1] % 2
        keys.append(first * LANES + slot_of_block * edge + second * (edge // 2))
    along = jnp.arange(edge, dtype=I32)

    def block_major(per_block, per_edge):
        return (per_block[:, None] + per_edge[None, :]).reshape(-1)

    def edge_major(per_block, per_edge):
        return (per_block[None, :] + per_edge[:, None]).reshape(-1)

    none = 0 * along
    key_rows = [
        block_major(keys[0], along // 2),
        block_major(keys[1], along // 2),
        edge_major(keys[2], along // 2),
        block_major(siblings[1] * edge, along),
        edge_major(siblings[2], along * edge),
        block_major(bits[1], none),
        edge_major(bits[2], none),
    ]
    key_table = jnp.concatenate(
        [
            jnp.pad(jnp.stack(key_rows), ((0, 16 - len(key_rows)), (0, 0))),
            jnp.broadcast_to(siblings[0][:, None], (nb, width)),
            jnp.broadcast_to(bits[0][:, None], (nb, width)),
        ],
        axis=0,
    )
    octant_table = jnp.stack([octants, slot_of_block])
    beside_f = beside.astype(F32)
    zeros = jnp.zeros((nb, edge), F32)
    mask = jnp.stack(
        [
            jnp.broadcast_to(beside_f[:, 0][:, None], (nb, width)),
            jnp.broadcast_to(beside_f[:, 1][:, None], (nb, width)),
            jnp.broadcast_to((beside_f[:, 2][:, None] + zeros).reshape(1, -1), (nb, width)),
            jnp.broadcast_to((beside_f[:, 3][:, None] + zeros).reshape(1, -1), (nb, width)),
            jnp.broadcast_to((beside_f[:, 4][None, :] + zeros.T).reshape(1, -1), (nb, width)),
            jnp.broadcast_to((beside_f[:, 5][None, :] + zeros.T).reshape(1, -1), (nb, width)),
        ]
    )

    part = functools.partial
    cell_shape = u.shape
    plane_shape = (6, 3, 5 * edge, width)
    ghost_shape = (6, 2, 5 * edge, width)
    layer_shape = (6, 1, 5 * edge, width)
    face_shape = (6, 5 * edge, width)
    rim_shape = (5 * edge, 2 * LANES)
    wide_send = (devices, groups * 5 * edge, LANES)
    thin_rows = 5 * edge // 2
    thin_send = (devices, groups * thin_rows, LANES)
    wide_mix = (6, 2, 2, 5 * edge, LANES)
    thin_mix = (6, 2, 2, thin_rows, LANES)
    work = 220 * 3 * 5 * nb * edge * square

    planes = run(part(planes_kernel, nb, edge), plane_shape, [u])

    def interior(cells):
        return run(part(interior_kernel, nb, edge), cell_shape, [cells], flops=work)

    def coarse_first(planes, u):
        send = run(part(pack_kernel, nb, edge), wide_send, [table, planes], [wide_mix], 1)
        received = route(send)
        partial_new = interior(u)
        rims = run(
            part(rims_kernel, nb, edge, parents_here, 80), rim_shape, [table, received], (), 1
        )
        return partial_new, received, rims

    def fine_first(planes, u):
        return interior(u), jnp.zeros(wide_send, F32), jnp.zeros(rim_shape, F32)

    partial_new, received, rims = lax.cond(level_id == 0, coarse_first, fine_first, planes, u)
    early_rims = level_shift(rims, 0)

    def coarse_second(partial_new, planes, received, early_rims):
        cells, faces, send = run(
            part(coarse_kernel, nb, edge),
            [cell_shape, face_shape, thin_send],
            [table, partial_new, planes, received],
            [wide_mix, ghost_shape, ghost_shape, ghost_shape, layer_shape, thin_mix],
            1,
        )
        late = run(
            part(rims_kernel, nb, edge, parents_here, thin_rows),
            rim_shape,
            [table, route(send)],
            (),
            1,
        )
        return cells, faces, late, planes, cells

    def advance_fine(late, partial_new, planes, rim, rim2):
        return run(
            part(fine_kernel, nb, edge, late),
            [cell_shape, face_shape],
            [key_table, partial_new, planes, rim, rim2],
            [ghost_shape, ghost_shape, ghost_shape],
        )

    def fine_second(partial_new, planes, received, early_rims):
        cells, faces = advance_fine(False, partial_new, planes, early_rims, early_rims)
        new_planes = run(part(planes_kernel, nb, edge), plane_shape, [cells])
        return cells, faces, early_rims, new_planes, interior(cells)

    cells, faces, late, planes, partial_new = lax.cond(
        level_id == 0, coarse_second, fine_second, partial_new, planes, received, early_rims
    )
    late_rims = level_shift(late, 0)

    def fine_third(partial_new, planes, faces, early_rims, late_rims):
        out, more = advance_fine(True, partial_new, planes, early_rims, late_rims)
        means = run(
            part(means_kernel, nb, edge), rim_shape, [key_table, faces, more], [ghost_shape]
        )
        averages = run(
            part(averages_kernel, nb, edge),
            (parents_here,) + cell_shape[1:],
            [octant_table, out],
            (),
            1,
        )
        return out, means, averages

    def coarse_third(partial_new, planes, faces, early_rims, late_rims):
        return (
            partial_new,
            early_rims,
            jnp.zeros((parents_here,) + cell_shape[1:], F32),
        )

    out, means, averages = lax.cond(
        level_id == 0, coarse_third, fine_third, partial_new, planes, faces, early_rims, late_rims
    )
    means = level_shift(means, 1)
    averages = level_shift(averages, 1)

    def coarse_fourth(out, cells, faces, means, averages):
        send = run(
            part(return_kernel, nb, edge, parents_here), thin_send, [table, means], (), 1
        )
        return run(
            part(correct_kernel, nb, edge, parents_here),
            cell_shape,
            [table, cells, faces, mask, route(send), averages],
            [thin_mix, layer_shape, layer_shape, layer_shape, cell_shape],
            1,
        )

    def fine_fourth(out, cells, faces, means, averages):
        return out

    finished = lax.cond(
        level_id == 0, coarse_fourth, fine_fourth, out, cells, faces, means, averages
    )
    return finished[None]


def solution(mesh):
    return jax.shard_map(
        local,
        mesh=mesh,
        in_specs=(P("level", "blk", None, None, None), P(), P()),
        out_specs=P("level", "blk", None, None, None),
        check_vma=False,
    )
```

```python
import functools
import math

import jax
import jax.numpy as jnp
from jax import lax
from jax.experimental import pallas as pl
from jax.experimental.pallas import tpu as pltpu
from jax.sharding import PartitionSpec as P

GAS_GAMMA = 1.4
STEP_RATIO = 0.12
BIT_OF = (4, 2, 1)
TANGENT = ((2, 1), (4, 1), (4, 2))
F32 = jnp.float32
I32 = jnp.int32
SPARE = 8 * 1024 * 1024
LANES = 128
ROWS = 8


def iota(shape, dim):
    return lax.broadcasted_iota(I32, shape, dim)


def reciprocal(x):
    return pltpu.reciprocal(x, approx=True)


def exact_dot(a, b):
    return jnp.dot(a, b, precision=lax.Precision.HIGHEST, preferred_element_type=F32)


def physical_flux(s, n):
    inv = reciprocal(s[0])
    vn = s[n] * inv
    kinetic = s[1] * s[1] + s[2] * s[2] + s[3] * s[3]
    p = (GAS_GAMMA - 1.0) * (s[4] - 0.5 * (kinetic * inv))
    out = [s[n], s[1] * vn, s[2] * vn, s[3] * vn, (s[4] + p) * vn]
    out[n] = out[n] + p
    return out


def evolve(u, below, above, n):
    low = []
    high = []
    for c in range(5):
        d = jnp.maximum(jnp.minimum(below[c], above[c]), 0.0) + jnp.minimum(
            jnp.maximum(below[c], above[c]), 0.0
        )
        d = 0.5 * d
        low.append(u[c] - d)
        high.append(u[c] + d)
    fl = physical_flux(low, n)
    fh = physical_flux(high, n)
    for c in range(5):
        change = (0.5 * STEP_RATIO) * (fl[c] - fh[c])
        low[c] = low[c] + change
        high[c] = high[c] + change
    return low, high


def side_values(s, n):
    inv = reciprocal(s[0])
    vn = s[n] * inv
    kinetic = s[1] * s[1] + s[2] * s[2] + s[3] * s[3]
    p = (GAS_GAMMA - 1.0) * (s[4] - 0.5 * (kinetic * inv))
    square = GAS_GAMMA * p * inv
    sound = square * lax.rsqrt(square)
    return vn, p, sound


def hllc(a, b, n):
    va, pa, ca = side_values(a, n)
    vb, pb, cb = side_values(b, n)
    slow = jnp.minimum(va - ca, vb - cb)
    fast = jnp.maximum(va + ca, vb + cb)
    qa = a[0] * (slow - va)
    qb = b[0] * (fast - vb)
    contact = (pb - pa + va * qa - vb * qb) * reciprocal(qa - qb)
    is_low = contact >= 0.0

    def pick(x, y):
        return jnp.where(is_low, x, y)

    s = [pick(a[c], b[c]) for c in range(5)]
    v = pick(va, vb)
    p = pick(pa, pb)
    q = pick(qa, qb)
    speed = pick(slow, fast)
    clipped = pick(jnp.minimum(slow, 0.0), jnp.maximum(fast, 0.0))
    extra = clipped * (contact - v) * reciprocal(speed - contact)
    h = v + extra
    push = extra * q
    out = [s[0] * h, s[1] * h, s[2] * h, s[3] * h, (s[4] + p) * h + push * contact]
    out[n] = out[n] + p + push
    return out


def lane_of():
    return iota((ROWS, LANES), 1)


def row_of():
    return iota((ROWS, LANES), 0)


def take_lanes(v, index):
    return jnp.take_along_axis(v, index, axis=1, mode="promise_in_bounds")


def slide_groups(tiles, edge):
    group = lane_of() // edge
    for bit in (1, 2, 4):
        moves = (group & bit) != 0
        tiles = [jnp.where(moves, pltpu.roll(g, bit, 0), g) for g in tiles]
    return tiles


def swap_front(tiles, edge, skews):
    base = lane_of() + edge * row_of()
    return slide_groups(
        [take_lanes(v, (base + skew) % LANES) for v, skew in zip(tiles, skews)], edge
    )


def swap_back_index(lane, edge):
    return edge * ((row_of() - lane // edge + ROWS) % ROWS) + lane % edge


def extract(u_ref, plane_ref, layers, nb, edge):
    groups = LANES // edge
    for side in range(2):
        for layer in range(layers):
            x = layer if side == 0 else edge - 1 - layer
            for c in range(5):
                for half in range(2):
                    at = (layer * 2 + half) * nb
                    plane_ref[side, c, at : at + nb, :] = u_ref[
                        :, c, x, half * LANES : (half + 1) * LANES
                    ]
    lane = lane_of()
    row = row_of()
    grp = lane // edge
    sub = lane % edge
    zero = jnp.zeros((ROWS, LANES), F32)
    offsets = [o for layer in range(layers) for o in (layer, edge - 1 - layer)]

    def rows_at(layer, rt, h):
        at = (layer * 2 + rt) * nb + h * ROWS
        return slice(at, at + ROWS)

    def gather(c, carry):
        for rt in range(2):
            rows = slice(rt * ROWS, (rt + 1) * ROWS)
            ylow = [[zero, zero] for _ in range(layers)]
            yhigh = [[zero, zero] for _ in range(layers)]
            for b in range(nb):
                t = b // groups
                turn = edge * b % LANES
                low = u_ref[b, c, rows, :LANES]
                high = u_ref[b, c, rows, LANES:]
                low = pltpu.roll(low, turn, 1) if turn else low
                high = pltpu.roll(high, turn, 1) if turn else high
                for layer in range(layers):
                    ylow[layer][t] = jnp.where(grp == (b + layer) % groups, low, ylow[layer][t])
                    yhigh[layer][t] = jnp.where(
                        grp == (b + groups - 1 - layer) % groups, high, yhigh[layer][t]
                    )
            for layer in range(layers):
                for h in range(2):
                    plane_ref[2, c, rows_at(layer, rt, h), :] = ylow[layer][h]
                    plane_ref[3, c, rows_at(layer, rt, h), :] = yhigh[layer][h]
            for h in range(2):
                zacc = {o: zero for o in offsets}
                for b in range(nb):
                    r = u_ref[b, c, rows, h * LANES : (h + 1) * LANES]
                    r = pltpu.roll(r, b, 1) if b else r
                    for o in offsets:
                        zacc[o] = jnp.where(sub == (b + o) % edge, r, zacc[o])
                for layer in range(layers):
                    plane_ref[4, c, rows_at(layer, rt, h), :] = zacc[layer]
                    plane_ref[5, c, rows_at(layer, rt, h), :] = zacc[edge - 1 - layer]
        return carry

    lax.fori_loop(0, 5, gather, 0)

    def turn(c, carry):
        last = swap_back_index(lane, edge)
        places = [
            (face, rows_at(layer, rt, h), skew)
            for layer in range(layers)
            for face, skew in ((2, edge * layer), (3, edge * (groups - 1 - layer)))
            for rt in range(2)
            for h in range(2)
        ]
        tiles = swap_front(
            [plane_ref[face, c, at, :] for face, at, _ in places], edge, [p[2] for p in places]
        )
        tiles = [take_lanes(v, last) for v in tiles]
        for (face, at, _), v in zip(places, tiles):
            plane_ref[face, c, at, :] = v
        places = []
        tiles = []
        for layer in range(layers):
            for face, o in ((4, layer), (5, edge - 1 - layer)):
                for rt in range(2):
                    raw = [plane_ref[face, c, rows_at(layer, rt, h), :] for h in range(2)]
                    for h in range(2):
                        index = (edge * (sub % ROWS) + ROWS * h + (grp + row) % ROWS + o) % LANES
                        tiles.append([take_lanes(v, index) for v in raw])
                        places.append((face, rows_at(layer, rt, h)))
        tiles = slide_groups([jnp.where(sub < ROWS, v, w) for v, w in tiles], edge)
        tiles = [take_lanes(v, last) for v in tiles]
        for (face, at), v in zip(places, tiles):
            plane_ref[face, c, at, :] = v
        return carry

    lax.fori_loop(0, 5, turn, 0)


def expand_add(base_ref, add_ref, out_ref, layers, nb, edge):
    groups = LANES // edge
    lane = lane_of()
    row = row_of()
    grp = lane // edge
    sub = lane % edge

    def rows_at(layer, rt, h):
        at = (layer * 2 + rt) * nb + h * ROWS
        return slice(at, at + ROWS)

    def turn(c, carry):
        places = [
            (face, layer, rt, skew)
            for layer in range(layers)
            for face, skew in (
                (2, edge * layer),
                (3, (LANES - edge * layer) % LANES),
                (4, layer),
                (5, edge - 1 - layer),
            )
            for rt in range(2)
        ]
        loaded = [
            add_ref[face, c, rows_at(layer, rt, h), :]
            for face, layer, rt, _ in places
            for h in range(2)
        ]
        mid = swap_front(loaded, edge, [0] * len(loaded))
        out = []
        for k, (face, layer, rt, skew) in enumerate(places):
            moved = (lane - skew + LANES) % LANES
            pair = mid[2 * k : 2 * k + 2]
            if face < 4:
                index = swap_back_index(moved, edge)
                out.append([take_lanes(v, index) for v in pair])
            else:
                block = moved % edge
                base = edge * ((row - block % ROWS + ROWS) % ROWS) + moved // edge
                parts = [[take_lanes(v, base + ROWS * h) for v in pair] for h in range(2)]
                out.append([jnp.where(block < ROWS, v, w) for v, w in parts])
        for (face, layer, rt, _), pair in zip(places, out):
            for h in range(2):
                add_ref[face, c, rows_at(layer, rt, h), :] = pair[h]
        return carry

    lax.fori_loop(0, 5, turn, 0)

    def spread(c, carry):
        for rt in range(2):
            rows = slice(rt * ROWS, (rt + 1) * ROWS)

            def tile(face, h):
                return [add_ref[face, c, rows_at(layer, rt, h), :] for layer in range(layers)]

            ylow = [tile(2, h) for h in range(2)]
            yhigh = [tile(3, h) for h in range(2)]
            zlow = [tile(4, h) for h in range(2)]
            zhigh = [tile(5, h) for h in range(2)]
            for b in range(nb):
                t = b // groups
                place = b % groups
                low = ylow[t][0]
                high = yhigh[t][0]
                if layers > 1:
                    low = jnp.where(grp == place, low, ylow[t][1])
                    high = jnp.where(grp == place, high, yhigh[t][1])
                low = pltpu.roll(low, (LANES - edge * place) % LANES, 1)
                high = pltpu.roll(high, edge * (groups - 1 - place) % LANES, 1)
                parts = [
                    jnp.where(grp < layers, low, 0.0),
                    jnp.where(grp >= groups - layers, high, 0.0),
                ]
                for h in range(2):
                    lanes = slice(h * LANES, (h + 1) * LANES)
                    z = zhigh[h][0]
                    if layers > 1:
                        z = jnp.where(sub == (b + edge - 1) % edge, z, zhigh[h][1])
                        z = jnp.where(sub == (b + 1) % edge, zlow[h][1], z)
                    z = jnp.where(sub == b, zlow[h][0], z)
                    if b:
                        z = pltpu.roll(z, LANES - b, 1)
                    total = parts[h] + jnp.where((sub < layers) | (sub >= edge - layers), z, 0.0)
                    x = add_ref[rt, c, h * nb + b : h * nb + b + 1, :]
                    x = jnp.where(row == (ROWS - 1) * rt, x, 0.0)
                    if layers > 1:
                        deeper = add_ref[rt, c, (2 + h) * nb + b : (2 + h) * nb + b + 1, :]
                        x = jnp.where(row == 1 + (ROWS - 3) * rt, deeper, x)
                    out_ref[b, c, rows, lanes] = base_ref[b, c, rows, lanes] + (total + x)
        return carry

    lax.fori_loop(0, 5, spread, 0)


def block_rows(block, nb, count):
    return pl.ds(block, count, stride=nb)


def pack(tab_ref, valid_row, slot_row, plane_ref, send_ref, count, nb):
    for face in range(6):
        for block in range(nb):
            item = block * 6 + face

            def move(item=item, face=face, block=block):
                target = tab_ref[0, item]
                first = tab_ref[slot_row, item] * 5
                for c in range(5):
                    send_ref[target, first + c] = plane_ref[
                        face, c, block_rows(block, nb, count), :
                    ]

            if valid_row is None:
                move()
            else:
                pl.when(tab_ref[valid_row, item] > 0)(move)


def unpack(tab_ref, valid_row, slot_row, recv_ref, plane_ref, count, nb):
    for face in range(6):
        for block in range(nb):
            item = block * 6 + face

            def move(item=item, face=face, block=block):
                target = tab_ref[0, item]
                first = tab_ref[slot_row, item] * 5
                for c in range(5):
                    plane_ref[face, c, block_rows(block, nb, count), :] = recv_ref[
                        target, first + c
                    ]

            if valid_row is None:
                move()
            else:
                pl.when(tab_ref[valid_row, item] > 0)(move)


def take_rims(tab_ref, slot_row, recv_ref, rim_ref, parents_here):
    for face in range(6):
        for p in range(parents_here):
            item = tab_ref[9, p] * 6 + face
            target = tab_ref[0, item]
            first = tab_ref[slot_row, item] * 5
            for c in range(5):
                rim_ref[face, c, 2 * p : 2 * p + 2, :] = recv_ref[target, first + c, 0:2, :]


def interior(nb, edge, u_ref, d_ref):
    square = edge * edge

    def sweep(u, axis, index, size, step, dim):
        n = 1 + axis
        below = [x - pltpu.roll(x, step, dim) for x in u]
        above = [pltpu.roll(x, size - step, dim) for x in below]
        low, high = evolve(u, below, above, n)
        prev = [pltpu.roll(x, step, dim) for x in high]
        inside = (index >= 2) & (index <= edge - 2)
        flux = [jnp.where(inside, x, 0.0) for x in hllc(prev, low, n)]
        return [pltpu.roll(x, size - step, dim) - x for x in flux]

    def body(b, carry):
        for rt in range(edge // ROWS):
            rows = slice(rt * ROWS, (rt + 1) * ROWS)
            u = [u_ref[b, c, rows, :] for c in range(5)]
            div = sweep(u, 1, iota((ROWS, square), 1) // edge, square, edge, 1)
            for c in range(5):
                d_ref[b, c, rows, :] = u[c] - STEP_RATIO * div[c]
        for half in range(square // LANES):
            lanes = slice(half * LANES, (half + 1) * LANES)
            u = [u_ref[b, c, :, lanes] for c in range(5)]
            div = sweep(u, 0, iota((edge, LANES), 0), edge, 1, 0)
            more = sweep(u, 2, iota((edge, LANES), 1) % edge, LANES, 1, 1)
            for c in range(5):
                d_ref[b, c, :, lanes] = d_ref[b, c, :, lanes] - STEP_RATIO * (div[c] + more[c])
        return carry

    lax.fori_loop(0, nb, body, 0)


def face_fluxes(plane_ref, ghost_ref, add_ref, face_ref, nb):
    for face in range(6):
        axis = face // 2
        side = face % 2
        n = 1 + axis
        sign = 1.0 - 2.0 * side

        def body(half, carry):
            def rows(layer):
                return pl.ds(pl.multiple_of((layer * 2 + half) * nb, ROWS), nb)

            def load(ref, layer):
                return [ref[face, c, rows(layer), :] for c in range(5)]

            near, mid, deep = (load(plane_ref, layer) for layer in range(3))
            ghost, far = (load(ghost_ref, layer) for layer in range(2))

            def steps(a, b):
                return [sign * (y - x) for x, y in zip(a, b)]

            d0, d1, d2, d3 = steps(far, ghost), steps(ghost, near), steps(near, mid), steps(mid, deep)
            if side == 0:
                first = hllc(evolve(ghost, d0, d1, n)[1], evolve(near, d1, d2, n)[0], n)
                second = hllc(evolve(near, d1, d2, n)[1], evolve(mid, d2, d3, n)[0], n)
            else:
                first = hllc(evolve(near, d1, d2, n)[1], evolve(ghost, d0, d1, n)[0], n)
                second = hllc(evolve(mid, d2, d3, n)[1], evolve(near, d1, d2, n)[0], n)
            for c in range(5):
                face_ref[face, c, rows(0), :] = first[c]
                add_ref[face, c, rows(0), :] = (sign * STEP_RATIO) * (first[c] - second[c])
                add_ref[face, c, rows(1), :] = (sign * STEP_RATIO) * second[c]
            return carry

        lax.fori_loop(0, 2, body, 0)


def inner_kernel(nb, edge, u_ref, d_ref, plane_ref):
    extract(u_ref, plane_ref, 3, nb, edge)
    interior(nb, edge, u_ref, d_ref)


def send_kernel(nb, edge, tab_ref, u_ref, send_ref, plane_ref):
    extract(u_ref, plane_ref, 2, nb, edge)
    pack(tab_ref, None, 1, plane_ref, send_ref, 4, nb)


def coarse_kernel(
    nb, edge, parents_here, tab_ref, d_ref, plane_ref, recv_ref, new_ref, face_ref, send_ref,
    rim_ref, ghost_ref, add_ref, near_ref,
):
    take_rims(tab_ref, 2, recv_ref, rim_ref, parents_here)
    unpack(tab_ref, None, 2, recv_ref, ghost_ref, 4, nb)
    face_fluxes(plane_ref, ghost_ref, add_ref, face_ref, nb)
    expand_add(d_ref, add_ref, new_ref, 2, nb, edge)
    extract(new_ref, near_ref, 1, nb, edge)
    pack(tab_ref, 3, 5, near_ref, send_ref, 2, nb)


def rims_kernel(parents_here, tab_ref, recv_ref, rim_ref):
    take_rims(tab_ref, 6, recv_ref, rim_ref, parents_here)


def fine_ghosts(nb, edge, fam_ref, bits_ref, plane_ref, rim_ref, rim2_ref, ghost_ref, parents_here):
    lane = lane_of()
    for face in range(6):
        axis = face // 2
        side = face % 2
        opposite = face + 1 - 2 * side
        for block in range(nb):
            sibling = fam_ref[2 + axis, block]
            for c in range(5):
                ghost_ref[face, c, block_rows(block, nb, 4), :] = plane_ref[
                    opposite, c, block_rows(sibling, nb, 4), :
                ]
        for rt in range(nb // ROWS):
            octant = bits_ref[rt * ROWS : (rt + 1) * ROWS, :]
            slot = bits_ref[nb + rt * ROWS : nb + (rt + 1) * ROWS, :]
            outward = (octant // BIT_OF[axis]) % 2 == side
            first = (octant // TANGENT[axis][0]) % 2
            second = (octant // TANGENT[axis][1]) % 2
            which = 2 * slot + first
            for c in range(5):
                rims = rim_ref[face, c]
                if rim2_ref is not None:
                    rims = 0.5 * (rims + rim2_ref[face, c])
                source = jnp.broadcast_to(rims[0:1, :], (ROWS, LANES))
                for k in range(1, 2 * parents_here):
                    source = jnp.where(which == k, rims[k : k + 1, :], source)
                for half in range(2):
                    index = (
                        edge * ((edge // 4) * half + lane // edge // 2)
                        + (edge // 2) * second
                        + lane % edge // 2
                    )
                    outer = take_lanes(source, index)
                    for layer in range(2):
                        at = (layer * 2 + half) * nb + rt * ROWS
                        at = slice(at, at + ROWS)
                        ghost_ref[face, c, at, :] = jnp.where(
                            outward, outer, ghost_ref[face, c, at, :]
                        )


def fine_kernel(
    nb, edge, parents_here, fam_ref, bits_ref, d_ref, plane_ref, rim_ref, new_ref, face_ref,
    ghost_ref, add_ref,
):
    fine_ghosts(nb, edge, fam_ref, bits_ref, plane_ref, rim_ref, None, ghost_ref, parents_here)
    face_fluxes(plane_ref, ghost_ref, add_ref, face_ref, nb)
    expand_add(d_ref, add_ref, new_ref, 2, nb, edge)


def face_means(nb, edge, parents_here, fam_ref, one_ref, two_ref, mean_ref, quarter_ref):
    lane = lane_of()
    group = lane // edge
    sub = lane % edge
    index = edge * (2 * (group % (ROWS // 2))) + 2 * (sub % (edge // 2))
    for face in range(6):
        places = [
            (c, slice(half * nb + rt * ROWS, half * nb + (rt + 1) * ROWS))
            for c in range(5)
            for rt in range(nb // ROWS)
            for half in range(2)
        ]
        tiles = [one_ref[face, c, at, :] + two_ref[face, c, at, :] for c, at in places]
        tiles = [v + pltpu.roll(v, LANES - 1, 1) for v in tiles]
        tiles = [v + pltpu.roll(v, LANES - edge, 1) for v in tiles]
        tiles = [0.125 * take_lanes(v, index) for v in tiles]
        for k in range(0, len(tiles), 2):
            at = k // 2 * ROWS
            quarter_ref[face, at : at + ROWS, :] = jnp.where(
                group < ROWS // 2, tiles[k], tiles[k + 1]
            )
    left = iota((5, LANES), 1) % edge < edge // 2
    for face in range(6):
        axis = face // 2
        for p in range(parents_here):
            for half in range(2):
                octant = (face % 2) * BIT_OF[axis] + half * TANGENT[axis][0]
                one = fam_ref[5 + p, octant]
                two = fam_ref[5 + p, octant + TANGENT[axis][1]]
                value = jnp.where(
                    left,
                    quarter_ref[face, pl.ds(one, 5, stride=nb), :],
                    quarter_ref[face, pl.ds(two, 5, stride=nb), :],
                )
                for c in range(5):
                    mean_ref[face, c, 2 * p + half : 2 * p + half + 1, :] = value[c : c + 1, :]


def last_fine_kernel(
    nb, edge, parents_here, fam_ref, bits_ref, d_ref, plane_ref, rim_ref, rim2_ref, one_ref,
    new_ref, mean_ref, ghost_ref, add_ref, face_ref, quarter_ref,
):
    fine_ghosts(nb, edge, fam_ref, bits_ref, plane_ref, rim_ref, rim2_ref, ghost_ref, parents_here)
    face_fluxes(plane_ref, ghost_ref, add_ref, face_ref, nb)
    face_means(nb, edge, parents_here, fam_ref, one_ref, face_ref, mean_ref, quarter_ref)
    expand_add(d_ref, add_ref, new_ref, 2, nb, edge)


def averages_kernel(nb, edge, family_ref, u_ref, out_ref):
    square = edge * edge
    half = edge // 2
    i = iota((square, LANES), 0)
    pairs = jnp.where(
        iota((square, LANES), 1) == (i // edge // 2) * edge + (i % edge) // 2, 0.125, 0.0
    ).astype(F32)
    i = iota((5 * half, 5 * edge), 0)
    j = iota((5 * half, 5 * edge), 1)
    rows = jnp.where(j // 2 == i, 1.0, 0.0).astype(F32)
    high = (iota((5 * half, LANES), 1) % edge) // half
    out_ref[...] = jnp.zeros(out_ref.shape, F32)

    def body(b, carry):
        octant = family_ref[0, b]
        p = family_ref[1, b]
        oz = octant % 2
        u = u_ref[b].reshape(5 * edge, square)
        v = exact_dot(rows, exact_dot(u, pairs))
        v = jnp.where(high == oz, pltpu.roll(v, half * oz, 1), 0.0)
        lanes = pl.ds(pl.multiple_of((octant // 2 % 2) * LANES, LANES), LANES)
        at = pl.ds(pl.multiple_of((octant // 4) * ROWS, ROWS), ROWS)
        for c in range(5):
            out_ref[p, c, at, lanes] = out_ref[p, c, at, lanes] + v[c * half : (c + 1) * half, :]
        return carry

    lax.fori_loop(0, nb, body, 0)


def return_kernel(parents_here, tab_ref, mean_ref, send_ref):
    for face in range(6):
        for p in range(parents_here):
            item = tab_ref[9, p] * 6 + face
            target = tab_ref[0, item]
            first = tab_ref[7, item] * 5
            for c in range(5):
                send_ref[target, first + c] = mean_ref[face, c, 2 * p : 2 * p + 2, :]


def correct_kernel(
    nb, edge, parents_here, tab_ref, bits_ref, new_ref, face_ref, recv_ref, cells_ref, out_ref,
    mean_ref, add_ref, base_ref,
):
    unpack(tab_ref, 3, 8, recv_ref, mean_ref, 2, nb)
    beside = bits_ref[2 * nb : 3 * nb, :]
    for face in range(6):
        sign = STEP_RATIO if face % 2 else -STEP_RATIO
        hit = (beside // (1 << face)) % 2 > 0
        for c in range(5):
            for half in range(2):
                at = slice(half * nb, (half + 1) * nb)
                add_ref[face, c, at, :] = jnp.where(
                    hit, sign * (face_ref[face, c, at, :] - mean_ref[face, c, at, :]), 0.0
                )
    base_ref[...] = new_ref[...]
    for p in range(parents_here):
        base_ref[tab_ref[9, p]] = cells_ref[p]
    expand_add(base_ref, add_ref, out_ref, 1, nb, edge)


def run(kernel, outs, operands, scratch=(), scalars=0, flops=0):
    single = isinstance(outs[0], int)
    shapes = [outs] if single else list(outs)
    held = [o.shape for o in operands] + shapes + list(scratch)
    limit = sum(4 * max(math.prod(s), 8 * LANES) for s in held) + SPARE
    smem = pl.BlockSpec(memory_space=pltpu.SMEM)
    vmem = pl.BlockSpec(memory_space=pltpu.VMEM)
    result = pl.pallas_call(
        kernel,
        out_shape=[jax.ShapeDtypeStruct(s, F32) for s in shapes],
        in_specs=[smem if k < scalars else vmem for k in range(len(operands))],
        out_specs=[vmem] * len(shapes),
        scratch_shapes=[pltpu.VMEM(s, F32) for s in scratch],
        compiler_params=pltpu.CompilerParams(vmem_limit_bytes=limit),
        cost_estimate=pl.CostEstimate(
            flops=flops, bytes_accessed=4 * sum(o.size for o in operands), transcendentals=0
        ),
    )(*operands)
    return result[0] if single else result


def blank(*shapes):
    return pl.pallas_call(
        lambda *refs: None,
        out_shape=[jax.ShapeDtypeStruct(s, F32) for s in shapes],
        out_specs=[pl.BlockSpec(memory_space=pl.ANY)] * len(shapes),
    )()


def level_shift(array, source):
    return lax.ppermute(array, "level", [(source, 1 - source)])


def route(buffer):
    return lax.all_to_all(buffer, "blk", split_axis=0, concat_axis=0, tiled=True)


def local(fluid_state, neighbours, parents):
    level_id = lax.axis_index("level")
    blk_index = lax.axis_index("blk")
    devices = lax.axis_size("blk")
    u = fluid_state[0]
    nb, _, edge, square = u.shape
    parents_here = nb // 8
    capacity = 2 * ((6 * nb + devices - 1) // devices)

    own_rows = lax.dynamic_slice_in_dim(neighbours, blk_index * nb, nb, 0)
    parent_rows = lax.dynamic_slice_in_dim(parents, blk_index * nb, nb, 0)
    parent_of = parent_rows[:, 0] - blk_index * nb
    octants = parent_rows[:, 1]
    beside = jnp.any(own_rows[:, :, None] == parents[None, None, :, 0], axis=2)
    is_parent = jnp.any(jnp.arange(nb)[:, None] == parent_of[None, :], axis=1)
    flat = own_rows.reshape(-1)
    items = jnp.arange(6 * nb, dtype=I32)
    targets = flat // nb
    faces = items % 6
    wanted = flat % nb * 6 + faces + 1 - 2 * (faces % 2)
    beside_item = beside.reshape(-1)
    parent_item = jnp.repeat(is_parent, 6)
    same = targets[:, None] == targets[None, :]
    by_own = same & (items[None, :] < items[:, None])
    by_wanted = same & (wanted[None, :] < wanted[:, None])

    def rank(order, mask=None):
        return jnp.sum(order if mask is None else order & mask[None, :], axis=1, dtype=I32)

    slot_of_block = jnp.sum(parent_of[None, :] < parent_of[:, None], axis=1, dtype=I32) // 8
    parent_list = jnp.sum(
        jnp.where(
            (slot_of_block[None, :] == jnp.arange(6 * nb)[:, None]) & (octants[None, :] == 0),
            parent_of[None, :],
            0,
        ),
        axis=1,
        dtype=I32,
    )
    table = jnp.stack(
        [
            targets,
            rank(by_own),
            rank(by_wanted),
            beside_item.astype(I32),
            parent_item.astype(I32),
            rank(by_own, beside_item),
            rank(by_wanted, parent_item),
            rank(by_own, parent_item),
            rank(by_wanted, beside_item),
            parent_list,
        ]
    )
    blocks = jnp.arange(nb, dtype=I32)
    family = [octants, slot_of_block]
    for axis in range(3):
        bit = BIT_OF[axis]
        partner = octants + bit - 2 * bit * (octants // bit % 2)
        match = (parent_of[:, None] == parent_of[None, :]) & (octants[None, :] == partner[:, None])
        family.append(jnp.sum(jnp.where(match, blocks[None, :], 0), axis=1, dtype=I32))
    for p in range(parents_here):
        match = (slot_of_block[None, :] == p) & (octants[None, :] == blocks[:, None])
        family.append(jnp.sum(jnp.where(match, blocks[None, :], 0), axis=1, dtype=I32))
    family = jnp.stack(family)
    beside_bits = jnp.sum(
        beside.astype(I32) * (1 << jnp.arange(6, dtype=I32))[None, :], axis=1, dtype=I32
    )
    bits = jnp.broadcast_to(
        jnp.concatenate([octants, slot_of_block, beside_bits])[:, None], (3 * nb, LANES)
    )

    part = functools.partial
    cell_shape = u.shape
    plane_shape = (6, 5, 6 * nb, LANES)
    ghost_shape = (6, 5, 4 * nb, LANES)
    face_shape = (6, 5, 2 * nb, LANES)
    rim_shape = (6, 5, 2 * parents_here, LANES)
    wide_send = (devices, capacity * 5, 4, LANES)
    thin_send = (devices, capacity * 5, 2, LANES)
    average_shape = (parents_here,) + cell_shape[1:]
    work = 220 * 3 * 5 * nb * edge * square

    def inner(cells):
        return run(part(inner_kernel, nb, edge), [cell_shape, plane_shape], [cells], flops=work)

    def coarse_first(u):
        send = run(part(send_kernel, nb, edge), wide_send, [table, u], [ghost_shape], 1)
        received = route(send)
        partial_new, planes = inner(u)
        cells, faces, send, rims = run(
            part(coarse_kernel, nb, edge, parents_here),
            [cell_shape, face_shape, thin_send, rim_shape],
            [table, partial_new, planes, received],
            [ghost_shape, ghost_shape, face_shape],
            1,
        )
        (unused,) = blank(plane_shape)
        return cells, faces, send, rims, unused

    def fine_first(u):
        partial_new, planes = inner(u)
        faces, send, rims = blank(face_shape, thin_send, rim_shape)
        return partial_new, faces, send, rims, planes

    cells, faces, send, rims, planes = lax.cond(level_id == 0, coarse_first, fine_first, u)
    early_rims = level_shift(rims, 0)

    def coarse_second(cells, send, planes, early_rims):
        late = run(
            part(rims_kernel, parents_here), rim_shape, [table, route(send)], (), 1
        )
        return (late, *blank(cell_shape, plane_shape, face_shape))

    def fine_second(cells, send, planes, early_rims):
        half, faces = run(
            part(fine_kernel, nb, edge, parents_here),
            [cell_shape, face_shape],
            [family, bits, cells, planes, early_rims],
            [ghost_shape, ghost_shape],
            1,
        )
        (late,) = blank(rim_shape)
        return (late, *inner(half), faces)

    late, half_cells, half_planes, half_faces = lax.cond(
        level_id == 0, coarse_second, fine_second, cells, send, planes, early_rims
    )
    late_rims = level_shift(late, 0)

    def coarse_third(half_cells, half_planes, half_faces, early_rims, late_rims):
        return tuple(blank(cell_shape, rim_shape))

    def fine_third(half_cells, half_planes, half_faces, early_rims, late_rims):
        return tuple(
            run(
                part(last_fine_kernel, nb, edge, parents_here),
                [cell_shape, rim_shape],
                [family, bits, half_cells, half_planes, early_rims, late_rims, half_faces],
                [ghost_shape, ghost_shape, face_shape, (6, 5 * nb, LANES)],
                1,
            )
        )

    out, means = lax.cond(
        level_id == 0, coarse_third, fine_third,
        half_cells, half_planes, half_faces, early_rims, late_rims,
    )
    means = level_shift(means, 1)

    def coarse_fourth(means, out):
        send = run(part(return_kernel, parents_here), thin_send, [table, means], (), 1)
        return route(send), blank(average_shape)[0]

    def fine_fourth(means, out):
        averages = run(part(averages_kernel, nb, edge), average_shape, [family, out], (), 1)
        return blank(thin_send)[0], averages

    returned, averages = lax.cond(level_id == 0, coarse_fourth, fine_fourth, means, out)
    averages = level_shift(averages, 1)

    def correct(out, cells, faces, returned, averages):
        return run(
            part(correct_kernel, nb, edge, parents_here),
            cell_shape,
            [table, bits, cells, faces, returned, averages],
            [face_shape, face_shape, cell_shape],
            1,
        )

    finished = lax.cond(
        level_id == 0, correct, lambda out, *rest: out, out, cells, faces, returned, averages
    )
    return finished[None]


def solution(mesh):
    return jax.shard_map(
        local,
        mesh=mesh,
        in_specs=(P("level", "blk", None, None, None), P(), P()),
        out_specs=P("level", "blk", None, None, None),
        check_vma=False,
    )
```

```python
import functools
import math

import jax
import jax.numpy as jnp
from jax import lax
from jax.experimental import pallas as pl
from jax.experimental.pallas import tpu as pltpu
from jax.sharding import PartitionSpec as P

GAS_GAMMA = 1.4
STEP_RATIO = 0.12
BIT_OF = (4, 2, 1)
TANGENT = ((2, 1), (4, 1), (4, 2))
F32 = jnp.float32
I32 = jnp.int32
SPARE = 8 * 1024 * 1024
LANES = 128
ROWS = 8


def iota(shape, dim):
    return lax.broadcasted_iota(I32, shape, dim)


def reciprocal(x):
    return pltpu.reciprocal(x, approx=True)


def physical_flux(s, n):
    inv = reciprocal(s[0])
    vn = s[n] * inv
    kinetic = s[1] * s[1] + s[2] * s[2] + s[3] * s[3]
    p = (GAS_GAMMA - 1.0) * (s[4] - 0.5 * (kinetic * inv))
    out = [s[n], s[1] * vn, s[2] * vn, s[3] * vn, (s[4] + p) * vn]
    out[n] = out[n] + p
    return out


def evolve(u, below, above, n):
    low = []
    high = []
    for c in range(5):
        d = jnp.maximum(jnp.minimum(below[c], above[c]), 0.0) + jnp.minimum(
            jnp.maximum(below[c], above[c]), 0.0
        )
        d = 0.5 * d
        low.append(u[c] - d)
        high.append(u[c] + d)
    fl = physical_flux(low, n)
    fh = physical_flux(high, n)
    for c in range(5):
        change = (0.5 * STEP_RATIO) * (fl[c] - fh[c])
        low[c] = low[c] + change
        high[c] = high[c] + change
    return low, high


def side_values(s, n):
    inv = reciprocal(s[0])
    vn = s[n] * inv
    kinetic = s[1] * s[1] + s[2] * s[2] + s[3] * s[3]
    p = (GAS_GAMMA - 1.0) * (s[4] - 0.5 * (kinetic * inv))
    square = GAS_GAMMA * p * inv
    sound = square * lax.rsqrt(square)
    return vn, p, sound


def hllc(a, b, n):
    va, pa, ca = side_values(a, n)
    vb, pb, cb = side_values(b, n)
    slow = jnp.minimum(va - ca, vb - cb)
    fast = jnp.maximum(va + ca, vb + cb)
    qa = a[0] * (slow - va)
    qb = b[0] * (fast - vb)
    contact = (pb - pa + va * qa - vb * qb) * reciprocal(qa - qb)
    is_low = contact >= 0.0

    def pick(x, y):
        return jnp.where(is_low, x, y)

    s = [pick(a[c], b[c]) for c in range(5)]
    v = pick(va, vb)
    p = pick(pa, pb)
    q = pick(qa, qb)
    speed = pick(slow, fast)
    clipped = pick(jnp.minimum(slow, 0.0), jnp.maximum(fast, 0.0))
    extra = clipped * (contact - v) * reciprocal(speed - contact)
    h = v + extra
    push = extra * q
    out = [s[0] * h, s[1] * h, s[2] * h, s[3] * h, (s[4] + p) * h + push * contact]
    out[n] = out[n] + p + push
    return out


def lane_of():
    return iota((ROWS, LANES), 1)


def row_of():
    return iota((ROWS, LANES), 0)


def take_lanes(v, index):
    return jnp.take_along_axis(v, index, axis=1, mode="promise_in_bounds")


def slide_groups(tiles, edge):
    group = lane_of() // edge
    for bit in (1, 2, 4):
        moves = (group & bit) != 0
        tiles = [jnp.where(moves, pltpu.roll(g, bit, 0), g) for g in tiles]
    return tiles


def swap_front(tiles, edge, skews):
    base = lane_of() + edge * row_of()
    return slide_groups(
        [take_lanes(v, (base + skew) % LANES) for v, skew in zip(tiles, skews)], edge
    )


def swap_back_index(lane, edge):
    return edge * ((row_of() - lane // edge + ROWS) % ROWS) + lane % edge


def extract(u_ref, plane_ref, layers, nb, edge):
    groups = LANES // edge
    for side in range(2):
        for layer in range(layers):
            x = layer if side == 0 else edge - 1 - layer
            for c in range(5):
                for half in range(2):
                    at = (layer * 2 + half) * nb
                    plane_ref[side, c, at : at + nb, :] = u_ref[
                        :, c, x, half * LANES : (half + 1) * LANES
                    ]
    lane = lane_of()
    row = row_of()
    grp = lane // edge
    sub = lane % edge
    zero = jnp.zeros((ROWS, LANES), F32)
    offsets = [o for layer in range(layers) for o in (layer, edge - 1 - layer)]

    def rows_at(layer, rt, h):
        at = (layer * 2 + rt) * nb + h * ROWS
        return slice(at, at + ROWS)

    def gather(c, carry):
        for rt in range(2):
            rows = slice(rt * ROWS, (rt + 1) * ROWS)
            ylow = [[zero, zero] for _ in range(layers)]
            yhigh = [[zero, zero] for _ in range(layers)]
            for b in range(nb):
                t = b // groups
                turn = edge * b % LANES
                low = u_ref[b, c, rows, :LANES]
                high = u_ref[b, c, rows, LANES:]
                low = pltpu.roll(low, turn, 1) if turn else low
                high = pltpu.roll(high, turn, 1) if turn else high
                for layer in range(layers):
                    ylow[layer][t] = jnp.where(grp == (b + layer) % groups, low, ylow[layer][t])
                    yhigh[layer][t] = jnp.where(
                        grp == (b + groups - 1 - layer) % groups, high, yhigh[layer][t]
                    )
            for layer in range(layers):
                for h in range(2):
                    plane_ref[2, c, rows_at(layer, rt, h), :] = ylow[layer][h]
                    plane_ref[3, c, rows_at(layer, rt, h), :] = yhigh[layer][h]
            for h in range(2):
                zacc = {o: zero for o in offsets}
                for b in range(nb):
                    r = u_ref[b, c, rows, h * LANES : (h + 1) * LANES]
                    r = pltpu.roll(r, b, 1) if b else r
                    for o in offsets:
                        zacc[o] = jnp.where(sub == (b + o) % edge, r, zacc[o])
                for layer in range(layers):
                    plane_ref[4, c, rows_at(layer, rt, h), :] = zacc[layer]
                    plane_ref[5, c, rows_at(layer, rt, h), :] = zacc[edge - 1 - layer]
        return carry

    lax.fori_loop(0, 5, gather, 0)

    def turn(c, carry):
        last = swap_back_index(lane, edge)
        places = [
            (face, rows_at(layer, rt, h), skew)
            for layer in range(layers)
            for face, skew in ((2, edge * layer), (3, edge * (groups - 1 - layer)))
            for rt in range(2)
            for h in range(2)
        ]
        tiles = swap_front(
            [plane_ref[face, c, at, :] for face, at, _ in places], edge, [p[2] for p in places]
        )
        tiles = [take_lanes(v, last) for v in tiles]
        for (face, at, _), v in zip(places, tiles):
            plane_ref[face, c, at, :] = v
        places = []
        tiles = []
        for layer in range(layers):
            for face, o in ((4, layer), (5, edge - 1 - layer)):
                for rt in range(2):
                    raw = [plane_ref[face, c, rows_at(layer, rt, h), :] for h in range(2)]
                    for h in range(2):
                        index = (edge * (sub % ROWS) + ROWS * h + (grp + row) % ROWS + o) % LANES
                        tiles.append([take_lanes(v, index) for v in raw])
                        places.append((face, rows_at(layer, rt, h)))
        tiles = slide_groups([jnp.where(sub < ROWS, v, w) for v, w in tiles], edge)
        tiles = [take_lanes(v, last) for v in tiles]
        for (face, at), v in zip(places, tiles):
            plane_ref[face, c, at, :] = v
        return carry

    lax.fori_loop(0, 5, turn, 0)


def expand_add(base_ref, add_ref, out_ref, layers, nb, edge, split_ref=None):
    groups = LANES // edge
    lane = lane_of()
    row = row_of()
    grp = lane // edge
    sub = lane % edge

    def rows_at(layer, rt, h):
        at = (layer * 2 + rt) * nb + h * ROWS
        return slice(at, at + ROWS)

    def turn(c, carry):
        places = [
            (face, layer, rt, skew)
            for layer in range(layers)
            for face, skew in (
                (2, edge * layer),
                (3, (LANES - edge * layer) % LANES),
                (4, layer),
                (5, edge - 1 - layer),
            )
            for rt in range(2)
        ]
        loaded = [
            add_ref[face, c, rows_at(layer, rt, h), :]
            for face, layer, rt, _ in places
            for h in range(2)
        ]
        mid = swap_front(loaded, edge, [0] * len(loaded))
        out = []
        for k, (face, layer, rt, skew) in enumerate(places):
            moved = (lane - skew + LANES) % LANES
            pair = mid[2 * k : 2 * k + 2]
            if face < 4:
                index = swap_back_index(moved, edge)
                out.append([take_lanes(v, index) for v in pair])
            else:
                block = moved % edge
                base = edge * ((row - block % ROWS + ROWS) % ROWS) + moved // edge
                parts = [[take_lanes(v, base + ROWS * h) for v in pair] for h in range(2)]
                out.append([jnp.where(block < ROWS, v, w) for v, w in parts])
        for (face, layer, rt, _), pair in zip(places, out):
            for h in range(2):
                add_ref[face, c, rows_at(layer, rt, h), :] = pair[h]
        return carry

    lax.fori_loop(0, 5, turn, 0)

    def spread(c, carry):
        for rt in range(2):
            rows = slice(rt * ROWS, (rt + 1) * ROWS)

            def tile(face, h):
                return [add_ref[face, c, rows_at(layer, rt, h), :] for layer in range(layers)]

            ylow = [tile(2, h) for h in range(2)]
            yhigh = [tile(3, h) for h in range(2)]
            zlow = [tile(4, h) for h in range(2)]
            zhigh = [tile(5, h) for h in range(2)]
            for b in range(nb):
                t = b // groups
                place = b % groups
                low = ylow[t][0]
                high = yhigh[t][0]
                if layers > 1:
                    low = jnp.where(grp == place, low, ylow[t][1])
                    high = jnp.where(grp == place, high, yhigh[t][1])
                low = pltpu.roll(low, (LANES - edge * place) % LANES, 1)
                high = pltpu.roll(high, edge * (groups - 1 - place) % LANES, 1)
                parts = [
                    jnp.where(grp < layers, low, 0.0),
                    jnp.where(grp >= groups - layers, high, 0.0),
                ]
                for h in range(2):
                    lanes = slice(h * LANES, (h + 1) * LANES)
                    z = zhigh[h][0]
                    if layers > 1:
                        z = jnp.where(sub == (b + edge - 1) % edge, z, zhigh[h][1])
                        z = jnp.where(sub == (b + 1) % edge, zlow[h][1], z)
                    z = jnp.where(sub == b, zlow[h][0], z)
                    if b:
                        z = pltpu.roll(z, LANES - b, 1)
                    total = parts[h] + jnp.where((sub < layers) | (sub >= edge - layers), z, 0.0)
                    x = add_ref[rt, c, h * nb + b : h * nb + b + 1, :]
                    x = jnp.where(row == (ROWS - 1) * rt, x, 0.0)
                    if layers > 1:
                        deeper = add_ref[rt, c, (2 + h) * nb + b : (2 + h) * nb + b + 1, :]
                        x = jnp.where(row == 1 + (ROWS - 3) * rt, deeper, x)
                    value = base_ref[b, c, rows, lanes] + (total + x)
                    out_ref[b, c, rows, lanes] = value
                    if split_ref is not None:
                        split_ref[b, c, h, rows, :] = value
        return carry

    lax.fori_loop(0, 5, spread, 0)


def block_rows(block, nb, count):
    return pl.ds(block, count, stride=nb)


def pack(tab_ref, valid_row, slot_row, plane_ref, send_ref, count, nb):
    for face in range(6):
        for block in range(nb):
            item = face * nb + block

            def move(item=item, face=face, block=block):
                target = tab_ref[0, item]
                first = tab_ref[slot_row, item] * 5
                for c in range(5):
                    send_ref[target, first + c] = plane_ref[
                        face, c, block_rows(block, nb, count), :
                    ]

            if valid_row is None:
                move()
            else:
                pl.when(tab_ref[valid_row, item] > 0)(move)


def unpack(tab_ref, valid_row, slot_row, recv_ref, plane_ref, count, nb):
    for face in range(6):
        for block in range(nb):
            item = face * nb + block

            def move(item=item, face=face, block=block):
                target = tab_ref[0, item]
                first = tab_ref[slot_row, item] * 5
                for c in range(5):
                    plane_ref[face, c, block_rows(block, nb, count), :] = recv_ref[
                        target, first + c
                    ]

            if valid_row is None:
                move()
            else:
                pl.when(tab_ref[valid_row, item] > 0)(move)


def pack_wide(tab_ref, slots, plane_ref, send_ref, over_ref, nb):
    for face in range(6):
        for block in range(nb):
            item = face * nb + block
            slot = tab_ref[1, item]

            def move(ref, first, face=face, block=block):
                for c in range(5):
                    ref[first + c] = plane_ref[face, c, block_rows(block, nb, 4), :]

            target_ref = send_ref.at[tab_ref[0, item]]
            if over_ref is None:
                move(target_ref, slot * 5)
            else:
                pl.when(slot < slots)(functools.partial(move, target_ref, slot * 5))
                pl.when(slot >= slots)(functools.partial(move, over_ref, (slot - slots) * 5))


def unpack_wide(tab_ref, slots, recv_ref, over_ref, plane_ref, nb):
    for face in range(6):
        for block in range(nb):
            item = face * nb + block
            slot = tab_ref[2, item]

            def move(ref, first, face=face, block=block):
                for c in range(5):
                    plane_ref[face, c, block_rows(block, nb, 4), :] = ref[first + c]

            source_ref = recv_ref.at[tab_ref[0, item]]
            if over_ref is None:
                move(source_ref, slot * 5)
            else:
                pl.when(slot < slots)(functools.partial(move, source_ref, slot * 5))
                pl.when(slot >= slots)(functools.partial(move, over_ref, (slot - slots) * 5))


def take_rims(tab_ref, slot_row, recv_ref, rim_ref, parents_here, nb):
    for face in range(6):
        for p in range(parents_here):
            item = face * nb + tab_ref[9, p]
            target = tab_ref[0, item]
            first = tab_ref[slot_row, item] * 5
            for c in range(5):
                rim_ref[face, c, 2 * p : 2 * p + 2, :] = recv_ref[target, first + c, 0:2, :]


def interior(nb, edge, u_ref, d_ref):
    square = edge * edge

    def sweep(u, axis, index, size, step, dim):
        n = 1 + axis
        below = [x - pltpu.roll(x, step, dim) for x in u]
        above = [pltpu.roll(x, size - step, dim) for x in below]
        low, high = evolve(u, below, above, n)
        prev = [pltpu.roll(x, step, dim) for x in high]
        inside = (index >= 2) & (index <= edge - 2)
        flux = [jnp.where(inside, x, 0.0) for x in hllc(prev, low, n)]
        return [pltpu.roll(x, size - step, dim) - x for x in flux]

    def body(b, carry):
        for rt in range(edge // ROWS):
            rows = slice(rt * ROWS, (rt + 1) * ROWS)
            u = [u_ref[b, c, rows, :] for c in range(5)]
            div = sweep(u, 1, iota((ROWS, square), 1) // edge, square, edge, 1)
            for c in range(5):
                d_ref[b, c, rows, :] = u[c] - STEP_RATIO * div[c]
        for half in range(square // LANES):
            lanes = slice(half * LANES, (half + 1) * LANES)
            u = [u_ref[b, c, :, lanes] for c in range(5)]
            div = sweep(u, 0, iota((edge, LANES), 0), edge, 1, 0)
            more = sweep(u, 2, iota((edge, LANES), 1) % edge, LANES, 1, 1)
            for c in range(5):
                d_ref[b, c, :, lanes] = d_ref[b, c, :, lanes] - STEP_RATIO * (div[c] + more[c])
        return carry

    lax.fori_loop(0, nb, body, 0)


def face_fluxes(plane_ref, ghost_ref, add_ref, face_ref, nb):
    for face in range(6):
        axis = face // 2
        side = face % 2
        n = 1 + axis
        sign = 1.0 - 2.0 * side

        def body(half, carry):
            def rows(layer):
                return pl.ds(pl.multiple_of((layer * 2 + half) * nb, ROWS), nb)

            def load(ref, layer):
                return [ref[face, c, rows(layer), :] for c in range(5)]

            near, mid, deep = (load(plane_ref, layer) for layer in range(3))
            ghost, far = (load(ghost_ref, layer) for layer in range(2))

            def steps(a, b):
                return [sign * (y - x) for x, y in zip(a, b)]

            d0, d1, d2, d3 = steps(far, ghost), steps(ghost, near), steps(near, mid), steps(mid, deep)
            if side == 0:
                first = hllc(evolve(ghost, d0, d1, n)[1], evolve(near, d1, d2, n)[0], n)
                second = hllc(evolve(near, d1, d2, n)[1], evolve(mid, d2, d3, n)[0], n)
            else:
                first = hllc(evolve(near, d1, d2, n)[1], evolve(ghost, d0, d1, n)[0], n)
                second = hllc(evolve(mid, d2, d3, n)[1], evolve(near, d1, d2, n)[0], n)
            for c in range(5):
                face_ref[face, c, rows(0), :] = first[c]
                add_ref[face, c, rows(0), :] = (sign * STEP_RATIO) * (first[c] - second[c])
                add_ref[face, c, rows(1), :] = (sign * STEP_RATIO) * second[c]
            return carry

        lax.fori_loop(0, 2, body, 0)


def inner_kernel(nb, edge, u_ref, d_ref, plane_ref):
    extract(u_ref, plane_ref, 3, nb, edge)
    interior(nb, edge, u_ref, d_ref)


def coarse_inner_kernel(nb, edge, u_ref, d_ref, plane_ref, near_ref):
    inner_kernel(nb, edge, u_ref, d_ref, plane_ref)
    extract(d_ref, near_ref, 1, nb, edge)


def send_kernel(nb, edge, slots, tab_ref, u_ref, send_ref, *refs):
    *over_ref, plane_ref = refs
    extract(u_ref, plane_ref, 2, nb, edge)
    pack_wide(tab_ref, slots, plane_ref, send_ref, over_ref[0] if over_ref else None, nb)


def near_layers(near_ref, add_ref, new_ref, nb, edge):
    lane = lane_of()
    group = lane // edge
    sub = lane % edge
    views = ((1, 2), (0, 2), (0, 1))

    def rows_at(layer, half, rt):
        at = (layer * 2 + half) * nb + rt * ROWS
        return slice(at, at + ROWS)

    def body(c, carry):
        for face in range(6):
            axis = face // 2
            depth = 0 if face % 2 == 0 else edge - 1
            for half in range(2):
                tiles = []
                for rt in range(nb // ROWS):
                    at = rows_at(0, half, rt)
                    tiles.append(near_ref[face, c, at, :] + add_ref[face, c, at, :])
                for other in range(6):
                    lateral = other // 2
                    if lateral == axis:
                        continue
                    first = views[axis][0] == lateral
                    along = sub if first else group + half * ROWS
                    for layer in range(2):
                        place = layer if other % 2 == 0 else edge - 1 - layer
                        if first:
                            if place // ROWS != half:
                                continue
                            hit = group == place % ROWS
                        else:
                            hit = sub == place
                        for rt in range(nb // ROWS):
                            if views[lateral][0] == axis:
                                index = edge * (depth % ROWS) + along
                                value = take_lanes(
                                    add_ref[other, c, rows_at(layer, depth // ROWS, rt), :], index
                                )
                            elif first:
                                index = edge * (along % ROWS) + depth
                                value = jnp.where(
                                    along < ROWS,
                                    take_lanes(add_ref[other, c, rows_at(layer, 0, rt), :], index),
                                    take_lanes(add_ref[other, c, rows_at(layer, 1, rt), :], index),
                                )
                            else:
                                index = edge * group + depth
                                value = take_lanes(
                                    add_ref[other, c, rows_at(layer, half, rt), :], index
                                )
                            tiles[rt] = tiles[rt] + jnp.where(hit, value, 0.0)
                for rt in range(nb // ROWS):
                    new_ref[face, c, rows_at(0, half, rt), :] = tiles[rt]
        return carry

    lax.fori_loop(0, 5, body, 0)


def coarse_kernel(nb, edge, parents_here, slots, tab_ref, plane_ref, near_ref, recv_ref, *refs):
    *over_ref, add_ref, face_ref, send_ref, rim_ref, ghost_ref, new_ref = refs
    unpack_wide(tab_ref, slots, recv_ref, over_ref[0] if over_ref else None, ghost_ref, nb)
    for face in range(6):
        for p in range(parents_here):
            block = tab_ref[9, p]
            for c in range(5):
                rim_ref[face, c, 2 * p : 2 * p + 2, :] = ghost_ref[
                    face, c, block_rows(block, nb, 2), :
                ]
    face_fluxes(plane_ref, ghost_ref, add_ref, face_ref, nb)
    near_layers(near_ref, add_ref, new_ref, nb, edge)
    pack(tab_ref, 3, 5, new_ref, send_ref, 2, nb)


def coarse_cells_kernel(nb, edge, d_ref, add_ref, new_ref, temp_ref):
    temp_ref[...] = add_ref[...]
    expand_add(d_ref, temp_ref, new_ref, 2, nb, edge)


def rims_kernel(nb, parents_here, tab_ref, recv_ref, rim_ref):
    take_rims(tab_ref, 6, recv_ref, rim_ref, parents_here, nb)


def fine_ghosts(nb, edge, tab_ref, bits_ref, plane_ref, rim_ref, rim2_ref, ghost_ref, parents_here):
    lane = lane_of()
    for face in range(6):
        axis = face // 2
        side = face % 2
        opposite = face + 1 - 2 * side
        for block in range(nb):
            sibling = tab_ref[12 + axis, block]
            for c in range(5):
                ghost_ref[face, c, block_rows(block, nb, 4), :] = plane_ref[
                    opposite, c, block_rows(sibling, nb, 4), :
                ]
        for rt in range(nb // ROWS):
            octant = bits_ref[rt * ROWS : (rt + 1) * ROWS, :]
            slot = bits_ref[nb + rt * ROWS : nb + (rt + 1) * ROWS, :]
            outward = (octant // BIT_OF[axis]) % 2 == side
            first = (octant // TANGENT[axis][0]) % 2
            second = (octant // TANGENT[axis][1]) % 2
            which = 2 * slot + first
            for c in range(5):
                rims = rim_ref[face, c]
                if rim2_ref is not None:
                    rims = 0.5 * (rims + rim2_ref[face, c])
                source = jnp.broadcast_to(rims[0:1, :], (ROWS, LANES))
                for k in range(1, 2 * parents_here):
                    source = jnp.where(which == k, rims[k : k + 1, :], source)
                for half in range(2):
                    index = (
                        edge * ((edge // 4) * half + lane // edge // 2)
                        + (edge // 2) * second
                        + lane % edge // 2
                    )
                    outer = take_lanes(source, index)
                    for layer in range(2):
                        at = (layer * 2 + half) * nb + rt * ROWS
                        at = slice(at, at + ROWS)
                        ghost_ref[face, c, at, :] = jnp.where(
                            outward, outer, ghost_ref[face, c, at, :]
                        )


def fine_kernel(
    nb, edge, parents_here, tab_ref, bits_ref, d_ref, plane_ref, rim_ref, new_ref, face_ref,
    ghost_ref, add_ref, base_ref, sem,
):
    fetch = pltpu.make_async_copy(d_ref, base_ref, sem)
    fetch.start()
    fine_ghosts(nb, edge, tab_ref, bits_ref, plane_ref, rim_ref, None, ghost_ref, parents_here)
    face_fluxes(plane_ref, ghost_ref, add_ref, face_ref, nb)
    fetch.wait()
    expand_add(base_ref, add_ref, new_ref, 2, nb, edge)


def face_means(nb, edge, parents_here, tab_ref, one_ref, two_ref, mean_ref, quarter_ref):
    lane = lane_of()
    group = lane // edge
    sub = lane % edge
    index = edge * (2 * (group % (ROWS // 2))) + 2 * (sub % (edge // 2))
    for face in range(6):
        places = [
            (c, slice(half * nb + rt * ROWS, half * nb + (rt + 1) * ROWS))
            for c in range(5)
            for rt in range(nb // ROWS)
            for half in range(2)
        ]
        tiles = [one_ref[face, c, at, :] + two_ref[face, c, at, :] for c, at in places]
        tiles = [v + pltpu.roll(v, LANES - 1, 1) for v in tiles]
        tiles = [v + pltpu.roll(v, LANES - edge, 1) for v in tiles]
        tiles = [0.125 * take_lanes(v, index) for v in tiles]
        for k in range(0, len(tiles), 2):
            at = k // 2 * ROWS
            quarter_ref[face, at : at + ROWS, :] = jnp.where(
                group < ROWS // 2, tiles[k], tiles[k + 1]
            )
    left = iota((5, LANES), 1) % edge < edge // 2
    for face in range(6):
        axis = face // 2
        for p in range(parents_here):
            for half in range(2):
                octant = (face % 2) * BIT_OF[axis] + half * TANGENT[axis][0]
                one = tab_ref[15 + p, octant]
                two = tab_ref[15 + p, octant + TANGENT[axis][1]]
                value = jnp.where(
                    left,
                    quarter_ref[face, pl.ds(one, 5, stride=nb), :],
                    quarter_ref[face, pl.ds(two, 5, stride=nb), :],
                )
                for c in range(5):
                    mean_ref[face, c, 2 * p + half : 2 * p + half + 1, :] = value[c : c + 1, :]


def means_kernel(
    nb, edge, parents_here, tab_ref, bits_ref, plane_ref, rim_ref, rim2_ref, one_ref, send_ref,
    add_ref, ghost_ref, face_ref, quarter_ref, mean_ref,
):
    fine_ghosts(nb, edge, tab_ref, bits_ref, plane_ref, rim_ref, rim2_ref, ghost_ref, parents_here)
    face_fluxes(plane_ref, ghost_ref, add_ref, face_ref, nb)
    face_means(nb, edge, parents_here, tab_ref, one_ref, face_ref, mean_ref, quarter_ref)
    for face in range(6):
        for p in range(parents_here):
            item = face * nb + tab_ref[9, p]
            target = tab_ref[0, item]
            first = tab_ref[7, item] * 5
            for c in range(5):
                send_ref[target, first + c] = mean_ref[face, c, 2 * p : 2 * p + 2, :]


def finish_kernel(
    nb, edge, parents_here, tab_ref, d_ref, add_ref, new_ref, average_ref, temp_ref, split_ref,
    eighth_ref,
):
    temp_ref[...] = add_ref[...]
    expand_add(d_ref, temp_ref, new_ref, 2, nb, edge, split_ref)
    averages(nb, edge, parents_here, tab_ref, split_ref, average_ref, eighth_ref)


def averages(nb, edge, parents_here, tab_ref, split_ref, out_ref, eighth_ref):
    lane = lane_of()
    group = lane // edge
    index = edge * (2 * (group % (ROWS // 2))) + 2 * (lane % (edge // 2))
    for b in range(nb):
        tiles = [
            split_ref[b, c, h, pl.ds(0, ROWS, stride=2), :]
            + split_ref[b, c, h, pl.ds(1, ROWS, stride=2), :]
            for c in range(5)
            for h in range(2)
        ]
        tiles = [v + pltpu.roll(v, LANES - 1, 1) for v in tiles]
        tiles = [v + pltpu.roll(v, LANES - edge, 1) for v in tiles]
        tiles = [0.125 * take_lanes(v, index) for v in tiles]
        for c in range(5):
            eighth_ref[b, c] = jnp.where(group < ROWS // 2, tiles[2 * c], tiles[2 * c + 1])
    left = lane % edge < edge // 2
    for p in range(parents_here):
        for corner in range(4):
            one = tab_ref[15 + p, 2 * corner]
            two = tab_ref[15 + p, 2 * corner + 1]
            rows = slice(corner // 2 * ROWS, (corner // 2 + 1) * ROWS)
            lanes = slice(corner % 2 * LANES, (corner % 2 + 1) * LANES)
            for c in range(5):
                out_ref[p, c, rows, lanes] = jnp.where(left, eighth_ref[one, c], eighth_ref[two, c])


def correct_kernel(
    nb, edge, parents_here, tab_ref, bits_ref, new_ref, face_ref, recv_ref, cells_ref, out_ref,
    mean_ref, add_ref, base_ref, sem,
):
    fetch = pltpu.make_async_copy(new_ref, base_ref, sem)
    fetch.start()
    unpack(tab_ref, 3, 8, recv_ref, mean_ref, 2, nb)
    beside = bits_ref[2 * nb : 3 * nb, :]
    for face in range(6):
        sign = STEP_RATIO if face % 2 else -STEP_RATIO
        hit = (beside // (1 << face)) % 2 > 0
        for c in range(5):
            for half in range(2):
                at = slice(half * nb, (half + 1) * nb)
                add_ref[face, c, at, :] = jnp.where(
                    hit, sign * (face_ref[face, c, at, :] - mean_ref[face, c, at, :]), 0.0
                )
    fetch.wait()
    for p in range(parents_here):
        base_ref[tab_ref[9, p]] = cells_ref[p]
    expand_add(base_ref, add_ref, out_ref, 1, nb, edge)


def column(row):
    return jnp.transpose(jnp.broadcast_to(row.astype(F32), (LANES, LANES)))


def count(hits):
    return jnp.sum(jnp.where(hits, 1.0, 0.0), axis=0, keepdims=True).astype(I32)


def tables_kernel(
    nb, devices, parents_here, blk_ref, all_near_ref, all_parent_ref, tab_ref, bits_ref, near_ref,
    parent_ref, sems,
):
    fetches = [
        pltpu.make_async_copy(all_near_ref, near_ref, sems.at[0]),
        pltpu.make_async_copy(all_parent_ref, parent_ref, sems.at[1]),
    ]
    for fetch in fetches:
        fetch.start()
    for fetch in fetches:
        fetch.wait()
    total = near_ref.shape[1]
    tiles = total // LANES
    start = blk_ref[0] * nb
    tile = pl.ds(pl.multiple_of(start // LANES * LANES, LANES), LANES)
    turn = (LANES - start % LANES) % LANES
    own = pltpu.roll(near_ref[:, tile], turn, 1)
    own_parent = pltpu.roll(parent_ref[:, tile], turn, 1)
    lane = iota((1, LANES), 1)
    face = lane // nb
    block = lane % nb
    row = iota((LANES, LANES), 0)
    near = jnp.zeros((1, LANES), I32)
    for f in range(6):
        near = jnp.where(face == f, pltpu.roll(own[f : f + 1, :], nb * f, 1), near)
    target = near // nb
    wanted = (face + 1 - 2 * (face % 2)) * nb + near % nb
    wanted_f = wanted.astype(F32)
    parent_columns = [
        column(parent_ref[0:1, k * LANES : (k + 1) * LANES]) for k in range(tiles)
    ]

    def any_parent(ids):
        ids = ids.astype(F32)
        hits = [jnp.max(jnp.where(x == ids, 1.0, 0.0), axis=0, keepdims=True) for x in parent_columns]
        return functools.reduce(jnp.maximum, hits)

    beside = any_parent(near)
    parent = own_parent[0:1, :] - start
    octant = own_parent[1:2, :]
    parent_column = column(parent)
    octant_column = column(octant)
    mine = row < nb
    owned = jnp.max(
        jnp.where(mine & (parent_column == block.astype(F32)), 1.0, 0.0), axis=0, keepdims=True
    )
    same = (column(target) == target.astype(F32)) & (row < 6 * nb)
    by_own = same & (row < lane)
    by_wanted = same & (column(wanted) < wanted_f)
    beside_column = column(beside) > 0.0
    owned_column = column(owned) > 0.0
    parent_f = parent.astype(F32)
    slot = count(mine & (parent_column < parent_f)) // 8
    slot_column = column(slot)
    row_f = row.astype(F32)
    lane_f = lane.astype(F32)

    def pick(hits, values):
        return jnp.sum(jnp.where(mine & hits, values, 0.0), axis=0, keepdims=True).astype(I32)

    rows = [
        target,
        count(by_own),
        count(by_wanted),
        beside.astype(I32),
        owned.astype(I32),
        count(by_own & beside_column),
        count(by_wanted & owned_column),
        count(by_own & owned_column),
        count(by_wanted & beside_column),
        pick((octant_column == 0.0) & (slot_column == lane_f), parent_column),
        octant,
        slot,
    ]
    for bit in BIT_OF:
        partner = (octant + bit - 2 * bit * (octant // bit % 2)).astype(F32)
        rows.append(pick((parent_column == parent_f) & (octant_column == partner), row_f))
    for p in range(parents_here):
        rows.append(pick((slot_column == p) & (octant_column == lane_f), row_f))

    most = jnp.zeros((devices, LANES), F32)
    most_all = jnp.zeros((devices, LANES), F32)
    device = iota((devices, LANES), 0)
    lanes_2d = iota((devices, LANES), 1)
    for k in range(tiles):
        lanes = slice(k * LANES, (k + 1) * LANES)
        hits = jnp.zeros((devices, LANES), F32)
        for f in range(6):
            hits = hits + jnp.where(near_ref[f : f + 1, lanes] // nb == device, 1.0, 0.0)
        sums = [hits * any_parent(k * LANES + lane), hits]
        width = 1
        while width < nb:
            sums = [x + pltpu.roll(x, LANES - width, 1) for x in sums]
            width *= 2
        start_lane = lanes_2d % nb == 0
        opposite = (k * LANES + lanes_2d) // nb + devices // 2
        opposite = jnp.where(opposite >= devices, opposite - devices, opposite) == device
        most = jnp.maximum(most, jnp.where(start_lane, sums[0], 0.0))
        most_all = jnp.maximum(most_all, jnp.where(start_lane & ~opposite, sums[1], 0.0))
    for values in (most, most_all):
        values = jnp.max(jnp.max(values, axis=0, keepdims=True), axis=1, keepdims=True)
        rows.append(jnp.broadcast_to(values, (1, LANES)).astype(I32))
    for k, values in enumerate(rows):
        tab_ref[k : k + 1, :] = values

    beside_bits = jnp.zeros((1, LANES), F32)
    for f in range(6):
        part = jnp.where(face == f, beside * (1 << f), 0.0)
        beside_bits = beside_bits + pltpu.roll(part, (LANES - nb * f) % LANES, 1)
    for k, values in enumerate((octant_column, slot_column, column(beside_bits))):
        bits_ref[k * nb : (k + 1) * nb, :] = values[0:nb, :].astype(I32)


def run(kernel, outs, operands, scratch=(), scalars=0, far=None, flops=0):
    held = [o.shape for o in operands] + list(outs) + list(scratch)
    limit = sum(4 * max(math.prod(s), 8 * LANES) for s in held) + SPARE
    smem = pl.BlockSpec(memory_space=pltpu.SMEM)
    vmem = pl.BlockSpec(memory_space=pltpu.VMEM)
    specs = [smem if k < scalars else vmem for k in range(len(operands))]
    scratches = [pltpu.VMEM(s, F32) for s in scratch]
    if far is not None:
        specs[far] = pl.BlockSpec(memory_space=pltpu.HBM)
        scratches.append(pltpu.SemaphoreType.DMA)
    return pl.pallas_call(
        kernel,
        out_shape=[jax.ShapeDtypeStruct(s, F32) for s in outs],
        in_specs=specs,
        out_specs=[vmem] * len(outs),
        scratch_shapes=scratches,
        compiler_params=pltpu.CompilerParams(vmem_limit_bytes=limit),
        cost_estimate=pl.CostEstimate(
            flops=flops, bytes_accessed=4 * sum(o.size for o in operands), transcendentals=0
        ),
    )(*operands)


def blank(*shapes):
    return pl.pallas_call(
        lambda *refs: None,
        out_shape=[jax.ShapeDtypeStruct(s, F32) for s in shapes],
        out_specs=[pl.BlockSpec(memory_space=pl.ANY)] * len(shapes),
    )()


def level_shift(array, source):
    return lax.ppermute(array, "level", [(source, 1 - source)])


def route(buffer):
    return lax.all_to_all(buffer, "blk", split_axis=0, concat_axis=0, tiled=True)


def local(fluid_state, neighbours, parents):
    blk_index = lax.axis_index("blk")
    devices = lax.axis_size("blk")
    u = fluid_state[0]
    nb, _, edge, _ = u.shape
    parents_here = nb // 8
    capacity = 2 * ((6 * nb + devices - 1) // devices)
    smem = pl.BlockSpec(memory_space=pltpu.SMEM)
    vmem = pl.BlockSpec(memory_space=pltpu.VMEM)
    hbm = pl.BlockSpec(memory_space=pltpu.HBM)
    table, bits = pl.pallas_call(
        functools.partial(tables_kernel, nb, devices, parents_here),
        out_shape=[
            jax.ShapeDtypeStruct((17 + parents_here, LANES), I32),
            jax.ShapeDtypeStruct((3 * nb, LANES), I32),
        ],
        in_specs=[smem, hbm, hbm],
        out_specs=[vmem, vmem],
        scratch_shapes=[
            pltpu.VMEM(neighbours.shape[::-1], I32),
            pltpu.VMEM(parents.shape[::-1], I32),
            pltpu.SemaphoreType.DMA((2,)),
        ],
        compiler_params=pltpu.CompilerParams(vmem_limit_bytes=2 * SPARE),
    )(jnp.reshape(blk_index, (1,)).astype(I32), neighbours.T, parents.T)

    few = max(1, capacity // 3)
    half = max(1, capacity // 2)
    counts = table[15 + parents_here : 17 + parents_here, 0]
    finished = lax.cond(
        (counts[0] <= few) & (counts[1] <= half) & (devices % 2 == 0),
        functools.partial(step, capacity, half, few),
        functools.partial(step, capacity, capacity, capacity),
        u,
        table,
        bits,
    )
    return finished[None]


def step(capacity, wide, slots, u, table, bits):
    level_id = lax.axis_index("level")
    devices = lax.axis_size("blk")
    nb, _, edge, square = u.shape
    parents_here = nb // 8
    part = functools.partial
    cell_shape = u.shape
    plane_shape = (6, 5, 6 * nb, LANES)
    ghost_shape = (6, 5, 4 * nb, LANES)
    face_shape = (6, 5, 2 * nb, LANES)
    rim_shape = (6, 5, 2 * parents_here, LANES)
    wide_send = (devices, wide * 5, 4, LANES)
    over_send = [((capacity - wide) * 5, 4, LANES)] if wide < capacity else []
    thin_send = (devices, slots * 5, 2, LANES)
    average_shape = (parents_here,) + cell_shape[1:]
    work = 220 * 3 * 5 * nb * edge * square

    def inner(cells):
        return run(part(inner_kernel, nb, edge), [cell_shape, plane_shape], [cells], flops=work)

    def half_way_round(buffer):
        turned = [(d, (d + devices // 2) % devices) for d in range(devices)]
        return lax.ppermute(buffer, ("level", "blk"), turned)

    def coarse_first(u):
        send, *over = run(
            part(send_kernel, nb, edge, wide), [wide_send] + over_send, [table, u], [ghost_shape], 1
        )
        received = [route(send)] + [half_way_round(buffer) for buffer in over]
        partial_new, planes, near = run(
            part(coarse_inner_kernel, nb, edge),
            [cell_shape, plane_shape, face_shape],
            [u],
            flops=work,
        )
        adds, faces, send, rims = run(
            part(coarse_kernel, nb, edge, parents_here, wide),
            [ghost_shape, face_shape, thin_send, rim_shape],
            [table, planes, near] + received,
            [ghost_shape, face_shape],
            1,
        )
        return (partial_new, adds, faces, send, rims, *blank(plane_shape))

    def fine_first(u):
        partial_new, planes = inner(u)
        return (partial_new, *blank(ghost_shape, face_shape, thin_send, rim_shape), planes)

    partial_new, adds, faces, send, rims, planes = lax.cond(
        level_id == 0, coarse_first, fine_first, u
    )
    early_rims = level_shift(rims, 0)

    def coarse_second(send, partial_new, adds, planes, early_rims):
        received = route(send)
        (cells,) = run(
            part(coarse_cells_kernel, nb, edge),
            [cell_shape],
            [partial_new, adds],
            [ghost_shape],
            flops=work // 4,
        )
        (late,) = run(part(rims_kernel, nb, parents_here), [rim_shape], [table, received], (), 1)
        return (late, cells, *blank(plane_shape, face_shape))

    def fine_second(send, partial_new, adds, planes, early_rims):
        half, faces = run(
            part(fine_kernel, nb, edge, parents_here),
            [cell_shape, face_shape],
            [table, bits, partial_new, planes, early_rims],
            [ghost_shape, ghost_shape, cell_shape],
            1,
            far=2,
        )
        return (*blank(rim_shape), *inner(half), faces)

    late, cells, half_planes, half_faces = lax.cond(
        level_id == 0, coarse_second, fine_second, send, partial_new, adds, planes, early_rims
    )
    late_rims = level_shift(late, 0)

    def coarse_third(cells, half_planes, half_faces, early_rims, late_rims):
        return tuple(blank(thin_send, cell_shape, average_shape))

    def fine_third(cells, half_planes, half_faces, early_rims, late_rims):
        send, adds = run(
            part(means_kernel, nb, edge, parents_here),
            [thin_send, ghost_shape],
            [table, bits, half_planes, early_rims, late_rims, half_faces],
            [ghost_shape, face_shape, (6, 5 * nb, LANES), rim_shape],
            1,
        )
        received = route(send)
        out, averaged = run(
            part(finish_kernel, nb, edge, parents_here),
            [cell_shape, average_shape],
            [table, cells, adds],
            [ghost_shape, (nb, 5, 2, edge, LANES), (nb, 5, ROWS, LANES)],
            1,
            flops=work,
        )
        return received, out, averaged

    returned, out, averaged = lax.cond(
        level_id == 0, coarse_third, fine_third,
        cells, half_planes, half_faces, early_rims, late_rims,
    )
    returned = level_shift(returned, 1)
    averaged = level_shift(averaged, 1)

    def correct(out, cells, faces, returned, averaged):
        return run(
            part(correct_kernel, nb, edge, parents_here),
            [cell_shape],
            [table, bits, cells, faces, returned, averaged],
            [face_shape, face_shape, cell_shape],
            1,
            far=2,
        )[0]

    return lax.cond(
        level_id == 0, correct, lambda out, *rest: out, out, cells, faces, returned, averaged
    )


def solution(mesh):
    return jax.shard_map(
        local,
        mesh=mesh,
        in_specs=(P("level", "blk", None, None, None), P(), P()),
        out_specs=P("level", "blk", None, None, None),
        check_vma=False,
    )
```

```python
import functools
import math

import jax
import jax.numpy as jnp
from jax import lax
from jax.experimental import pallas as pl
from jax.experimental.pallas import tpu as pltpu
from jax.sharding import PartitionSpec as P

GAS_GAMMA = 1.4
STEP_RATIO = 0.12
BIT_OF = (4, 2, 1)
TANGENT = ((2, 1), (4, 1), (4, 2))
F32 = jnp.float32
I32 = jnp.int32
SPARE = 8 * 1024 * 1024
LANES = 128
ROWS = 8
COUNTS = 15
OTHERS = 17
SELF = 18
CHILDREN = 19


def iota(shape, dim):
    return lax.broadcasted_iota(I32, shape, dim)


def reciprocal(x):
    return pltpu.reciprocal(x, approx=True)


def physical_flux(s, n):
    inv = reciprocal(s[0])
    vn = s[n] * inv
    kinetic = s[1] * s[1] + s[2] * s[2] + s[3] * s[3]
    p = (GAS_GAMMA - 1.0) * (s[4] - 0.5 * (kinetic * inv))
    out = [s[n], s[1] * vn, s[2] * vn, s[3] * vn, (s[4] + p) * vn]
    out[n] = out[n] + p
    return out


def evolve(u, below, above, n):
    low = []
    high = []
    for c in range(5):
        d = jnp.maximum(jnp.minimum(below[c], above[c]), 0.0) + jnp.minimum(
            jnp.maximum(below[c], above[c]), 0.0
        )
        d = 0.5 * d
        low.append(u[c] - d)
        high.append(u[c] + d)
    fl = physical_flux(low, n)
    fh = physical_flux(high, n)
    for c in range(5):
        change = (0.5 * STEP_RATIO) * (fl[c] - fh[c])
        low[c] = low[c] + change
        high[c] = high[c] + change
    return low, high


def side_values(s, n):
    inv = reciprocal(s[0])
    vn = s[n] * inv
    kinetic = s[1] * s[1] + s[2] * s[2] + s[3] * s[3]
    p = (GAS_GAMMA - 1.0) * (s[4] - 0.5 * (kinetic * inv))
    square = GAS_GAMMA * p * inv
    sound = square * lax.rsqrt(square)
    return vn, p, sound


def hllc(a, b, n):
    va, pa, ca = side_values(a, n)
    vb, pb, cb = side_values(b, n)
    slow = jnp.minimum(va - ca, vb - cb)
    fast = jnp.maximum(va + ca, vb + cb)
    qa = a[0] * (slow - va)
    qb = b[0] * (fast - vb)
    contact = (pb - pa + va * qa - vb * qb) * reciprocal(qa - qb)
    is_low = contact >= 0.0

    def pick(x, y):
        return jnp.where(is_low, x, y)

    s = [pick(a[c], b[c]) for c in range(5)]
    v = pick(va, vb)
    p = pick(pa, pb)
    q = pick(qa, qb)
    speed = pick(slow, fast)
    clipped = pick(jnp.minimum(slow, 0.0), jnp.maximum(fast, 0.0))
    extra = clipped * (contact - v) * reciprocal(speed - contact)
    h = v + extra
    push = extra * q
    out = [s[0] * h, s[1] * h, s[2] * h, s[3] * h, (s[4] + p) * h + push * contact]
    out[n] = out[n] + p + push
    return out


def lane_of():
    return iota((ROWS, LANES), 1)


def row_of():
    return iota((ROWS, LANES), 0)


def take_lanes(v, index):
    return jnp.take_along_axis(v, index, axis=1, mode="promise_in_bounds")


def slide_groups(tiles, edge):
    group = lane_of() // edge
    for bit in (1, 2, 4):
        moves = (group & bit) != 0
        tiles = [jnp.where(moves, pltpu.roll(g, bit, 0), g) for g in tiles]
    return tiles


def swap_front(tiles, edge, skews):
    base = lane_of() + edge * row_of()
    return slide_groups(
        [take_lanes(v, (base + skew) % LANES) for v, skew in zip(tiles, skews)], edge
    )


def swap_back_index(lane, edge):
    return edge * ((row_of() - lane // edge + ROWS) % ROWS) + lane % edge


def extract(u_ref, plane_ref, layers, nb, edge, eager):
    groups = LANES // edge
    for side in range(2):
        for layer in range(layers):
            x = layer if side == 0 else edge - 1 - layer
            for c in range(5):
                for half in range(2):
                    at = (layer * 2 + half) * nb
                    plane_ref[side, c, at : at + nb, :] = u_ref[
                        :, c, x, half * LANES : (half + 1) * LANES
                    ]
    lane = lane_of()
    row = row_of()
    grp = lane // edge
    sub = lane % edge
    zero = jnp.zeros((ROWS, LANES), F32)
    offsets = [o for layer in range(layers) for o in (layer, edge - 1 - layer)]

    def rows_at(layer, rt, h):
        at = (layer * 2 + rt) * nb + h * ROWS
        return slice(at, at + ROWS)

    def gather(c, carry):
        for rt in range(2):
            rows = slice(rt * ROWS, (rt + 1) * ROWS)
            ylow = [[zero, zero] for _ in range(layers)]
            yhigh = [[zero, zero] for _ in range(layers)]
            for b in range(nb):
                t = b // groups
                turn = edge * b % LANES
                low = u_ref[b, c, rows, :LANES]
                high = u_ref[b, c, rows, LANES:]
                low = pltpu.roll(low, turn, 1) if turn else low
                high = pltpu.roll(high, turn, 1) if turn else high
                for layer in range(layers):
                    ylow[layer][t] = jnp.where(grp == (b + layer) % groups, low, ylow[layer][t])
                    yhigh[layer][t] = jnp.where(
                        grp == (b + groups - 1 - layer) % groups, high, yhigh[layer][t]
                    )
            for layer in range(layers):
                for h in range(2):
                    plane_ref[2, c, rows_at(layer, rt, h), :] = ylow[layer][h]
                    plane_ref[3, c, rows_at(layer, rt, h), :] = yhigh[layer][h]
            for h in range(2):
                zacc = {o: zero for o in offsets}
                for b in range(nb):
                    r = u_ref[b, c, rows, h * LANES : (h + 1) * LANES]
                    r = pltpu.roll(r, b, 1) if b else r
                    for o in offsets:
                        zacc[o] = jnp.where(sub == (b + o) % edge, r, zacc[o])
                for layer in range(layers):
                    plane_ref[4, c, rows_at(layer, rt, h), :] = zacc[layer]
                    plane_ref[5, c, rows_at(layer, rt, h), :] = zacc[edge - 1 - layer]
        return carry

    lax.fori_loop(0, 5, gather, 0, unroll=5 if eager else 1)

    def turn(c, carry):
        last = swap_back_index(lane, edge)
        places = [
            (face, rows_at(layer, rt, h), skew)
            for layer in range(layers)
            for face, skew in ((2, edge * layer), (3, edge * (groups - 1 - layer)))
            for rt in range(2)
            for h in range(2)
        ]
        tiles = swap_front(
            [plane_ref[face, c, at, :] for face, at, _ in places], edge, [p[2] for p in places]
        )
        tiles = [take_lanes(v, last) for v in tiles]
        for (face, at, _), v in zip(places, tiles):
            plane_ref[face, c, at, :] = v
        places = []
        tiles = []
        for layer in range(layers):
            for face, o in ((4, layer), (5, edge - 1 - layer)):
                for rt in range(2):
                    raw = [plane_ref[face, c, rows_at(layer, rt, h), :] for h in range(2)]
                    for h in range(2):
                        index = (edge * (sub % ROWS) + ROWS * h + (grp + row) % ROWS + o) % LANES
                        tiles.append([take_lanes(v, index) for v in raw])
                        places.append((face, rows_at(layer, rt, h)))
        tiles = slide_groups([jnp.where(sub < ROWS, v, w) for v, w in tiles], edge)
        tiles = [take_lanes(v, last) for v in tiles]
        for (face, at), v in zip(places, tiles):
            plane_ref[face, c, at, :] = v
        return carry

    lax.fori_loop(0, 5, turn, 0, unroll=5 if eager else 1)


def expand_add(base_ref, add_ref, out_ref, layers, nb, edge, eager, split_ref=None, copies=()):
    groups = LANES // edge
    lane = lane_of()
    row = row_of()
    grp = lane // edge
    sub = lane % edge

    def rows_at(layer, rt, h):
        at = (layer * 2 + rt) * nb + h * ROWS
        return slice(at, at + ROWS)

    def turn(c, carry):
        places = [
            (face, layer, rt, skew)
            for layer in range(layers)
            for face, skew in (
                (2, edge * layer),
                (3, (LANES - edge * layer) % LANES),
                (4, layer),
                (5, edge - 1 - layer),
            )
            for rt in range(2)
        ]
        loaded = [
            add_ref[face, c, rows_at(layer, rt, h), :]
            for face, layer, rt, _ in places
            for h in range(2)
        ]
        mid = swap_front(loaded, edge, [0] * len(loaded))
        out = []
        for k, (face, layer, rt, skew) in enumerate(places):
            moved = (lane - skew + LANES) % LANES
            pair = mid[2 * k : 2 * k + 2]
            if face < 4:
                index = swap_back_index(moved, edge)
                out.append([take_lanes(v, index) for v in pair])
            else:
                block = moved % edge
                base = edge * ((row - block % ROWS + ROWS) % ROWS) + moved // edge
                parts = [[take_lanes(v, base + ROWS * h) for v in pair] for h in range(2)]
                out.append([jnp.where(block < ROWS, v, w) for v, w in parts])
        for (face, layer, rt, _), pair in zip(places, out):
            for h in range(2):
                add_ref[face, c, rows_at(layer, rt, h), :] = pair[h]
        return carry

    lax.fori_loop(0, 5, turn, 0, unroll=5 if eager else 1)

    def spread(c, carry):
        for rt in range(2):
            rows = slice(rt * ROWS, (rt + 1) * ROWS)

            def tile(face, h):
                return [add_ref[face, c, rows_at(layer, rt, h), :] for layer in range(layers)]

            ylow = [tile(2, h) for h in range(2)]
            yhigh = [tile(3, h) for h in range(2)]
            zlow = [tile(4, h) for h in range(2)]
            zhigh = [tile(5, h) for h in range(2)]
            for b in range(nb):
                t = b // groups
                place = b % groups
                low = ylow[t][0]
                high = yhigh[t][0]
                if layers > 1:
                    low = jnp.where(grp == place, low, ylow[t][1])
                    high = jnp.where(grp == place, high, yhigh[t][1])
                low = pltpu.roll(low, (LANES - edge * place) % LANES, 1)
                high = pltpu.roll(high, edge * (groups - 1 - place) % LANES, 1)
                parts = [
                    jnp.where(grp < layers, low, 0.0),
                    jnp.where(grp >= groups - layers, high, 0.0),
                ]
                for h in range(2):
                    lanes = slice(h * LANES, (h + 1) * LANES)
                    z = zhigh[h][0]
                    if layers > 1:
                        z = jnp.where(sub == (b + edge - 1) % edge, z, zhigh[h][1])
                        z = jnp.where(sub == (b + 1) % edge, zlow[h][1], z)
                    z = jnp.where(sub == b, zlow[h][0], z)
                    if b:
                        z = pltpu.roll(z, LANES - b, 1)
                    total = parts[h] + jnp.where((sub < layers) | (sub >= edge - layers), z, 0.0)
                    x = add_ref[rt, c, h * nb + b : h * nb + b + 1, :]
                    x = jnp.where(row == (ROWS - 1) * rt, x, 0.0)
                    if layers > 1:
                        deeper = add_ref[rt, c, (2 + h) * nb + b : (2 + h) * nb + b + 1, :]
                        x = jnp.where(row == 1 + (ROWS - 3) * rt, deeper, x)
                    value = base_ref[b, c, rows, lanes] + (total + x)
                    out_ref[b, c, rows, lanes] = value
                    if split_ref is not None:
                        split_ref[b, c, h, rows, :] = value
        return carry

    if eager:
        for c in range(5):
            spread(c, 0)
            for copy in copies[c : c + 1]:
                copy.start()
    else:
        lax.fori_loop(0, 5, spread, 0)
        for copy in copies:
            copy.start()


def block_rows(block, nb, count):
    return pl.ds(block, count, stride=nb)


def pack(tab_ref, valid_row, slot_row, slots, plane_ref, send_ref, count, nb):
    for face in range(6):
        for block in range(nb):
            item = face * nb + block
            valid = tab_ref[valid_row, item] > 0
            target = jnp.where(valid, tab_ref[0, item], tab_ref[SELF, 0])
            first = jnp.where(valid, tab_ref[slot_row, item] * 5, 0)
            for c in range(5):
                send_ref[target, first + c] = plane_ref[face, c, block_rows(block, nb, count), :]


def unpack(tab_ref, slot_row, slots, recv_ref, plane_ref, count, nb):
    for face in range(6):
        for block in range(nb):
            item = face * nb + block
            target = tab_ref[0, item]
            first = jnp.minimum(tab_ref[slot_row, item], slots - 1) * 5
            for c in range(5):
                plane_ref[face, c, block_rows(block, nb, count), :] = recv_ref[target, first + c]


def pack_wide(tab_ref, slots, devices, plane_ref, all_ref, nb):
    for face in range(6):
        for block in range(nb):
            item = face * nb + block
            slot = tab_ref[1, item]
            first = jnp.where(
                slot < slots, tab_ref[0, item] * slots + slot, (devices - 1) * slots + slot
            )
            for c in range(5):
                all_ref[first * 5 + c] = plane_ref[face, c, block_rows(block, nb, 4), :]


def unpack_wide(tab_ref, slots, recv_ref, over_ref, plane_ref, nb):
    for face in range(6):
        for block in range(nb):
            item = face * nb + block
            target = tab_ref[0, item]
            slot = tab_ref[2, item]
            first = jnp.minimum(slot, slots - 1) * 5
            beyond = jnp.maximum(slot - slots, 0) * 5
            for c in range(5):
                value = recv_ref[target, first + c]
                if over_ref is not None:
                    value = jnp.where(slot < slots, value, over_ref[beyond + c])
                plane_ref[face, c, block_rows(block, nb, 4), :] = value


def take_rims(tab_ref, slot_row, recv_ref, rim_ref, parents_here, nb):
    for face in range(6):
        for p in range(parents_here):
            item = face * nb + tab_ref[9, p]
            target = tab_ref[0, item]
            first = tab_ref[slot_row, item] * 5
            for c in range(5):
                rim_ref[face, c, 2 * p : 2 * p + 2, :] = recv_ref[target, first + c, 0:2, :]


def interior(nb, edge, eager, u_ref, d_ref, tab_ref=None):
    square = edge * edge

    def sweep(u, axis, index, size, step, dim):
        n = 1 + axis
        below = [x - pltpu.roll(x, step, dim) for x in u]
        above = [pltpu.roll(x, size - step, dim) for x in below]
        low, high = evolve(u, below, above, n)
        prev = [pltpu.roll(x, step, dim) for x in high]
        inside = (index >= 2) & (index <= edge - 2)
        flux = [jnp.where(inside, x, 0.0) for x in hllc(prev, low, n)]
        return [pltpu.roll(x, size - step, dim) - x for x in flux]

    def work(b):
        for rt in range(edge // ROWS):
            rows = slice(rt * ROWS, (rt + 1) * ROWS)
            u = [u_ref[b, c, rows, :] for c in range(5)]
            div = sweep(u, 1, iota((ROWS, square), 1) // edge, square, edge, 1)
            for c in range(5):
                d_ref[b, c, rows, :] = u[c] - STEP_RATIO * div[c]
        for half in range(square // LANES):
            lanes = slice(half * LANES, (half + 1) * LANES)
            u = [u_ref[b, c, :, lanes] for c in range(5)]
            div = sweep(u, 0, iota((edge, LANES), 0), edge, 1, 0)
            more = sweep(u, 2, iota((edge, LANES), 1) % edge, LANES, 1, 1)
            for c in range(5):
                d_ref[b, c, :, lanes] = d_ref[b, c, :, lanes] - STEP_RATIO * (div[c] + more[c])

    def body(k, carry):
        work(k if tab_ref is None else tab_ref[OTHERS, k])
        return carry

    lax.fori_loop(0, nb if tab_ref is None else nb - nb // 8, body, 0, unroll=2 if eager else 1)


def face_fluxes(plane_ref, ghost_ref, add_ref, face_ref, nb, eager):
    for face in range(6):
        axis = face // 2
        side = face % 2
        n = 1 + axis
        sign = 1.0 - 2.0 * side

        def body(half, carry):
            def rows(layer):
                return pl.ds(pl.multiple_of((layer * 2 + half) * nb, ROWS), nb)

            def load(ref, layer):
                return [ref[face, c, rows(layer), :] for c in range(5)]

            near, mid, deep = (load(plane_ref, layer) for layer in range(3))
            ghost, far = (load(ghost_ref, layer) for layer in range(2))

            def steps(a, b):
                return [sign * (y - x) for x, y in zip(a, b)]

            d0, d1, d2, d3 = steps(far, ghost), steps(ghost, near), steps(near, mid), steps(mid, deep)
            if side == 0:
                first = hllc(evolve(ghost, d0, d1, n)[1], evolve(near, d1, d2, n)[0], n)
                second = hllc(evolve(near, d1, d2, n)[1], evolve(mid, d2, d3, n)[0], n)
            else:
                first = hllc(evolve(near, d1, d2, n)[1], evolve(ghost, d0, d1, n)[0], n)
                second = hllc(evolve(mid, d2, d3, n)[1], evolve(near, d1, d2, n)[0], n)
            for c in range(5):
                face_ref[face, c, rows(0), :] = first[c]
                add_ref[face, c, rows(0), :] = (sign * STEP_RATIO) * (first[c] - second[c])
                add_ref[face, c, rows(1), :] = (sign * STEP_RATIO) * second[c]
            return carry

        lax.fori_loop(0, 2, body, 0, unroll=2 if eager else 1)


def inner_kernel(nb, edge, eager, u_ref, d_ref, plane_ref):
    extract(u_ref, plane_ref, 3, nb, edge, eager)
    interior(nb, edge, eager, u_ref, d_ref)


def coarse_inner_kernel(nb, edge, eager, tab_ref, u_ref, d_ref, near_ref):
    interior(nb, edge, eager, u_ref, d_ref, tab_ref)
    extract(d_ref, near_ref, 1, nb, edge, eager)


def send_kernel(nb, edge, eager, slots, devices, tab_ref, u_ref, plane_ref, *refs):
    *out_refs, all_ref, sems = refs
    extract(u_ref, plane_ref, 3, nb, edge, eager)
    pack_wide(tab_ref, slots, devices, plane_ref, all_ref, nb)
    start = 0
    copies = []
    for k, out_ref in enumerate(out_refs):
        count = out_ref.shape[0]
        copies.append(
            pltpu.make_async_copy(all_ref.at[start : start + count], out_ref, sems.at[k])
        )
        copies[-1].start()
        start += count
    for copy in copies:
        copy.wait()


def near_layers(near_ref, add_ref, new_ref, nb, edge):
    lane = lane_of()
    group = lane // edge
    sub = lane % edge
    views = ((1, 2), (0, 2), (0, 1))

    def rows_at(layer, half, rt):
        at = (layer * 2 + half) * nb + rt * ROWS
        return slice(at, at + ROWS)

    def body(c, carry):
        for face in range(6):
            axis = face // 2
            depth = 0 if face % 2 == 0 else edge - 1
            for half in range(2):
                tiles = []
                for rt in range(nb // ROWS):
                    at = rows_at(0, half, rt)
                    tiles.append(near_ref[face, c, at, :] + add_ref[face, c, at, :])
                for other in range(6):
                    lateral = other // 2
                    if lateral == axis:
                        continue
                    first = views[axis][0] == lateral
                    along = sub if first else group + half * ROWS
                    for layer in range(2):
                        place = layer if other % 2 == 0 else edge - 1 - layer
                        if first:
                            if place // ROWS != half:
                                continue
                            hit = group == place % ROWS
                        else:
                            hit = sub == place
                        for rt in range(nb // ROWS):
                            if views[lateral][0] == axis:
                                index = edge * (depth % ROWS) + along
                                value = take_lanes(
                                    add_ref[other, c, rows_at(layer, depth // ROWS, rt), :], index
                                )
                            elif first:
                                index = edge * (along % ROWS) + depth
                                value = jnp.where(
                                    along < ROWS,
                                    take_lanes(add_ref[other, c, rows_at(layer, 0, rt), :], index),
                                    take_lanes(add_ref[other, c, rows_at(layer, 1, rt), :], index),
                                )
                            else:
                                index = edge * group + depth
                                value = take_lanes(
                                    add_ref[other, c, rows_at(layer, half, rt), :], index
                                )
                            tiles[rt] = tiles[rt] + jnp.where(hit, value, 0.0)
                for rt in range(nb // ROWS):
                    new_ref[face, c, rows_at(0, half, rt), :] = tiles[rt]
        return carry

    lax.fori_loop(0, 5, body, 0)


def coarse_kernel(
    nb, edge, eager, parents_here, slots, thin, tab_ref, plane_ref, near_ref, recv_ref, *refs
):
    *over_ref, add_ref, face_ref, send_ref, rim_ref, ghost_ref, new_ref = refs
    unpack_wide(tab_ref, slots, recv_ref, over_ref[0] if over_ref else None, ghost_ref, nb)
    for face in range(6):
        for p in range(parents_here):
            block = tab_ref[9, p]
            for c in range(5):
                rim_ref[face, c, 2 * p : 2 * p + 2, :] = ghost_ref[
                    face, c, block_rows(block, nb, 2), :
                ]
    face_fluxes(plane_ref, ghost_ref, add_ref, face_ref, nb, eager)
    near_layers(near_ref, add_ref, new_ref, nb, edge)
    pack(tab_ref, 3, 5, thin, new_ref, send_ref, 2, nb)


def coarse_cells_kernel(nb, edge, eager, d_ref, add_ref, new_ref, temp_ref):
    temp_ref[...] = add_ref[...]
    expand_add(d_ref, temp_ref, new_ref, 2, nb, edge, eager)


def rims_kernel(nb, parents_here, tab_ref, recv_ref, rim_ref):
    take_rims(tab_ref, 6, recv_ref, rim_ref, parents_here, nb)


def fine_ghosts(nb, edge, tab_ref, bits_ref, plane_ref, rim_ref, rim2_ref, ghost_ref, parents_here):
    lane = lane_of()
    for face in range(6):
        axis = face // 2
        side = face % 2
        opposite = face + 1 - 2 * side
        for block in range(nb):
            sibling = tab_ref[12 + axis, block]
            for c in range(5):
                ghost_ref[face, c, block_rows(block, nb, 4), :] = plane_ref[
                    opposite, c, block_rows(sibling, nb, 4), :
                ]
        for rt in range(nb // ROWS):
            octant = bits_ref[rt * ROWS : (rt + 1) * ROWS, :]
            slot = bits_ref[nb + rt * ROWS : nb + (rt + 1) * ROWS, :]
            outward = (octant // BIT_OF[axis]) % 2 == side
            first = (octant // TANGENT[axis][0]) % 2
            second = (octant // TANGENT[axis][1]) % 2
            which = 2 * slot + first
            for c in range(5):
                rims = rim_ref[face, c]
                if rim2_ref is not None:
                    rims = 0.5 * (rims + rim2_ref[face, c])
                source = jnp.broadcast_to(rims[0:1, :], (ROWS, LANES))
                for k in range(1, 2 * parents_here):
                    source = jnp.where(which == k, rims[k : k + 1, :], source)
                for half in range(2):
                    index = (
                        edge * ((edge // 4) * half + lane // edge // 2)
                        + (edge // 2) * second
                        + lane % edge // 2
                    )
                    outer = take_lanes(source, index)
                    for layer in range(2):
                        at = (layer * 2 + half) * nb + rt * ROWS
                        at = slice(at, at + ROWS)
                        ghost_ref[face, c, at, :] = jnp.where(
                            outward, outer, ghost_ref[face, c, at, :]
                        )


def fine_kernel(
    nb, edge, eager, parents_here, tab_ref, bits_ref, d_ref, plane_ref, rim_ref, new_ref, next_ref,
    face_ref, ghost_ref, add_ref, half_ref, base_ref, sem,
):
    fetch = pltpu.make_async_copy(d_ref, base_ref, sem)
    fetch.start()
    fine_ghosts(nb, edge, tab_ref, bits_ref, plane_ref, rim_ref, None, ghost_ref, parents_here)
    face_fluxes(plane_ref, ghost_ref, add_ref, face_ref, nb, eager)
    fetch.wait()
    expand_add(base_ref, add_ref, half_ref, 2, nb, edge, eager)
    inner_kernel(nb, edge, eager, half_ref, new_ref, next_ref)


def face_means(nb, edge, parents_here, tab_ref, one_ref, two_ref, mean_ref, quarter_ref):
    lane = lane_of()
    group = lane // edge
    sub = lane % edge
    index = edge * (2 * (group % (ROWS // 2))) + 2 * (sub % (edge // 2))
    for face in range(6):
        places = [
            (c, slice(half * nb + rt * ROWS, half * nb + (rt + 1) * ROWS))
            for c in range(5)
            for rt in range(nb // ROWS)
            for half in range(2)
        ]
        tiles = [one_ref[face, c, at, :] + two_ref[face, c, at, :] for c, at in places]
        tiles = [v + pltpu.roll(v, LANES - 1, 1) for v in tiles]
        tiles = [v + pltpu.roll(v, LANES - edge, 1) for v in tiles]
        tiles = [0.125 * take_lanes(v, index) for v in tiles]
        for k in range(0, len(tiles), 2):
            at = k // 2 * ROWS
            quarter_ref[face, at : at + ROWS, :] = jnp.where(
                group < ROWS // 2, tiles[k], tiles[k + 1]
            )
    left = iota((5, LANES), 1) % edge < edge // 2
    for face in range(6):
        axis = face // 2
        for p in range(parents_here):
            for half in range(2):
                octant = (face % 2) * BIT_OF[axis] + half * TANGENT[axis][0]
                one = tab_ref[CHILDREN + p, octant]
                two = tab_ref[CHILDREN + p, octant + TANGENT[axis][1]]
                value = jnp.where(
                    left,
                    quarter_ref[face, pl.ds(one, 5, stride=nb), :],
                    quarter_ref[face, pl.ds(two, 5, stride=nb), :],
                )
                for c in range(5):
                    mean_ref[face, c, 2 * p + half : 2 * p + half + 1, :] = value[c : c + 1, :]


def means_kernel(
    nb, edge, eager, parents_here, tab_ref, bits_ref, plane_ref, rim_ref, rim2_ref, one_ref, send_ref,
    add_ref, ghost_ref, face_ref, quarter_ref, mean_ref,
):
    fine_ghosts(nb, edge, tab_ref, bits_ref, plane_ref, rim_ref, rim2_ref, ghost_ref, parents_here)
    face_fluxes(plane_ref, ghost_ref, add_ref, face_ref, nb, eager)
    face_means(nb, edge, parents_here, tab_ref, one_ref, face_ref, mean_ref, quarter_ref)
    for face in range(6):
        for p in range(parents_here):
            item = face * nb + tab_ref[9, p]
            target = tab_ref[0, item]
            first = tab_ref[7, item] * 5
            for c in range(5):
                send_ref[target, first + c] = mean_ref[face, c, 2 * p : 2 * p + 2, :]


def finish_kernel(
    nb, edge, eager, parents_here, tab_ref, d_ref, add_ref, new_ref, average_ref, temp_ref, split_ref,
    eighth_ref,
):
    temp_ref[...] = add_ref[...]
    expand_add(d_ref, temp_ref, new_ref, 2, nb, edge, eager, split_ref)
    averages(nb, edge, parents_here, tab_ref, split_ref, average_ref, eighth_ref)


def averages(nb, edge, parents_here, tab_ref, split_ref, out_ref, eighth_ref):
    lane = lane_of()
    group = lane // edge
    index = edge * (2 * (group % (ROWS // 2))) + 2 * (lane % (edge // 2))
    for b in range(nb):
        tiles = [
            split_ref[b, c, h, pl.ds(0, ROWS, stride=2), :]
            + split_ref[b, c, h, pl.ds(1, ROWS, stride=2), :]
            for c in range(5)
            for h in range(2)
        ]
        tiles = [v + pltpu.roll(v, LANES - 1, 1) for v in tiles]
        tiles = [v + pltpu.roll(v, LANES - edge, 1) for v in tiles]
        tiles = [0.125 * take_lanes(v, index) for v in tiles]
        for c in range(5):
            eighth_ref[b, c] = jnp.where(group < ROWS // 2, tiles[2 * c], tiles[2 * c + 1])
    left = lane % edge < edge // 2
    for p in range(parents_here):
        for corner in range(4):
            one = tab_ref[CHILDREN + p, 2 * corner]
            two = tab_ref[CHILDREN + p, 2 * corner + 1]
            rows = slice(corner // 2 * ROWS, (corner // 2 + 1) * ROWS)
            lanes = slice(corner % 2 * LANES, (corner % 2 + 1) * LANES)
            for c in range(5):
                out_ref[p, c, rows, lanes] = jnp.where(left, eighth_ref[one, c], eighth_ref[two, c])


def correct_kernel(
    nb, edge, eager, parents_here, slots, tab_ref, bits_ref, new_ref, face_ref, recv_ref, cells_ref,
    out_ref, mean_ref, add_ref, done_ref, base_ref, sem, sems,
):
    fetch = pltpu.make_async_copy(new_ref, base_ref, sem)
    fetch.start()
    unpack(tab_ref, 8, slots, recv_ref, mean_ref, 2, nb)
    beside = bits_ref[2 * nb : 3 * nb, :]
    for face in range(6):
        sign = STEP_RATIO if face % 2 else -STEP_RATIO
        hit = (beside // (1 << face)) % 2 > 0
        for c in range(5):
            for half in range(2):
                at = slice(half * nb, (half + 1) * nb)
                add_ref[face, c, at, :] = jnp.where(
                    hit, sign * (face_ref[face, c, at, :] - mean_ref[face, c, at, :]), 0.0
                )
    fetch.wait()
    for p in range(parents_here):
        base_ref[tab_ref[9, p]] = cells_ref[p]
    copies = [
        pltpu.make_async_copy(done_ref.at[:, c], out_ref.at[:, c], sems.at[c]) for c in range(5)
    ]
    expand_add(base_ref, add_ref, done_ref, 1, nb, edge, eager, copies=copies)
    for copy in copies:
        copy.wait()


def column(row):
    return jnp.transpose(jnp.broadcast_to(row.astype(F32), (LANES, LANES)))


def count(hits):
    return jnp.sum(jnp.where(hits, 1.0, 0.0), axis=0, keepdims=True).astype(I32)


def tables_kernel(
    nb, devices, parents_here, blk_ref, all_near_ref, all_parent_ref, tab_ref, bits_ref, near_ref,
    parent_ref, sems,
):
    fetches = [
        pltpu.make_async_copy(all_near_ref, near_ref, sems.at[0]),
        pltpu.make_async_copy(all_parent_ref, parent_ref, sems.at[1]),
    ]
    for fetch in fetches:
        fetch.start()
    for fetch in fetches:
        fetch.wait()
    total = near_ref.shape[1]
    tiles = total // LANES
    start = blk_ref[0] * nb
    tile = pl.ds(pl.multiple_of(start // LANES * LANES, LANES), LANES)
    turn = (LANES - start % LANES) % LANES
    own = pltpu.roll(near_ref[:, tile], turn, 1)
    own_parent = pltpu.roll(parent_ref[:, tile], turn, 1)
    lane = iota((1, LANES), 1)
    face = lane // nb
    block = lane % nb
    row = iota((LANES, LANES), 0)
    near = jnp.zeros((1, LANES), I32)
    for f in range(6):
        near = jnp.where(face == f, pltpu.roll(own[f : f + 1, :], nb * f, 1), near)
    target = near // nb
    wanted = (face + 1 - 2 * (face % 2)) * nb + near % nb
    wanted_f = wanted.astype(F32)
    parent_columns = [
        column(parent_ref[0:1, k * LANES : (k + 1) * LANES]) for k in range(tiles)
    ]

    def any_parent(ids):
        ids = ids.astype(F32)
        hits = [jnp.max(jnp.where(x == ids, 1.0, 0.0), axis=0, keepdims=True) for x in parent_columns]
        return functools.reduce(jnp.maximum, hits)

    beside = any_parent(near)
    parent = own_parent[0:1, :] - start
    octant = own_parent[1:2, :]
    parent_column = column(parent)
    octant_column = column(octant)
    mine = row < nb
    owned = jnp.max(
        jnp.where(mine & (parent_column == block.astype(F32)), 1.0, 0.0), axis=0, keepdims=True
    )
    same = (column(target) == target.astype(F32)) & (row < 6 * nb)
    by_own = same & (row < lane)
    by_wanted = same & (column(wanted) < wanted_f)
    beside_column = column(beside) > 0.0
    owned_column = column(owned) > 0.0
    parent_f = parent.astype(F32)
    slot = count(mine & (parent_column < parent_f)) // 8
    slot_column = column(slot)
    row_f = row.astype(F32)
    lane_f = lane.astype(F32)

    def pick(hits, values):
        return jnp.sum(jnp.where(mine & hits, values, 0.0), axis=0, keepdims=True).astype(I32)

    rows = [
        target,
        count(by_own),
        count(by_wanted),
        beside.astype(I32),
        owned.astype(I32),
        count(by_own & beside_column),
        count(by_wanted & owned_column),
        count(by_own & owned_column),
        count(by_wanted & beside_column),
        pick((octant_column == 0.0) & (slot_column == lane_f), parent_column),
        octant,
        slot,
    ]
    for bit in BIT_OF:
        partner = (octant + bit - 2 * bit * (octant // bit % 2)).astype(F32)
        rows.append(pick((parent_column == parent_f) & (octant_column == partner), row_f))
    children = [
        pick((slot_column == p) & (octant_column == lane_f), row_f) for p in range(parents_here)
    ]
    free = mine & (owned_column == False)
    place = column(lane - count(mine & owned_column & (row < lane)))
    others = pick(free & (place == lane_f), row_f)

    most = jnp.zeros((devices, LANES), F32)
    most_all = jnp.zeros((devices, LANES), F32)
    device = iota((devices, LANES), 0)
    lanes_2d = iota((devices, LANES), 1)
    for k in range(tiles):
        lanes = slice(k * LANES, (k + 1) * LANES)
        hits = jnp.zeros((devices, LANES), F32)
        for f in range(6):
            hits = hits + jnp.where(near_ref[f : f + 1, lanes] // nb == device, 1.0, 0.0)
        sums = [hits * any_parent(k * LANES + lane), hits]
        width = 1
        while width < nb:
            sums = [x + pltpu.roll(x, LANES - width, 1) for x in sums]
            width *= 2
        start_lane = lanes_2d % nb == 0
        opposite = (k * LANES + lanes_2d) // nb + devices // 2
        opposite = jnp.where(opposite >= devices, opposite - devices, opposite) == device
        most = jnp.maximum(most, jnp.where(start_lane, sums[0], 0.0))
        most_all = jnp.maximum(most_all, jnp.where(start_lane & ~opposite, sums[1], 0.0))
    for values in (most, most_all):
        values = jnp.max(jnp.max(values, axis=0, keepdims=True), axis=1, keepdims=True)
        rows.append(jnp.broadcast_to(values, (1, LANES)).astype(I32))
    rows = rows + [others, jnp.broadcast_to(blk_ref[0], (1, LANES))] + children
    for k, values in enumerate(rows):
        tab_ref[k : k + 1, :] = values

    beside_bits = jnp.zeros((1, LANES), F32)
    for f in range(6):
        part = jnp.where(face == f, beside * (1 << f), 0.0)
        beside_bits = beside_bits + pltpu.roll(part, (LANES - nb * f) % LANES, 1)
    for k, values in enumerate((octant_column, slot_column, column(beside_bits))):
        bits_ref[k * nb : (k + 1) * nb, :] = values[0:nb, :].astype(I32)


def run(
    kernel, outs, operands, scratch=(), scalars=0, far=None, remote=(), copies=None, flops=0
):
    held = [o.shape for o in operands] + list(outs) + list(scratch)
    limit = sum(4 * max(math.prod(s), 8 * LANES) for s in held) + SPARE
    smem = pl.BlockSpec(memory_space=pltpu.SMEM)
    vmem = pl.BlockSpec(memory_space=pltpu.VMEM)
    hbm = pl.BlockSpec(memory_space=pltpu.HBM)
    specs = [smem if k < scalars else vmem for k in range(len(operands))]
    scratches = [pltpu.VMEM(s, F32) for s in scratch]
    if far is not None:
        specs[far] = hbm
        scratches.append(pltpu.SemaphoreType.DMA)
    if remote:
        scratches.append(pltpu.SemaphoreType.DMA((copies or len(remote),)))
    return pl.pallas_call(
        kernel,
        out_shape=[jax.ShapeDtypeStruct(s, F32) for s in outs],
        in_specs=specs,
        out_specs=[hbm if k in remote else vmem for k in range(len(outs))],
        scratch_shapes=scratches,
        compiler_params=pltpu.CompilerParams(vmem_limit_bytes=limit),
        cost_estimate=pl.CostEstimate(
            flops=flops, bytes_accessed=4 * sum(o.size for o in operands), transcendentals=0
        ),
    )(*operands)


def blank(*shapes):
    return pl.pallas_call(
        lambda *refs: None,
        out_shape=[jax.ShapeDtypeStruct(s, F32) for s in shapes],
        out_specs=[pl.BlockSpec(memory_space=pl.ANY)] * len(shapes),
    )()


def level_shift(array, source):
    return lax.ppermute(array, "level", [(source, 1 - source)])


def route(buffer):
    return lax.all_to_all(buffer, "blk", split_axis=0, concat_axis=0, tiled=True)


def local(fluid_state, neighbours, parents):
    blk_index = lax.axis_index("blk")
    devices = lax.axis_size("blk")
    u = fluid_state[0]
    nb, _, edge, _ = u.shape
    parents_here = nb // 8
    capacity = 2 * ((6 * nb + devices - 1) // devices)
    smem = pl.BlockSpec(memory_space=pltpu.SMEM)
    vmem = pl.BlockSpec(memory_space=pltpu.VMEM)
    hbm = pl.BlockSpec(memory_space=pltpu.HBM)
    table, bits = pl.pallas_call(
        functools.partial(tables_kernel, nb, devices, parents_here),
        out_shape=[
            jax.ShapeDtypeStruct((CHILDREN + parents_here, LANES), I32),
            jax.ShapeDtypeStruct((3 * nb, LANES), I32),
        ],
        in_specs=[smem, hbm, hbm],
        out_specs=[vmem, vmem],
        scratch_shapes=[
            pltpu.VMEM(neighbours.shape[::-1], I32),
            pltpu.VMEM(parents.shape[::-1], I32),
            pltpu.SemaphoreType.DMA((2,)),
        ],
        compiler_params=pltpu.CompilerParams(vmem_limit_bytes=7 * SPARE),
    )(jnp.reshape(blk_index, (1,)).astype(I32), neighbours.T, parents.T)

    few = max(1, capacity // 3)
    half = max(1, capacity // 2)
    counts = table[COUNTS : COUNTS + 2, 0]
    finished = lax.cond(
        (counts[0] <= few) & (counts[1] <= half) & (devices % 2 == 0),
        functools.partial(step, capacity, half, few),
        functools.partial(step, capacity, capacity, capacity),
        u,
        table,
        bits,
    )
    return finished[None]


def step(capacity, wide, slots, u, table, bits):
    eager = wide < capacity
    level_id = lax.axis_index("level")
    devices = lax.axis_size("blk")
    nb, _, edge, square = u.shape
    parents_here = nb // 8
    part = functools.partial
    cell_shape = u.shape
    plane_shape = (6, 5, 6 * nb, LANES)
    ghost_shape = (6, 5, 4 * nb, LANES)
    face_shape = (6, 5, 2 * nb, LANES)
    rim_shape = (6, 5, 2 * parents_here, LANES)
    wide_sends = [(devices * wide * 5, 4, LANES)]
    if wide < capacity:
        wide_sends.append(((capacity - wide) * 5, 4, LANES))
    thin_send = (devices, slots * 5, 2, LANES)
    average_shape = (parents_here,) + cell_shape[1:]
    work = 220 * 3 * 5 * nb * edge * square

    def inner(cells):
        return run(part(inner_kernel, nb, edge, False), [cell_shape, plane_shape], [cells], flops=work)

    def half_way_round(buffer):
        turned = [(d, (d + devices // 2) % devices) for d in range(devices)]
        return lax.ppermute(buffer, ("level", "blk"), turned)

    def coarse_first(u):
        planes, *sends = run(
            part(send_kernel, nb, edge, eager, wide, devices),
            [plane_shape] + wide_sends,
            [table, u],
            [(sum(x[0] for x in wide_sends), 4, LANES)],
            1,
            remote=range(1, 1 + len(wide_sends)),
        )
        received = [route(sends[0].reshape(devices, wide * 5, 4, LANES))]
        received += [half_way_round(buffer) for buffer in sends[1:]]
        partial_new, near = run(
            part(coarse_inner_kernel, nb, edge, False), [cell_shape, face_shape], [table, u], (), 1,
            flops=work,
        )
        adds, faces, send, rims = run(
            part(coarse_kernel, nb, edge, eager, parents_here, wide, slots),
            [ghost_shape, face_shape, thin_send, rim_shape],
            [table, planes, near] + received,
            [ghost_shape, face_shape],
            1,
        )
        return (partial_new, adds, faces, send, rims, *blank(plane_shape))

    def fine_first(u):
        partial_new, planes = inner(u)
        return (partial_new, *blank(ghost_shape, face_shape, thin_send, rim_shape), planes)

    partial_new, adds, faces, send, rims, planes = lax.cond(
        level_id == 0, coarse_first, fine_first, u
    )
    early_rims = level_shift(rims, 0)

    def coarse_second(send, partial_new, adds, planes, early_rims):
        received = route(send)
        (cells,) = run(
            part(coarse_cells_kernel, nb, edge, False),
            [cell_shape],
            [partial_new, adds],
            [ghost_shape],
            flops=work // 4,
        )
        (late,) = run(part(rims_kernel, nb, parents_here), [rim_shape], [table, received], (), 1)
        return (late, cells, *blank(plane_shape, face_shape))

    def fine_second(send, partial_new, adds, planes, early_rims):
        results = run(
            part(fine_kernel, nb, edge, eager, parents_here),
            [cell_shape, plane_shape, face_shape],
            [table, bits, partial_new, planes, early_rims],
            [ghost_shape, ghost_shape, cell_shape, cell_shape],
            1,
            far=2,
            flops=work,
        )
        return (*blank(rim_shape), *results)

    late, cells, half_planes, half_faces = lax.cond(
        level_id == 0, coarse_second, fine_second, send, partial_new, adds, planes, early_rims
    )
    late_rims = level_shift(late, 0)

    def coarse_third(cells, half_planes, half_faces, early_rims, late_rims):
        return tuple(blank(thin_send, cell_shape, average_shape))

    def fine_third(cells, half_planes, half_faces, early_rims, late_rims):
        send, adds = run(
            part(means_kernel, nb, edge, eager, parents_here),
            [thin_send, ghost_shape],
            [table, bits, half_planes, early_rims, late_rims, half_faces],
            [ghost_shape, face_shape, (6, 5 * nb, LANES), rim_shape],
            1,
        )
        received = route(send)
        out, averaged = run(
            part(finish_kernel, nb, edge, False, parents_here),
            [cell_shape, average_shape],
            [table, cells, adds],
            [ghost_shape, (nb, 5, 2, edge, LANES), (nb, 5, ROWS, LANES)],
            1,
            flops=work,
        )
        return received, out, averaged

    returned, out, averaged = lax.cond(
        level_id == 0, coarse_third, fine_third,
        cells, half_planes, half_faces, early_rims, late_rims,
    )
    returned = level_shift(returned, 1)
    averaged = level_shift(averaged, 1)

    def correct(out, cells, faces, returned, averaged):
        return run(
            part(correct_kernel, nb, edge, eager, parents_here, slots),
            [cell_shape],
            [table, bits, cells, faces, returned, averaged],
            [face_shape, face_shape, cell_shape, cell_shape],
            1,
            far=2,
            remote=range(1),
            copies=5,
        )[0]

    return lax.cond(
        level_id == 0, correct, lambda out, *rest: out, out, cells, faces, returned, averaged
    )


def solution(mesh):
    return jax.shard_map(
        local,
        mesh=mesh,
        in_specs=(P("level", "blk", None, None, None), P(), P()),
        out_specs=P("level", "blk", None, None, None),
        check_vma=False,
    )
```

```python
import functools
import math

import jax
import jax.numpy as jnp
from jax import lax
from jax.experimental import pallas as pl
from jax.experimental.pallas import tpu as pltpu
from jax.sharding import PartitionSpec as P

GAS_GAMMA = 1.4
STEP_RATIO = 0.12
BIT_OF = (4, 2, 1)
TANGENT = ((2, 1), (4, 1), (4, 2))
F32 = jnp.float32
I32 = jnp.int32
SPARE = 8 * 1024 * 1024
LANES = 128
ROWS = 8
COUNTS = 15
OTHERS = 17
SELF = 18
CHILDREN = 19


def iota(shape, dim):
    return lax.broadcasted_iota(I32, shape, dim)


def reciprocal(x):
    return pltpu.reciprocal(x, approx=True)


def physical_flux(s, n):
    inv = reciprocal(s[0])
    vn = s[n] * inv
    kinetic = s[1] * s[1] + s[2] * s[2] + s[3] * s[3]
    p = (GAS_GAMMA - 1.0) * (s[4] - 0.5 * (kinetic * inv))
    out = [s[n], s[1] * vn, s[2] * vn, s[3] * vn, (s[4] + p) * vn]
    out[n] = out[n] + p
    return out


def evolve(u, below, above, n):
    low = []
    high = []
    for c in range(5):
        d = jnp.maximum(jnp.minimum(below[c], above[c]), 0.0) + jnp.minimum(
            jnp.maximum(below[c], above[c]), 0.0
        )
        d = 0.5 * d
        low.append(u[c] - d)
        high.append(u[c] + d)
    fl = physical_flux(low, n)
    fh = physical_flux(high, n)
    for c in range(5):
        change = (0.5 * STEP_RATIO) * (fl[c] - fh[c])
        low[c] = low[c] + change
        high[c] = high[c] + change
    return low, high


def side_values(s, n):
    inv = reciprocal(s[0])
    vn = s[n] * inv
    kinetic = s[1] * s[1] + s[2] * s[2] + s[3] * s[3]
    p = (GAS_GAMMA - 1.0) * (s[4] - 0.5 * (kinetic * inv))
    square = GAS_GAMMA * p * inv
    sound = square * lax.rsqrt(square)
    return vn, p, sound


def hllc(a, b, n):
    va, pa, ca = side_values(a, n)
    vb, pb, cb = side_values(b, n)
    slow = jnp.minimum(va - ca, vb - cb)
    fast = jnp.maximum(va + ca, vb + cb)
    qa = a[0] * (slow - va)
    qb = b[0] * (fast - vb)
    contact = (pb - pa + va * qa - vb * qb) * reciprocal(qa - qb)
    is_low = contact >= 0.0

    def pick(x, y):
        return jnp.where(is_low, x, y)

    s = [pick(a[c], b[c]) for c in range(5)]
    v = pick(va, vb)
    p = pick(pa, pb)
    q = pick(qa, qb)
    speed = pick(slow, fast)
    clipped = pick(jnp.minimum(slow, 0.0), jnp.maximum(fast, 0.0))
    extra = clipped * (contact - v) * reciprocal(speed - contact)
    h = v + extra
    push = extra * q
    out = [s[0] * h, s[1] * h, s[2] * h, s[3] * h, (s[4] + p) * h + push * contact]
    out[n] = out[n] + p + push
    return out


def lane_of():
    return iota((ROWS, LANES), 1)


def row_of():
    return iota((ROWS, LANES), 0)


def take_lanes(v, index):
    return jnp.take_along_axis(v, index, axis=1, mode="promise_in_bounds")


def slide_groups(tiles, edge):
    group = lane_of() // edge
    for bit in (1, 2, 4):
        moves = (group & bit) != 0
        tiles = [jnp.where(moves, pltpu.roll(g, bit, 0), g) for g in tiles]
    return tiles


def swap_front(tiles, edge, skews):
    base = lane_of() + edge * row_of()
    return slide_groups(
        [take_lanes(v, (base + skew) % LANES) for v, skew in zip(tiles, skews)], edge
    )


def swap_back_index(lane, edge):
    return edge * ((row_of() - lane // edge + ROWS) % ROWS) + lane % edge


def extract(u_ref, plane_ref, layers, nb, edge, eager):
    groups = LANES // edge
    for side in range(2):
        for layer in range(layers):
            x = layer if side == 0 else edge - 1 - layer
            for c in range(5):
                for half in range(2):
                    at = (layer * 2 + half) * nb
                    plane_ref[side, c, at : at + nb, :] = u_ref[
                        :, c, x, half * LANES : (half + 1) * LANES
                    ]
    lane = lane_of()
    row = row_of()
    grp = lane // edge
    sub = lane % edge
    zero = jnp.zeros((ROWS, LANES), F32)
    offsets = [o for layer in range(layers) for o in (layer, edge - 1 - layer)]

    def rows_at(layer, rt, h):
        at = (layer * 2 + rt) * nb + h * ROWS
        return slice(at, at + ROWS)

    def gather(c, carry):
        for rt in range(2):
            rows = slice(rt * ROWS, (rt + 1) * ROWS)
            ylow = [[zero, zero] for _ in range(layers)]
            yhigh = [[zero, zero] for _ in range(layers)]
            for b in range(nb):
                t = b // groups
                turn = edge * b % LANES
                low = u_ref[b, c, rows, :LANES]
                high = u_ref[b, c, rows, LANES:]
                low = pltpu.roll(low, turn, 1) if turn else low
                high = pltpu.roll(high, turn, 1) if turn else high
                for layer in range(layers):
                    ylow[layer][t] = jnp.where(grp == (b + layer) % groups, low, ylow[layer][t])
                    yhigh[layer][t] = jnp.where(
                        grp == (b + groups - 1 - layer) % groups, high, yhigh[layer][t]
                    )
            for layer in range(layers):
                for h in range(2):
                    plane_ref[2, c, rows_at(layer, rt, h), :] = ylow[layer][h]
                    plane_ref[3, c, rows_at(layer, rt, h), :] = yhigh[layer][h]
            for h in range(2):
                zacc = {o: zero for o in offsets}
                for b in range(nb):
                    r = u_ref[b, c, rows, h * LANES : (h + 1) * LANES]
                    r = pltpu.roll(r, b, 1) if b else r
                    for o in offsets:
                        zacc[o] = jnp.where(sub == (b + o) % edge, r, zacc[o])
                for layer in range(layers):
                    plane_ref[4, c, rows_at(layer, rt, h), :] = zacc[layer]
                    plane_ref[5, c, rows_at(layer, rt, h), :] = zacc[edge - 1 - layer]
        return carry

    lax.fori_loop(0, 5, gather, 0, unroll=5 if eager else 1)

    def turn(c, carry):
        last = swap_back_index(lane, edge)
        places = [
            (face, rows_at(layer, rt, h), skew)
            for layer in range(layers)
            for face, skew in ((2, edge * layer), (3, edge * (groups - 1 - layer)))
            for rt in range(2)
            for h in range(2)
        ]
        tiles = swap_front(
            [plane_ref[face, c, at, :] for face, at, _ in places], edge, [p[2] for p in places]
        )
        tiles = [take_lanes(v, last) for v in tiles]
        for (face, at, _), v in zip(places, tiles):
            plane_ref[face, c, at, :] = v
        places = []
        tiles = []
        for layer in range(layers):
            for face, o in ((4, layer), (5, edge - 1 - layer)):
                for rt in range(2):
                    raw = [plane_ref[face, c, rows_at(layer, rt, h), :] for h in range(2)]
                    for h in range(2):
                        index = (edge * (sub % ROWS) + ROWS * h + (grp + row) % ROWS + o) % LANES
                        tiles.append([take_lanes(v, index) for v in raw])
                        places.append((face, rows_at(layer, rt, h)))
        tiles = slide_groups([jnp.where(sub < ROWS, v, w) for v, w in tiles], edge)
        tiles = [take_lanes(v, last) for v in tiles]
        for (face, at), v in zip(places, tiles):
            plane_ref[face, c, at, :] = v
        return carry

    lax.fori_loop(0, 5, turn, 0, unroll=5 if eager else 1)


def expand_add(base_ref, add_ref, out_ref, layers, nb, edge, eager, split_ref=None, copies=()):
    groups = LANES // edge
    lane = lane_of()
    row = row_of()
    grp = lane // edge
    sub = lane % edge

    def rows_at(layer, rt, h):
        at = (layer * 2 + rt) * nb + h * ROWS
        return slice(at, at + ROWS)

    def turn(c, carry):
        places = [
            (face, layer, rt, skew)
            for layer in range(layers)
            for face, skew in (
                (2, edge * layer),
                (3, (LANES - edge * layer) % LANES),
                (4, layer),
                (5, edge - 1 - layer),
            )
            for rt in range(2)
        ]
        loaded = [
            add_ref[face, c, rows_at(layer, rt, h), :]
            for face, layer, rt, _ in places
            for h in range(2)
        ]
        mid = swap_front(loaded, edge, [0] * len(loaded))
        out = []
        for k, (face, layer, rt, skew) in enumerate(places):
            moved = (lane - skew + LANES) % LANES
            pair = mid[2 * k : 2 * k + 2]
            if face < 4:
                index = swap_back_index(moved, edge)
                out.append([take_lanes(v, index) for v in pair])
            else:
                block = moved % edge
                base = edge * ((row - block % ROWS + ROWS) % ROWS) + moved // edge
                parts = [[take_lanes(v, base + ROWS * h) for v in pair] for h in range(2)]
                out.append([jnp.where(block < ROWS, v, w) for v, w in parts])
        for (face, layer, rt, _), pair in zip(places, out):
            for h in range(2):
                add_ref[face, c, rows_at(layer, rt, h), :] = pair[h]
        return carry

    lax.fori_loop(0, 5, turn, 0, unroll=5 if eager else 1)

    def spread(c, carry):
        for rt in range(2):
            rows = slice(rt * ROWS, (rt + 1) * ROWS)

            def tile(face, h):
                return [add_ref[face, c, rows_at(layer, rt, h), :] for layer in range(layers)]

            ylow = [tile(2, h) for h in range(2)]
            yhigh = [tile(3, h) for h in range(2)]
            zlow = [tile(4, h) for h in range(2)]
            zhigh = [tile(5, h) for h in range(2)]
            for b in range(nb):
                t = b // groups
                place = b % groups
                low = ylow[t][0]
                high = yhigh[t][0]
                if layers > 1:
                    low = jnp.where(grp == place, low, ylow[t][1])
                    high = jnp.where(grp == place, high, yhigh[t][1])
                low = pltpu.roll(low, (LANES - edge * place) % LANES, 1)
                high = pltpu.roll(high, edge * (groups - 1 - place) % LANES, 1)
                parts = [
                    jnp.where(grp < layers, low, 0.0),
                    jnp.where(grp >= groups - layers, high, 0.0),
                ]
                for h in range(2):
                    lanes = slice(h * LANES, (h + 1) * LANES)
                    z = zhigh[h][0]
                    if layers > 1:
                        z = jnp.where(sub == (b + edge - 1) % edge, z, zhigh[h][1])
                        z = jnp.where(sub == (b + 1) % edge, zlow[h][1], z)
                    z = jnp.where(sub == b, zlow[h][0], z)
                    if b:
                        z = pltpu.roll(z, LANES - b, 1)
                    total = parts[h] + jnp.where((sub < layers) | (sub >= edge - layers), z, 0.0)
                    x = add_ref[rt, c, h * nb + b : h * nb + b + 1, :]
                    x = jnp.where(row == (ROWS - 1) * rt, x, 0.0)
                    if layers > 1:
                        deeper = add_ref[rt, c, (2 + h) * nb + b : (2 + h) * nb + b + 1, :]
                        x = jnp.where(row == 1 + (ROWS - 3) * rt, deeper, x)
                    value = base_ref[b, c, rows, lanes] + (total + x)
                    out_ref[b, c, rows, lanes] = value
                    if split_ref is not None:
                        split_ref[b, c, h, rows, :] = value
        return carry

    if eager:
        for c in range(5):
            spread(c, 0)
            for copy in copies[c : c + 1]:
                copy.start()
    else:
        lax.fori_loop(0, 5, spread, 0)
        for copy in copies:
            copy.start()


def block_rows(block, nb, count):
    return pl.ds(block, count, stride=nb)


def pack(tab_ref, valid_row, slot_row, slots, plane_ref, send_ref, count, nb):
    for face in range(6):
        for block in range(nb):
            item = face * nb + block
            valid = tab_ref[valid_row, item] > 0
            target = jnp.where(valid, tab_ref[0, item], tab_ref[SELF, 0])
            first = jnp.where(valid, tab_ref[slot_row, item] * 5, 0)
            for c in range(5):
                send_ref[target, first + c] = plane_ref[face, c, block_rows(block, nb, count), :]


def unpack(tab_ref, slot_row, slots, recv_ref, plane_ref, count, nb):
    for face in range(6):
        for block in range(nb):
            item = face * nb + block
            target = tab_ref[0, item]
            first = jnp.minimum(tab_ref[slot_row, item], slots - 1) * 5
            for c in range(5):
                plane_ref[face, c, block_rows(block, nb, count), :] = recv_ref[target, first + c]


def pack_wide(tab_ref, slots, devices, plane_ref, all_ref, nb):
    for face in range(6):
        for block in range(nb):
            item = face * nb + block
            slot = tab_ref[1, item]
            first = jnp.where(
                slot < slots, tab_ref[0, item] * slots + slot, (devices - 1) * slots + slot
            )
            for c in range(5):
                all_ref[first * 5 + c] = plane_ref[face, c, block_rows(block, nb, 4), :]


def unpack_wide(tab_ref, slots, recv_ref, over_ref, plane_ref, nb):
    for face in range(6):
        for block in range(nb):
            item = face * nb + block
            target = tab_ref[0, item]
            slot = tab_ref[2, item]
            first = jnp.minimum(slot, slots - 1) * 5
            beyond = jnp.maximum(slot - slots, 0) * 5
            for c in range(5):
                value = recv_ref[target, first + c]
                if over_ref is not None:
                    value = jnp.where(slot < slots, value, over_ref[beyond + c])
                plane_ref[face, c, block_rows(block, nb, 4), :] = value


def take_rims(tab_ref, slot_row, recv_ref, rim_ref, parents_here, nb):
    for face in range(6):
        for p in range(parents_here):
            item = face * nb + tab_ref[9, p]
            target = tab_ref[0, item]
            first = tab_ref[slot_row, item] * 5
            for c in range(5):
                rim_ref[face, c, 2 * p : 2 * p + 2, :] = recv_ref[target, first + c, 0:2, :]


def interior(nb, edge, eager, u_ref, d_ref, tab_ref=None, axes=(0, 1, 2), from_ref=None):
    square = edge * edge

    def sweep(u, axis, index, size, step, dim):
        n = 1 + axis
        below = [x - pltpu.roll(x, step, dim) for x in u]
        above = [pltpu.roll(x, size - step, dim) for x in below]
        low, high = evolve(u, below, above, n)
        prev = [pltpu.roll(x, step, dim) for x in high]
        inside = (index >= 2) & (index <= edge - 2)
        flux = [jnp.where(inside, x, 0.0) for x in hllc(prev, low, n)]
        return [pltpu.roll(x, size - step, dim) - x for x in flux]

    columns = {0: (iota((edge, LANES), 0), edge, 1, 0), 2: (iota((edge, LANES), 1) % edge, LANES, 1, 1)}
    from_ref = d_ref if from_ref is None else from_ref

    def work(b):
        for rt in range(edge // ROWS if 1 in axes else 0):
            rows = slice(rt * ROWS, (rt + 1) * ROWS)
            u = [u_ref[b, c, rows, :] for c in range(5)]
            div = sweep(u, 1, iota((ROWS, square), 1) // edge, square, edge, 1)
            for c in range(5):
                d_ref[b, c, rows, :] = u[c] - STEP_RATIO * div[c]
        for half in range(square // LANES):
            lanes = slice(half * LANES, (half + 1) * LANES)
            u = [u_ref[b, c, :, lanes] for c in range(5)]
            parts = [sweep(u, axis, *columns[axis]) for axis in (0, 2) if axis in axes]
            for c in range(5):
                total = sum(part[c] for part in parts)
                d_ref[b, c, :, lanes] = from_ref[b, c, :, lanes] - STEP_RATIO * total

    def body(k, carry):
        work(k if tab_ref is None else tab_ref[OTHERS, k])
        return carry

    lax.fori_loop(0, nb if tab_ref is None else nb - nb // 8, body, 0, unroll=2 if eager else 1)


def face_fluxes(plane_ref, ghost_ref, add_ref, face_ref, nb, eager):
    for face in range(6):
        axis = face // 2
        side = face % 2
        n = 1 + axis
        sign = 1.0 - 2.0 * side

        def body(half, carry):
            def rows(layer):
                return pl.ds(pl.multiple_of((layer * 2 + half) * nb, ROWS), nb)

            def load(ref, layer):
                return [ref[face, c, rows(layer), :] for c in range(5)]

            near, mid, deep = (load(plane_ref, layer) for layer in range(3))
            ghost, far = (load(ghost_ref, layer) for layer in range(2))

            def steps(a, b):
                return [sign * (y - x) for x, y in zip(a, b)]

            d0, d1, d2, d3 = steps(far, ghost), steps(ghost, near), steps(near, mid), steps(mid, deep)
            if side == 0:
                first = hllc(evolve(ghost, d0, d1, n)[1], evolve(near, d1, d2, n)[0], n)
                second = hllc(evolve(near, d1, d2, n)[1], evolve(mid, d2, d3, n)[0], n)
            else:
                first = hllc(evolve(near, d1, d2, n)[1], evolve(ghost, d0, d1, n)[0], n)
                second = hllc(evolve(mid, d2, d3, n)[1], evolve(near, d1, d2, n)[0], n)
            for c in range(5):
                face_ref[face, c, rows(0), :] = first[c]
                add_ref[face, c, rows(0), :] = (sign * STEP_RATIO) * (first[c] - second[c])
                add_ref[face, c, rows(1), :] = (sign * STEP_RATIO) * second[c]
            return carry

        lax.fori_loop(0, 2, body, 0, unroll=2 if eager else 1)


def inner_kernel(nb, edge, eager, u_ref, d_ref, plane_ref):
    extract(u_ref, plane_ref, 3, nb, edge, eager)
    interior(nb, edge, eager, u_ref, d_ref)


def coarse_inner_kernel(nb, edge, eager, tab_ref, u_ref, d_ref, near_ref):
    interior(nb, edge, eager, u_ref, d_ref, tab_ref)
    extract(d_ref, near_ref, 1, nb, edge, eager)


def send_kernel(nb, edge, eager, slots, devices, tab_ref, u_ref, plane_ref, *refs):
    *out_refs, all_ref, sems = refs
    extract(u_ref, plane_ref, 3, nb, edge, eager)
    pack_wide(tab_ref, slots, devices, plane_ref, all_ref, nb)
    start = 0
    copies = []
    for k, out_ref in enumerate(out_refs):
        count = out_ref.shape[0]
        copies.append(
            pltpu.make_async_copy(all_ref.at[start : start + count], out_ref, sems.at[k])
        )
        copies[-1].start()
        start += count
    for copy in copies:
        copy.wait()


def near_layers(near_ref, add_ref, new_ref, nb, edge):
    lane = lane_of()
    group = lane // edge
    sub = lane % edge
    views = ((1, 2), (0, 2), (0, 1))

    def rows_at(layer, half, rt):
        at = (layer * 2 + half) * nb + rt * ROWS
        return slice(at, at + ROWS)

    def body(c, carry):
        for face in range(6):
            axis = face // 2
            depth = 0 if face % 2 == 0 else edge - 1
            for half in range(2):
                tiles = []
                for rt in range(nb // ROWS):
                    at = rows_at(0, half, rt)
                    tiles.append(near_ref[face, c, at, :] + add_ref[face, c, at, :])
                for other in range(6):
                    lateral = other // 2
                    if lateral == axis:
                        continue
                    first = views[axis][0] == lateral
                    along = sub if first else group + half * ROWS
                    for layer in range(2):
                        place = layer if other % 2 == 0 else edge - 1 - layer
                        if first:
                            if place // ROWS != half:
                                continue
                            hit = group == place % ROWS
                        else:
                            hit = sub == place
                        for rt in range(nb // ROWS):
                            if views[lateral][0] == axis:
                                index = edge * (depth % ROWS) + along
                                value = take_lanes(
                                    add_ref[other, c, rows_at(layer, depth // ROWS, rt), :], index
                                )
                            elif first:
                                index = edge * (along % ROWS) + depth
                                value = jnp.where(
                                    along < ROWS,
                                    take_lanes(add_ref[other, c, rows_at(layer, 0, rt), :], index),
                                    take_lanes(add_ref[other, c, rows_at(layer, 1, rt), :], index),
                                )
                            else:
                                index = edge * group + depth
                                value = take_lanes(
                                    add_ref[other, c, rows_at(layer, half, rt), :], index
                                )
                            tiles[rt] = tiles[rt] + jnp.where(hit, value, 0.0)
                for rt in range(nb // ROWS):
                    new_ref[face, c, rows_at(0, half, rt), :] = tiles[rt]
        return carry

    lax.fori_loop(0, 5, body, 0)


def coarse_kernel(
    nb, edge, eager, parents_here, slots, thin, tab_ref, plane_ref, near_ref, recv_ref, *refs
):
    *over_ref, add_ref, face_ref, send_ref, rim_ref, ghost_ref, new_ref = refs
    unpack_wide(tab_ref, slots, recv_ref, over_ref[0] if over_ref else None, ghost_ref, nb)
    for face in range(6):
        for p in range(parents_here):
            block = tab_ref[9, p]
            for c in range(5):
                rim_ref[face, c, 2 * p : 2 * p + 2, :] = ghost_ref[
                    face, c, block_rows(block, nb, 2), :
                ]
    face_fluxes(plane_ref, ghost_ref, add_ref, face_ref, nb, eager)
    near_layers(near_ref, add_ref, new_ref, nb, edge)
    pack(tab_ref, 3, 5, thin, new_ref, send_ref, 2, nb)


def coarse_cells_kernel(nb, edge, eager, d_ref, add_ref, new_ref, temp_ref):
    temp_ref[...] = add_ref[...]
    expand_add(d_ref, temp_ref, new_ref, 2, nb, edge, eager)


def rims_kernel(nb, parents_here, tab_ref, recv_ref, rim_ref):
    take_rims(tab_ref, 6, recv_ref, rim_ref, parents_here, nb)


def fine_ghosts(nb, edge, tab_ref, bits_ref, plane_ref, rim_ref, rim2_ref, ghost_ref, parents_here):
    lane = lane_of()
    for face in range(6):
        axis = face // 2
        side = face % 2
        opposite = face + 1 - 2 * side
        for block in range(nb):
            sibling = tab_ref[12 + axis, block]
            for c in range(5):
                ghost_ref[face, c, block_rows(block, nb, 4), :] = plane_ref[
                    opposite, c, block_rows(sibling, nb, 4), :
                ]
        for rt in range(nb // ROWS):
            octant = bits_ref[rt * ROWS : (rt + 1) * ROWS, :]
            slot = bits_ref[nb + rt * ROWS : nb + (rt + 1) * ROWS, :]
            outward = (octant // BIT_OF[axis]) % 2 == side
            first = (octant // TANGENT[axis][0]) % 2
            second = (octant // TANGENT[axis][1]) % 2
            which = 2 * slot + first
            for c in range(5):
                rims = rim_ref[face, c]
                if rim2_ref is not None:
                    rims = 0.5 * (rims + rim2_ref[face, c])
                source = jnp.broadcast_to(rims[0:1, :], (ROWS, LANES))
                for k in range(1, 2 * parents_here):
                    source = jnp.where(which == k, rims[k : k + 1, :], source)
                for half in range(2):
                    index = (
                        edge * ((edge // 4) * half + lane // edge // 2)
                        + (edge // 2) * second
                        + lane % edge // 2
                    )
                    outer = take_lanes(source, index)
                    for layer in range(2):
                        at = (layer * 2 + half) * nb + rt * ROWS
                        at = slice(at, at + ROWS)
                        ghost_ref[face, c, at, :] = jnp.where(
                            outward, outer, ghost_ref[face, c, at, :]
                        )


def fine_kernel(
    nb, edge, eager, parents_here, tab_ref, bits_ref, d_ref, plane_ref, rim_ref, new_ref, next_ref,
    face_ref, half_ref, ghost_ref, add_ref, base_ref, sem,
):
    fetch = pltpu.make_async_copy(d_ref, base_ref, sem)
    fetch.start()
    fine_ghosts(nb, edge, tab_ref, bits_ref, plane_ref, rim_ref, None, ghost_ref, parents_here)
    face_fluxes(plane_ref, ghost_ref, add_ref, face_ref, nb, eager)
    fetch.wait()
    expand_add(base_ref, add_ref, half_ref, 2, nb, edge, eager)
    extract(half_ref, next_ref, 3, nb, edge, eager)
    interior(nb, edge, eager, half_ref, new_ref, axes=(1, 2))


def face_means(nb, edge, parents_here, tab_ref, one_ref, two_ref, mean_ref, quarter_ref):
    lane = lane_of()
    group = lane // edge
    sub = lane % edge
    index = edge * (2 * (group % (ROWS // 2))) + 2 * (sub % (edge // 2))
    for face in range(6):
        places = [
            (c, slice(half * nb + rt * ROWS, half * nb + (rt + 1) * ROWS))
            for c in range(5)
            for rt in range(nb // ROWS)
            for half in range(2)
        ]
        tiles = [one_ref[face, c, at, :] + two_ref[face, c, at, :] for c, at in places]
        tiles = [v + pltpu.roll(v, LANES - 1, 1) for v in tiles]
        tiles = [v + pltpu.roll(v, LANES - edge, 1) for v in tiles]
        tiles = [0.125 * take_lanes(v, index) for v in tiles]
        for k in range(0, len(tiles), 2):
            at = k // 2 * ROWS
            quarter_ref[face, at : at + ROWS, :] = jnp.where(
                group < ROWS // 2, tiles[k], tiles[k + 1]
            )
    left = iota((5, LANES), 1) % edge < edge // 2
    for face in range(6):
        axis = face // 2
        for p in range(parents_here):
            for half in range(2):
                octant = (face % 2) * BIT_OF[axis] + half * TANGENT[axis][0]
                one = tab_ref[CHILDREN + p, octant]
                two = tab_ref[CHILDREN + p, octant + TANGENT[axis][1]]
                value = jnp.where(
                    left,
                    quarter_ref[face, pl.ds(one, 5, stride=nb), :],
                    quarter_ref[face, pl.ds(two, 5, stride=nb), :],
                )
                for c in range(5):
                    mean_ref[face, c, 2 * p + half : 2 * p + half + 1, :] = value[c : c + 1, :]


def means_kernel(
    nb, edge, eager, parents_here, tab_ref, bits_ref, plane_ref, rim_ref, rim2_ref, one_ref, send_ref,
    add_ref, ghost_ref, face_ref, quarter_ref, mean_ref,
):
    fine_ghosts(nb, edge, tab_ref, bits_ref, plane_ref, rim_ref, rim2_ref, ghost_ref, parents_here)
    face_fluxes(plane_ref, ghost_ref, add_ref, face_ref, nb, eager)
    face_means(nb, edge, parents_here, tab_ref, one_ref, face_ref, mean_ref, quarter_ref)
    for face in range(6):
        for p in range(parents_here):
            item = face * nb + tab_ref[9, p]
            target = tab_ref[0, item]
            first = tab_ref[7, item] * 5
            for c in range(5):
                send_ref[target, first + c] = mean_ref[face, c, 2 * p : 2 * p + 2, :]


def finish_kernel(
    nb, edge, eager, parents_here, tab_ref, d_ref, add_ref, half_ref, new_ref, average_ref,
    temp_ref, split_ref, eighth_ref, base_ref,
):
    temp_ref[...] = add_ref[...]
    interior(nb, edge, eager, half_ref, base_ref, axes=(0,), from_ref=d_ref)
    expand_add(base_ref, temp_ref, new_ref, 2, nb, edge, eager, split_ref)
    averages(nb, edge, parents_here, tab_ref, split_ref, average_ref, eighth_ref)


def averages(nb, edge, parents_here, tab_ref, split_ref, out_ref, eighth_ref):
    lane = lane_of()
    group = lane // edge
    index = edge * (2 * (group % (ROWS // 2))) + 2 * (lane % (edge // 2))
    for b in range(nb):
        tiles = [
            split_ref[b, c, h, pl.ds(0, ROWS, stride=2), :]
            + split_ref[b, c, h, pl.ds(1, ROWS, stride=2), :]
            for c in range(5)
            for h in range(2)
        ]
        tiles = [v + pltpu.roll(v, LANES - 1, 1) for v in tiles]
        tiles = [v + pltpu.roll(v, LANES - edge, 1) for v in tiles]
        tiles = [0.125 * take_lanes(v, index) for v in tiles]
        for c in range(5):
            eighth_ref[b, c] = jnp.where(group < ROWS // 2, tiles[2 * c], tiles[2 * c + 1])
    left = lane % edge < edge // 2
    for p in range(parents_here):
        for corner in range(4):
            one = tab_ref[CHILDREN + p, 2 * corner]
            two = tab_ref[CHILDREN + p, 2 * corner + 1]
            rows = slice(corner // 2 * ROWS, (corner // 2 + 1) * ROWS)
            lanes = slice(corner % 2 * LANES, (corner % 2 + 1) * LANES)
            for c in range(5):
                out_ref[p, c, rows, lanes] = jnp.where(left, eighth_ref[one, c], eighth_ref[two, c])


def correct_kernel(
    nb, edge, eager, parents_here, slots, tab_ref, bits_ref, new_ref, face_ref, recv_ref, cells_ref,
    out_ref, mean_ref, add_ref, done_ref, base_ref, sem, sems,
):
    fetch = pltpu.make_async_copy(new_ref, base_ref, sem)
    fetch.start()
    unpack(tab_ref, 8, slots, recv_ref, mean_ref, 2, nb)
    beside = bits_ref[2 * nb : 3 * nb, :]
    for face in range(6):
        sign = STEP_RATIO if face % 2 else -STEP_RATIO
        hit = (beside // (1 << face)) % 2 > 0
        for c in range(5):
            for half in range(2):
                at = slice(half * nb, (half + 1) * nb)
                add_ref[face, c, at, :] = jnp.where(
                    hit, sign * (face_ref[face, c, at, :] - mean_ref[face, c, at, :]), 0.0
                )
    fetch.wait()
    for p in range(parents_here):
        base_ref[tab_ref[9, p]] = cells_ref[p]
    copies = [
        pltpu.make_async_copy(done_ref.at[:, c], out_ref.at[:, c], sems.at[c]) for c in range(5)
    ]
    expand_add(base_ref, add_ref, done_ref, 1, nb, edge, eager, copies=copies)
    for copy in copies:
        copy.wait()


def column(row):
    return jnp.transpose(jnp.broadcast_to(row.astype(F32), (LANES, LANES)))


def count(hits):
    return jnp.sum(jnp.where(hits, 1.0, 0.0), axis=0, keepdims=True).astype(I32)


def tables_kernel(
    nb, devices, parents_here, blk_ref, all_near_ref, all_parent_ref, tab_ref, bits_ref, near_ref,
    parent_ref, sems,
):
    fetches = [
        pltpu.make_async_copy(all_near_ref, near_ref, sems.at[0]),
        pltpu.make_async_copy(all_parent_ref, parent_ref, sems.at[1]),
    ]
    for fetch in fetches:
        fetch.start()
    for fetch in fetches:
        fetch.wait()
    total = near_ref.shape[1]
    tiles = total // LANES
    start = blk_ref[0] * nb
    tile = pl.ds(pl.multiple_of(start // LANES * LANES, LANES), LANES)
    turn = (LANES - start % LANES) % LANES
    own = pltpu.roll(near_ref[:, tile], turn, 1)
    own_parent = pltpu.roll(parent_ref[:, tile], turn, 1)
    lane = iota((1, LANES), 1)
    face = lane // nb
    block = lane % nb
    row = iota((LANES, LANES), 0)
    near = jnp.zeros((1, LANES), I32)
    for f in range(6):
        near = jnp.where(face == f, pltpu.roll(own[f : f + 1, :], nb * f, 1), near)
    target = near // nb
    wanted = (face + 1 - 2 * (face % 2)) * nb + near % nb
    wanted_f = wanted.astype(F32)
    parent_columns = [
        column(parent_ref[0:1, k * LANES : (k + 1) * LANES]) for k in range(tiles)
    ]

    def any_parent(ids):
        ids = ids.astype(F32)
        hits = [jnp.max(jnp.where(x == ids, 1.0, 0.0), axis=0, keepdims=True) for x in parent_columns]
        return functools.reduce(jnp.maximum, hits)

    beside = any_parent(near)
    parent = own_parent[0:1, :] - start
    octant = own_parent[1:2, :]
    parent_column = column(parent)
    octant_column = column(octant)
    mine = row < nb
    owned = jnp.max(
        jnp.where(mine & (parent_column == block.astype(F32)), 1.0, 0.0), axis=0, keepdims=True
    )
    same = (column(target) == target.astype(F32)) & (row < 6 * nb)
    by_own = same & (row < lane)
    by_wanted = same & (column(wanted) < wanted_f)
    beside_column = column(beside) > 0.0
    owned_column = column(owned) > 0.0
    parent_f = parent.astype(F32)
    slot = count(mine & (parent_column < parent_f)) // 8
    slot_column = column(slot)
    row_f = row.astype(F32)
    lane_f = lane.astype(F32)

    def pick(hits, values):
        return jnp.sum(jnp.where(mine & hits, values, 0.0), axis=0, keepdims=True).astype(I32)

    rows = [
        target,
        count(by_own),
        count(by_wanted),
        beside.astype(I32),
        owned.astype(I32),
        count(by_own & beside_column),
        count(by_wanted & owned_column),
        count(by_own & owned_column),
        count(by_wanted & beside_column),
        pick((octant_column == 0.0) & (slot_column == lane_f), parent_column),
        octant,
        slot,
    ]
    for bit in BIT_OF:
        partner = (octant + bit - 2 * bit * (octant // bit % 2)).astype(F32)
        rows.append(pick((parent_column == parent_f) & (octant_column == partner), row_f))
    children = [
        pick((slot_column == p) & (octant_column == lane_f), row_f) for p in range(parents_here)
    ]
    free = mine & (owned_column == False)
    place = column(lane - count(mine & owned_column & (row < lane)))
    others = pick(free & (place == lane_f), row_f)

    most = jnp.zeros((devices, LANES), F32)
    most_all = jnp.zeros((devices, LANES), F32)
    device = iota((devices, LANES), 0)
    lanes_2d = iota((devices, LANES), 1)
    for k in range(tiles):
        lanes = slice(k * LANES, (k + 1) * LANES)
        hits = jnp.zeros((devices, LANES), F32)
        for f in range(6):
            hits = hits + jnp.where(near_ref[f : f + 1, lanes] // nb == device, 1.0, 0.0)
        sums = [hits * any_parent(k * LANES + lane), hits]
        width = 1
        while width < nb:
            sums = [x + pltpu.roll(x, LANES - width, 1) for x in sums]
            width *= 2
        start_lane = lanes_2d % nb == 0
        opposite = (k * LANES + lanes_2d) // nb + devices // 2
        opposite = jnp.where(opposite >= devices, opposite - devices, opposite) == device
        most = jnp.maximum(most, jnp.where(start_lane, sums[0], 0.0))
        most_all = jnp.maximum(most_all, jnp.where(start_lane & ~opposite, sums[1], 0.0))
    for values in (most, most_all):
        values = jnp.max(jnp.max(values, axis=0, keepdims=True), axis=1, keepdims=True)
        rows.append(jnp.broadcast_to(values, (1, LANES)).astype(I32))
    rows = rows + [others, jnp.broadcast_to(blk_ref[0], (1, LANES))] + children
    for k, values in enumerate(rows):
        tab_ref[k : k + 1, :] = values

    beside_bits = jnp.zeros((1, LANES), F32)
    for f in range(6):
        part = jnp.where(face == f, beside * (1 << f), 0.0)
        beside_bits = beside_bits + pltpu.roll(part, (LANES - nb * f) % LANES, 1)
    for k, values in enumerate((octant_column, slot_column, column(beside_bits))):
        bits_ref[k * nb : (k + 1) * nb, :] = values[0:nb, :].astype(I32)


def run(
    kernel, outs, operands, scratch=(), scalars=0, far=None, remote=(), copies=None, flops=0
):
    held = [o.shape for o in operands] + list(outs) + list(scratch)
    limit = sum(4 * max(math.prod(s), 8 * LANES) for s in held) + SPARE
    smem = pl.BlockSpec(memory_space=pltpu.SMEM)
    vmem = pl.BlockSpec(memory_space=pltpu.VMEM)
    hbm = pl.BlockSpec(memory_space=pltpu.HBM)
    specs = [smem if k < scalars else vmem for k in range(len(operands))]
    scratches = [pltpu.VMEM(s, F32) for s in scratch]
    if far is not None:
        specs[far] = hbm
        scratches.append(pltpu.SemaphoreType.DMA)
    if remote:
        scratches.append(pltpu.SemaphoreType.DMA((copies or len(remote),)))
    return pl.pallas_call(
        kernel,
        out_shape=[jax.ShapeDtypeStruct(s, F32) for s in outs],
        in_specs=specs,
        out_specs=[hbm if k in remote else vmem for k in range(len(outs))],
        scratch_shapes=scratches,
        compiler_params=pltpu.CompilerParams(vmem_limit_bytes=limit),
        cost_estimate=pl.CostEstimate(
            flops=flops, bytes_accessed=4 * sum(o.size for o in operands), transcendentals=0
        ),
    )(*operands)


def blank(*shapes):
    return pl.pallas_call(
        lambda *refs: None,
        out_shape=[jax.ShapeDtypeStruct(s, F32) for s in shapes],
        out_specs=[pl.BlockSpec(memory_space=pl.ANY)] * len(shapes),
    )()


def level_shift(array, source):
    return lax.ppermute(array, "level", [(source, 1 - source)])


def route(buffer):
    return lax.all_to_all(buffer, "blk", split_axis=0, concat_axis=0, tiled=True)


def local(fluid_state, neighbours, parents):
    blk_index = lax.axis_index("blk")
    devices = lax.axis_size("blk")
    u = fluid_state[0]
    nb, _, edge, _ = u.shape
    parents_here = nb // 8
    capacity = 2 * ((6 * nb + devices - 1) // devices)
    smem = pl.BlockSpec(memory_space=pltpu.SMEM)
    vmem = pl.BlockSpec(memory_space=pltpu.VMEM)
    hbm = pl.BlockSpec(memory_space=pltpu.HBM)
    table, bits = pl.pallas_call(
        functools.partial(tables_kernel, nb, devices, parents_here),
        out_shape=[
            jax.ShapeDtypeStruct((CHILDREN + parents_here, LANES), I32),
            jax.ShapeDtypeStruct((3 * nb, LANES), I32),
        ],
        in_specs=[smem, hbm, hbm],
        out_specs=[vmem, vmem],
        scratch_shapes=[
            pltpu.VMEM(neighbours.shape[::-1], I32),
            pltpu.VMEM(parents.shape[::-1], I32),
            pltpu.SemaphoreType.DMA((2,)),
        ],
        compiler_params=pltpu.CompilerParams(vmem_limit_bytes=7 * SPARE),
    )(jnp.reshape(blk_index, (1,)).astype(I32), neighbours.T, parents.T)

    few = max(1, capacity // 3)
    half = max(1, capacity // 2)
    counts = table[COUNTS : COUNTS + 2, 0]
    finished = lax.cond(
        (counts[0] <= few) & (counts[1] <= half) & (devices % 2 == 0),
        functools.partial(step, capacity, half, few),
        functools.partial(step, capacity, capacity, capacity),
        u,
        table,
        bits,
    )
    return finished[None]


def step(capacity, wide, slots, u, table, bits):
    eager = wide < capacity
    level_id = lax.axis_index("level")
    devices = lax.axis_size("blk")
    nb, _, edge, square = u.shape
    parents_here = nb // 8
    part = functools.partial
    cell_shape = u.shape
    plane_shape = (6, 5, 6 * nb, LANES)
    ghost_shape = (6, 5, 4 * nb, LANES)
    face_shape = (6, 5, 2 * nb, LANES)
    rim_shape = (6, 5, 2 * parents_here, LANES)
    wide_sends = [(devices * wide * 5, 4, LANES)]
    if wide < capacity:
        wide_sends.append(((capacity - wide) * 5, 4, LANES))
    thin_send = (devices, slots * 5, 2, LANES)
    average_shape = (parents_here,) + cell_shape[1:]
    work = 220 * 3 * 5 * nb * edge * square

    def inner(cells):
        return run(part(inner_kernel, nb, edge, False), [cell_shape, plane_shape], [cells], flops=work)

    def half_way_round(buffer):
        turned = [(d, (d + devices // 2) % devices) for d in range(devices)]
        return lax.ppermute(buffer, ("level", "blk"), turned)

    def coarse_first(u):
        planes, *sends = run(
            part(send_kernel, nb, edge, eager, wide, devices),
            [plane_shape] + wide_sends,
            [table, u],
            [(sum(x[0] for x in wide_sends), 4, LANES)],
            1,
            remote=range(1, 1 + len(wide_sends)),
        )
        received = [route(sends[0].reshape(devices, wide * 5, 4, LANES))]
        received += [half_way_round(buffer) for buffer in sends[1:]]
        partial_new, near = run(
            part(coarse_inner_kernel, nb, edge, False), [cell_shape, face_shape], [table, u], (), 1,
            flops=work,
        )
        adds, faces, send, rims = run(
            part(coarse_kernel, nb, edge, eager, parents_here, wide, slots),
            [ghost_shape, face_shape, thin_send, rim_shape],
            [table, planes, near] + received,
            [ghost_shape, face_shape],
            1,
        )
        return (partial_new, adds, faces, send, rims, *blank(plane_shape))

    def fine_first(u):
        partial_new, planes = inner(u)
        return (partial_new, *blank(ghost_shape, face_shape, thin_send, rim_shape), planes)

    partial_new, adds, faces, send, rims, planes = lax.cond(
        level_id == 0, coarse_first, fine_first, u
    )
    early_rims = level_shift(rims, 0)

    def coarse_second(send, partial_new, adds, planes, early_rims):
        received = route(send)
        (cells,) = run(
            part(coarse_cells_kernel, nb, edge, False),
            [cell_shape],
            [partial_new, adds],
            [ghost_shape],
            flops=work // 4,
        )
        (late,) = run(part(rims_kernel, nb, parents_here), [rim_shape], [table, received], (), 1)
        return (late, cells, *blank(plane_shape, face_shape, cell_shape))

    def fine_second(send, partial_new, adds, planes, early_rims):
        results = run(
            part(fine_kernel, nb, edge, eager, parents_here),
            [cell_shape, plane_shape, face_shape, cell_shape],
            [table, bits, partial_new, planes, early_rims],
            [ghost_shape, ghost_shape, cell_shape],
            1,
            far=2,
            flops=work,
        )
        return (*blank(rim_shape), *results)

    late, cells, half_planes, half_faces, half = lax.cond(
        level_id == 0, coarse_second, fine_second, send, partial_new, adds, planes, early_rims
    )
    late_rims = level_shift(late, 0)

    def coarse_third(cells, half_planes, half_faces, half, early_rims, late_rims):
        return tuple(blank(thin_send, cell_shape, average_shape))

    def fine_third(cells, half_planes, half_faces, half, early_rims, late_rims):
        send, adds = run(
            part(means_kernel, nb, edge, eager, parents_here),
            [thin_send, ghost_shape],
            [table, bits, half_planes, early_rims, late_rims, half_faces],
            [ghost_shape, face_shape, (6, 5 * nb, LANES), rim_shape],
            1,
        )
        received = route(send)
        out, averaged = run(
            part(finish_kernel, nb, edge, False, parents_here),
            [cell_shape, average_shape],
            [table, cells, adds, half],
            [ghost_shape, (nb, 5, 2, edge, LANES), (nb, 5, ROWS, LANES), cell_shape],
            1,
            flops=work,
        )
        return received, out, averaged

    returned, out, averaged = lax.cond(
        level_id == 0, coarse_third, fine_third,
        cells, half_planes, half_faces, half, early_rims, late_rims,
    )
    returned = level_shift(returned, 1)
    averaged = level_shift(averaged, 1)

    def correct(out, cells, faces, returned, averaged):
        return run(
            part(correct_kernel, nb, edge, eager, parents_here, slots),
            [cell_shape],
            [table, bits, cells, faces, returned, averaged],
            [face_shape, face_shape, cell_shape, cell_shape],
            1,
            far=2,
            remote=range(1),
            copies=5,
        )[0]

    return lax.cond(
        level_id == 0, correct, lambda out, *rest: out, out, cells, faces, returned, averaged
    )


def solution(mesh):
    return jax.shard_map(
        local,
        mesh=mesh,
        in_specs=(P("level", "blk", None, None, None), P(), P()),
        out_specs=P("level", "blk", None, None, None),
        check_vma=False,
    )
```
